512 devices in a mesh: tm: 32 (over z_lo, y), tile: 16 (over z_hi, x, core).
Axes of the slice: x: 4, y: 8, z: 8 (z_hi: 2, z_lo: 4; z = z_hi * 4 + z_lo), core: 2. Of those that a mesh axis runs over, the one named last changes fastest.
Arguments:
- latents: float32 [32, 64, 16, 128], P('tm', 'tile'), may hold values from -15 to 15
- new_frames: float32 [1, 64, 16, 128], P(None, 'tile'), may hold values from -15 to 15
- levels: int32 [2, 32], P(None, 'tm'), may hold values from 1 to 64
- offset: int32 [1], replicated, may hold values from 0 to 511
- w_in: bfloat16 [64, 1152], P('tm', 'tile'), may hold values from -0.75 to 0.75
- w_qkv: bfloat16 [1152, 3456], P('tm', 'tile'), as said below
- w_o: bfloat16 [1152, 1152], P('tm', 'tile'), may hold values from -0.1875 to 0.1875
- w_out: bfloat16 [1152, 64], P('tm', 'tile'), may hold values from -0.1875 to 0.1875
- w_time: bfloat16 [256, 1152], P('tm', 'tile'), may hold values from -0.375 to 0.375
- w_pos: bfloat16 [256, 1152], P('tm', 'tile'), may hold values from -0.375 to 0.375
- mod_gain: float32 [3, 1152], replicated, may hold values from -3 to 3
- mod_bias: float32 [3, 1152], replicated, may hold values from -3 to 3
- refiner: float32 [16, 27, 16], replicated, may hold values from -0.3125 to 0.3125
Outputs:
- window: float32 [32, 64, 16, 128], P('tm', 'tile')
The draws below stay inside these ranges and needn't reach their ends.
Inputs may be any that keep to these rules, and one draw needn't show every extreme that they name: `w_qkv`: a projection.
All inputs are finite; a program needn't handle non-finite values.
Results may differ from the reference program's by a relative error of at most 0.00555.
Values may be sent and summed in bfloat16 or wider, within the bound.
No kernel may reach another device: no remote copies, remote signals or barrier semaphores. Data moves between devices by JAX's collectives and lax.ppermute only.
A program may use at most 64 MiB of HBM per device.

```python
import math
import jax
import jax.numpy as jnp
from jax import lax

D = 1152
HEADS = 16
HEAD = 72
C = 16
PF = 64
FREQ = 256
WL = 128
HL = 64
FRAMES = 32
STEPS = 2
LEVELS = 64
TAPS = 27


def draw_w_qkv(key, part):
    key = jax.random.fold_in(key, 11)
    first_key = jax.random.fold_in(key, 0)
    base = jax.random.normal(first_key, (D, 3, D), jnp.float32) * D ** (-0.5)
    return base.reshape(D, 3 * D).astype(jnp.bfloat16)


def with_ends(drawn, stream_key, smallest, largest):
    dims = drawn.shape
    spot = [jax.random.randint(jax.random.fold_in(stream_key, axis), (), 0, dims[axis]) for axis in range(len(dims))]
    drawn = drawn.at[tuple(spot)].set(smallest)
    longest = dims.index(max(dims))
    spot[longest] = (spot[longest] + 1) % dims[longest]
    return drawn.at[tuple(spot)].set(largest)


def level_of(rng, extent, cuts, smallest, top_value):
    def one(dim, blocks):
        steps = jax.random.uniform(jax.random.fold_in(jax.random.fold_in(rng, 6), dim), (blocks,), jnp.float32, smallest / len(cuts), top_value / len(cuts))
        return jnp.repeat(jnp.exp(steps), extent[dim] // blocks).reshape((-1,) + (1,) * (len(extent) - dim - 1))

    level = one(*cuts[0])
    for cut in cuts[1:]:
        level = level * one(*cut)
    return level


def centred(stream_key, extent, scale, limit, cuts=(), kind=jnp.bfloat16):
    array = jax.random.normal(stream_key, extent, jnp.float32) * scale
    if len(cuts) > 0:
        array = level_of(stream_key, extent, cuts, -0.22, 0.18) * array
    return jnp.clip(array, min=-limit, max=limit).astype(kind)


def setup_inputs(seed: int = 0) -> dict:
    key_of = jax.random.split(jax.random.key(seed), 14)
    latents = centred(key_of[0], (FRAMES, HL, C, WL), 2.5, 15.0, ((0, 32), (1, 16)), jnp.float32)
    new_frames = centred(key_of[1], (STEPS - 1, HL, C, WL), 2.5, 15.0, ((1, 16),), jnp.float32)
    levels = with_ends(jax.random.randint(key_of[2], (STEPS, FRAMES), 1, LEVELS + 1), jax.random.fold_in(key_of[2], 1), 1, LEVELS).astype(jnp.int32)
    offset = jax.random.randint(key_of[3], (1,), 0, 512).astype(jnp.int32)
    w_in = centred(key_of[4], (PF, D), PF ** -0.5, 0.75, ((0, 32), (1, 16)))
    w_qkv = draw_w_qkv(jax.random.fold_in(key_of[13], 71), 0)
    w_o = centred(key_of[6], (D, D), D ** -0.5, 0.1875, ((0, 32), (1, 16)))
    w_out = centred(key_of[7], (D, PF), D ** -0.5, 0.1875, ((0, 32), (1, 16)))
    w_time = centred(key_of[8], (FREQ, D), FREQ ** -0.5, 0.375, ((0, 32), (1, 16)))
    w_pos = centred(key_of[9], (FREQ, D), FREQ ** -0.5, 0.375, ((0, 32), (1, 16)))
    mod_gain = centred(key_of[10], (3, D), 0.6, 3.0, (), jnp.float32)
    mod_bias = centred(key_of[11], (3, D), 0.5, 3.0, (), jnp.float32)
    refiner = centred(key_of[12], (C, TAPS, C), (TAPS * C) ** -0.5, 0.3125, (), jnp.float32)
    return dict(latents=latents, new_frames=new_frames, levels=levels, offset=offset, w_in=w_in, w_qkv=w_qkv, w_o=w_o, w_out=w_out, w_time=w_time, w_pos=w_pos, mod_gain=mod_gain, mod_bias=mod_bias, refiner=refiner)


SIGMA_LOW = 0.02
SIGMA_RATIO = 1000.0
NORM_EPS = 1e-06

def sigma_of(level_ids):
    scaled_level = level_ids.astype(jnp.float32) / LEVELS
    return jnp.where(level_ids > 0, SIGMA_LOW * jnp.exp(math.log(SIGMA_RATIO) * scaled_level), jnp.float32(0.0))

def sinusoid(values):
    half_freq = FREQ // 2
    frequency = jnp.exp(-math.log(10000.0) * jnp.arange(half_freq, dtype=jnp.float32) / half_freq)
    angles = values[:, None] * frequency[None, :]
    return jnp.concatenate([jnp.cos(angles), jnp.sin(angles)], axis=1)

def modulation(level_row, position_row, w_time, w_pos, mod_gain, mod_bias):
    level_emb = sinusoid(level_row.astype(jnp.float32)).astype(jnp.bfloat16)
    position_emb = sinusoid(position_row.astype(jnp.float32)).astype(jnp.bfloat16)
    hidden_sum = jnp.dot(level_emb, w_time, preferred_element_type=jnp.float32) + jnp.dot(position_emb, w_pos, preferred_element_type=jnp.float32)
    condition = jax.nn.silu(hidden_sum)
    return condition[:, None, :] * mod_gain[None] + mod_bias[None]

def layer_norm(stream):
    center = stream - lax.optimization_barrier(jnp.mean(stream, axis=-1, keepdims=True))
    spread = lax.optimization_barrier(jnp.mean(center * center, axis=-1, keepdims=True))
    return center * lax.rsqrt(spread + NORM_EPS)

def patchify(latent):
    frames, row_count, channels, col_count = latent.shape
    shaped = latent.reshape(frames, row_count // 2, 2, channels, col_count // 2, 2).transpose(0, 1, 4, 3, 2, 5)
    return shaped.reshape(frames, row_count // 2 * (col_count // 2), channels * 4)

def unpatchify(token_rows, row_count, col_count):
    frames = token_rows.shape[0]
    channels = token_rows.shape[2] // 4
    shaped = token_rows.reshape(frames, row_count // 2, col_count // 2, channels, 2, 2).transpose(0, 1, 4, 3, 2, 5)
    return shaped.reshape(frames, row_count, channels, col_count)

def one_head(packed):
    head_q, head_k, head_v = packed
    scores = jnp.dot(head_q.astype(jnp.float32), head_k.astype(jnp.float32).T) / math.sqrt(HEAD)
    highest = lax.optimization_barrier(jnp.max(scores, axis=-1, keepdims=True))
    exponent = jnp.exp(scores - highest)
    probability = (exponent / lax.optimization_barrier(jnp.sum(exponent, axis=-1, keepdims=True))).astype(jnp.bfloat16)
    return jnp.dot(probability.astype(jnp.float32), head_v.astype(jnp.float32)).astype(jnp.bfloat16)

def attention(queries, keyed, valued):
    packed = (queries.transpose(1, 0, 2), keyed.transpose(1, 0, 2), valued.transpose(1, 0, 2))
    return lax.map(one_head, packed).transpose(1, 0, 2)

def frame_block(frame_tokens, frame_mods, w_in, w_qkv, w_o, w_out):
    stream = jnp.dot(frame_tokens, w_in, preferred_element_type=jnp.float32)
    normed = (layer_norm(stream) * (1.0 + frame_mods[1]) + frame_mods[0]).astype(jnp.bfloat16)
    project = jnp.dot(normed, w_qkv, preferred_element_type=jnp.float32).astype(jnp.bfloat16)
    project = project.reshape(project.shape[0], 3, HEADS, HEAD)
    attended = attention(project[:, 0], project[:, 1], project[:, 2]).reshape(project.shape[0], HEADS * HEAD)
    stream = stream + frame_mods[2] * jnp.dot(attended, w_o, preferred_element_type=jnp.float32)
    final_in = layer_norm(stream).astype(jnp.bfloat16)
    return jnp.dot(final_in, w_out, preferred_element_type=jnp.float32)

def refine(noise_pred, refiner):
    frames = noise_pred.shape[0]
    row_count = noise_pred.shape[1]
    col_count = noise_pred.shape[3]
    padded = jnp.pad(noise_pred, ((1, 1), (1, 1), (0, 0), (1, 1)))
    refined = noise_pred
    tap_index = 0
    for time_off in range(3):
        for row_off in range(3):
            for col_off in range(3):
                window_cells = padded[time_off:time_off + frames, row_off:row_off + row_count, :, col_off:col_off + col_count]
                refined = refined + jnp.einsum('oi,fric->froc', refiner[:, tap_index, :], window_cells, precision=lax.Precision.HIGHEST)
                tap_index += 1
    return refined

def denoise(latent, level_row, position_row, w_in, w_qkv, w_o, w_out, w_time, w_pos, mod_gain, mod_bias, refiner):
    sigma_now = sigma_of(level_row)
    sigma_next = sigma_of(level_row - 1)
    scale_in = lax.rsqrt(1.0 + sigma_now * sigma_now)
    scaled = (latent * scale_in[:, None, None, None]).astype(jnp.bfloat16)
    tokens_in = patchify(scaled)
    mods = modulation(level_row, position_row, w_time, w_pos, mod_gain, mod_bias)

    def per_frame(packed):
        return frame_block(packed[0], packed[1], w_in, w_qkv, w_o, w_out)
    noise_tokens = lax.map(per_frame, (tokens_in, mods))
    noise_pred = unpatchify(noise_tokens, HL, WL)
    refined = refine(noise_pred, refiner)
    return latent + (sigma_next - sigma_now)[:, None, None, None] * refined

def reference(latents, new_frames, levels, offset, w_in, w_qkv, w_o, w_out, w_time, w_pos, mod_gain, mod_bias, refiner):
    base_positions = offset[0] + jnp.arange(FRAMES, dtype=jnp.int32)
    latent = latents
    for step_index in range(STEPS):
        if step_index > 0:
            latent = jnp.concatenate([latent[1:], new_frames[step_index - 1][None]], axis=0)
        latent = denoise(latent, levels[step_index], base_positions + step_index, w_in, w_qkv, w_o, w_out, w_time, w_pos, mod_gain, mod_bias, refiner)
    return latent
```

```python
import math

import jax
import jax.numpy as jnp
from jax import lax
from jax.experimental import pallas as pl
from jax.experimental.pallas import tpu as pltpu
from jax.sharding import PartitionSpec as P

D = 1152
HEADS = 16
HEAD = 72
C = 16
PF = 64
FREQ = 256
STEPS = 2
LEVELS = 64
TM = 32
TILE = 16
ROWS = 36
TOK = 128
LANES = 128
SPAN = TILE * TOK

SIGMA_LOW = 0.02
SIGMA_RATIO = 1000.0
NORM_EPS = 1e-06

F32 = jnp.float32
BF16 = jnp.bfloat16
HIGHEST = lax.Precision.HIGHEST


def swapped(block, axis, mask):
    size = lax.axis_size(axis)
    return lax.ppermute(block, axis, [(i, i ^ mask) for i in range(size)])


def shifted(block, axis, distance):
    devices = range(lax.axis_size(axis))
    route = [(i - distance, i) for i in devices if i - distance in devices]
    return lax.ppermute(block, axis, route)


def group_gather(block, axis, unit, count, dim):
    spot = (lax.axis_index(axis) // unit) % count
    parts = [block] + [swapped(block, axis, unit * k) for k in range(1, count)]
    shape = block.shape[:dim] + (count,) + block.shape[dim:]
    stacked = jnp.zeros(shape, block.dtype)
    for k, part in enumerate(parts):
        stacked = lax.dynamic_update_index_in_dim(stacked, part, spot ^ k, dim)
    return stacked


def tile_gather(block):
    both = group_gather(block, "tile", 8, 2, 0)
    four = group_gather(both, "tile", 2, 4, 1)
    full = group_gather(four, "tile", 1, 2, 2)
    return full.reshape((TILE,) + block.shape)


def tile_collect(block):
    both = jnp.stack([block, swapped(block, "tile", 8)])
    four = jnp.concatenate([both] + [swapped(both, "tile", 2 * k) for k in (1, 2, 3)])
    return jnp.concatenate([four, swapped(four, "tile", 1)])


def tm_gather(block):
    lo = group_gather(block, "tm", 8, 4, 0)
    full = group_gather(lo, "tm", 1, 8, 1)
    return full.reshape((TM,) + block.shape)


def sigma_of(level_ids):
    scaled_level = level_ids.astype(F32) / LEVELS
    return jnp.where(
        level_ids > 0, SIGMA_LOW * jnp.exp(math.log(SIGMA_RATIO) * scaled_level), F32(0.0)
    )


def sinusoid(values):
    half_freq = FREQ // 2
    frequency = jnp.exp(-math.log(10000.0) * jnp.arange(half_freq, dtype=F32) / half_freq)
    angles = values[:, None] * frequency[None, :]
    return jnp.concatenate([jnp.cos(angles), jnp.sin(angles)], axis=1)


def split_bf16(x):
    head = lax.reduce_precision(x, exponent_bits=8, mantissa_bits=7)
    return head.astype(BF16), (x - head).astype(BF16)


def nn(a, b, precision=None):
    return lax.dot_general(
        a, b, (((1,), (0,)), ((), ())), preferred_element_type=F32, precision=precision
    )


def nt(a, b):
    return lax.dot_general(a, b, (((1,), (1,)), ((), ())), preferred_element_type=F32)


def spread_matrix(shape, token_dim, hp, b, dtype):
    token = lax.broadcasted_iota(jnp.int32, shape, token_dim)
    col = lax.broadcasted_iota(jnp.int32, shape, 1 - token_dim)
    hit = col + 128 * hp == 2 * token + b
    return jnp.where(hit, 1.0, 0.0).astype(dtype)


def patch_rows(scaled):
    halves = []
    for b in range(2):
        total = None
        for hp in range(2):
            rows = scaled[2 * hp : 2 * hp + 2].reshape(2 * C, LANES)
            term = nn(rows, spread_matrix((LANES, TOK), 1, hp, b, BF16))
            total = term if total is None else total + term
        halves.append(total)
    return jnp.concatenate(halves, axis=0).astype(BF16)


def prep_kernel(scalar_ref, lat_ref, out_ref):
    scaled = (lat_ref[...] * scalar_ref[0]).astype(BF16)
    out_ref[...] = patch_rows(scaled)


def refined_rows(noise_ref, mix_ref):
    lane = lax.broadcasted_iota(jnp.int32, (C, LANES), 1)
    tri = {}
    for td in range(3):
        for row in range(6):
            x = noise_ref[td, row]
            before = jnp.where(lane == 0, 0.0, pltpu.roll(x, 1, 1))
            after = jnp.where(lane == LANES - 1, 0.0, pltpu.roll(x, LANES - 1, 1))
            tri[td, row] = [before, x, after]
    columns = []
    for r in range(4):
        pieces = []
        for td in range(3):
            for dr in range(3):
                pieces += tri[td, r + dr]
        columns.append(jnp.concatenate(pieces, axis=0))
    cells = jnp.concatenate(columns, axis=1)
    mixed = nn(mix_ref[...], cells, HIGHEST)
    return [noise_ref[1, r + 1] + mixed[:, r * LANES : (r + 1) * LANES] for r in range(4)]


def middle_kernel(scalar_ref, flag_ref, noise_ref, lat_ref, new_ref, mix_ref, lat_out, patch_out):
    refined = refined_rows(noise_ref, mix_ref)
    last = flag_ref[0] == 1
    rows = []
    for r in range(4):
        moved = lat_ref[r] + lat_ref[4, 0:1, :] * refined[r]
        rows.append(jnp.where(last, new_ref[r], moved))
        lat_out[r] = rows[r]
    scaled = (jnp.stack(rows) * scalar_ref[0]).astype(BF16)
    patch_out[...] = patch_rows(scaled)


def final_kernel(scalar_ref, noise_ref, lat_ref, mix_ref, out_ref):
    refined = refined_rows(noise_ref, mix_ref)
    for r in range(4):
        out_ref[r] = lat_ref[r] + scalar_ref[0] * refined[r]


def block_kernel(
    pt_ref, gram_ref, n_ref, mvt_ref, wint_ref, wot_ref, woutt_ref, gate_ref, out_ref,
    keys_t, keys, att,
):
    row = lax.broadcasted_iota(jnp.int32, (PF, TOK), 0)
    ones = jnp.where(row == 0, 1.0, 0.0).astype(F32)
    for j in range(TILE):
        patches = pt_ref[j].astype(F32)
        spread = jnp.sum(patches * nn(gram_ref[...], patches, HIGHEST), axis=0, keepdims=True)
        unit = patches * lax.rsqrt(jnp.maximum(spread, 0.0) * (1.0 / D) + NORM_EPS)
        wide = jnp.concatenate([unit, ones], axis=0)
        keys_t[:, j * TOK : (j + 1) * TOK] = wide.astype(BF16)
        keys[j * TOK : (j + 1) * TOK, :] = wide.T.astype(BF16)

    def two_heads(pair):
        own = keys[0:TOK, :]
        queries = jnp.concatenate(
            [nn(own, n_ref[2 * pair]), nn(own, n_ref[2 * pair + 1])], axis=0
        ).astype(BF16)
        scores = nn(queries, keys_t[...])
        highest = jnp.max(scores, axis=1, keepdims=True)
        weights = jnp.exp2(scores - highest).astype(BF16)
        summed = nn(weights, keys[...])
        mean = (summed / summed[:, PF : PF + 1]).astype(BF16)
        for k in range(2):
            head = 2 * pair + k
            value = nt(mvt_ref[head], mean[k * TOK : (k + 1) * TOK])
            att[pl.ds(pl.multiple_of(head * HEAD, 8), HEAD), :] = value[0:HEAD]

    @pl.loop(0, HEADS // 4)
    def _(i):
        two_heads(2 * i)
        two_heads(2 * i + 1)

    stream = nn(wint_ref[...], pt_ref[0])
    stream = stream + gate_ref[...] * nn(wot_ref[...], att[...].astype(BF16))
    center = stream - jnp.sum(stream, axis=0, keepdims=True) * (1.0 / D)
    spread = jnp.sum(center * center, axis=0, keepdims=True) * (1.0 / D)
    final = (center * lax.rsqrt(spread + NORM_EPS)).astype(BF16)
    noise = nn(woutt_ref[...], final)
    for hp in range(2):
        rows = None
        for b in range(2):
            term = nn(
                noise[b * 32 : (b + 1) * 32], spread_matrix((TOK, LANES), 0, hp, b, F32), HIGHEST
            )
            rows = term if rows is None else rows + term
        out_ref[2 * hp] = rows[0:C]
        out_ref[2 * hp + 1] = rows[C : 2 * C]


VMEM = pl.BlockSpec(memory_space=pltpu.VMEM)
SMEM = pl.BlockSpec(memory_space=pltpu.SMEM)


def frame_block(pt, gram, n, mvt, w_in_t, w_o_t, w_out_t, gate):
    return pl.pallas_call(
        block_kernel,
        out_shape=jax.ShapeDtypeStruct((4, C, LANES), F32),
        in_specs=[VMEM] * 8,
        out_specs=VMEM,
        scratch_shapes=[
            pltpu.VMEM((LANES, SPAN), BF16),
            pltpu.VMEM((SPAN, LANES), BF16),
            pltpu.VMEM((D, TOK), F32),
        ],
        compiler_params=pltpu.CompilerParams(vmem_limit_bytes=48 * 1024 * 1024),
        cost_estimate=pl.CostEstimate(
            flops=2 * 2 * SPAN * SPAN * LANES + 2 * D * D * TOK,
            bytes_accessed=2 * D * D + 4 * SPAN * LANES,
            transcendentals=SPAN * SPAN,
        ),
        name="frame_block",
    )(pt, gram, n, mvt, w_in_t, w_o_t, w_out_t, gate)


def prep(scale_in, latent):
    return pl.pallas_call(
        prep_kernel,
        out_shape=jax.ShapeDtypeStruct((PF, TOK), BF16),
        in_specs=[SMEM, VMEM],
        out_specs=VMEM,
        name="prep",
    )(scale_in, latent)


def middle(scale_in, last, noise, lat, new, mix):
    return pl.pallas_call(
        middle_kernel,
        out_shape=(
            jax.ShapeDtypeStruct((4, C, LANES), F32),
            jax.ShapeDtypeStruct((PF, TOK), BF16),
        ),
        in_specs=[SMEM, SMEM] + [VMEM] * 4,
        out_specs=(VMEM, VMEM),
        compiler_params=pltpu.CompilerParams(vmem_limit_bytes=32 * 1024 * 1024),
        name="middle",
    )(scale_in, last, noise, lat, new, mix)


def finish(drop, noise, lat, mix):
    return pl.pallas_call(
        final_kernel,
        out_shape=jax.ShapeDtypeStruct((4, C, LANES), F32),
        in_specs=[SMEM] + [VMEM] * 3,
        out_specs=VMEM,
        compiler_params=pltpu.CompilerParams(vmem_limit_bytes=32 * 1024 * 1024),
        name="finish",
    )(drop, noise, lat, mix)


def with_rows(frames):
    before = shifted(frames[:, 3:4], "tile", 1)
    after = shifted(frames[:, 0:1], "tile", -1)
    return jnp.concatenate([before, frames, after], axis=1)


def per_device(
    latents, new_frames, levels, offset, w_in, w_qkv, w_o, w_out, w_time, w_pos,
    mod_gain, mod_bias, refiner,
):
    frame = lax.axis_index("tm")
    mix = refiner.reshape(C, 27 * C)
    latent = latents[0]
    level = levels[:, 0]
    sigma_now = sigma_of(level)
    drop = sigma_of(level - 1) - sigma_now
    scale_in = lax.rsqrt(1.0 + sigma_now * sigma_now)

    patches = tile_collect(prep(scale_in[0:1], latent))
    marked = jnp.concatenate([latent, jnp.full((1, C, LANES), drop[0], F32)], axis=0)
    marked = shifted(marked, "tm", -1)

    small = jnp.concatenate([w_time, w_pos, w_in, jnp.zeros((18, HEAD), BF16)], axis=0)
    packed = jnp.concatenate([w_qkv, w_o, w_out, small], axis=1)
    rows = tm_gather(packed)
    qkv_cols = rows[:, :, 0:216].reshape(D, 216)
    out_cols = rows[:, :, 216:292].reshape(D, 76)
    small = rows[:, :, 292:364]
    time_cols = small[:, 0:8].reshape(FREQ, HEAD)
    pos_cols = small[:, 8:16].reshape(FREQ, HEAD)
    in_cols = small[:, 16:18].reshape(C, 2, 2, HEAD).transpose(2, 1, 0, 3).reshape(PF, HEAD)

    steps = jnp.arange(STEPS, dtype=jnp.int32)
    level_emb = sinusoid(level.astype(F32)).astype(BF16)
    position_emb = sinusoid((offset + frame + steps).astype(F32)).astype(BF16)
    hidden = nn(level_emb, time_cols) + nn(position_emb, pos_cols)
    head_part, tail_part = split_bf16(jax.nn.silu(hidden))
    parts = jnp.concatenate([in_cols, head_part, tail_part, jnp.zeros((12, HEAD), BF16)], axis=0)
    parts = tile_gather(parts).transpose(1, 0, 2).reshape(80, D)
    full_in = parts[0:PF]
    condition = parts[64:66].astype(F32) + parts[66:68].astype(F32)
    mods = condition[:, None, :] * mod_gain[None] + mod_bias[None]

    wide_in = full_in.astype(F32)
    centred_in = wide_in - jnp.mean(wide_in, axis=1, keepdims=True)
    gram = lax.dot_general(
        centred_in, centred_in, (((1,), (1,)), ((), ())), precision=HIGHEST,
        preferred_element_type=F32,
    )
    scaled_in = centred_in[None] * (1.0 + mods[:, 1])[:, None, :]
    lines = jnp.concatenate([scaled_in.reshape(2 * PF, D), mods[:, 0]], axis=0)
    folded = lax.dot_general(
        qkv_cols.astype(F32), lines, (((0,), (1,)), ((), ())), precision=HIGHEST,
        preferred_element_type=F32,
    )
    bias = jnp.pad(folded[:, 2 * PF :].T, ((0, 0), (0, 40))).reshape(4, LANES)
    folded = jnp.concatenate([folded[:, : 2 * PF], bias, jnp.zeros((4, LANES), F32)], axis=0)
    folded = tile_gather(folded.astype(BF16))
    main = folded[:, 0:216].reshape(3, HEADS, HEAD, STEPS, PF)
    bias = folded[:, 216:220].reshape(TILE, STEPS, 256)[:, :, :216]
    bias = bias.reshape(TILE, STEPS, 3, HEAD).transpose(1, 0, 2, 3).reshape(STEPS, 3, HEADS, HEAD)

    out_t = jnp.pad(out_cols.T, ((0, 4), (0, 0)))
    out_t = tile_gather(out_t)
    full_o_t = out_t[:, 0:72].reshape(D, D)
    full_out_t = out_t[:, 72:76].reshape(C, 2, 2, D).transpose(2, 1, 0, 3).reshape(PF, D)
    full_in_t = full_in.T

    fold_scale = math.log2(math.e) / math.sqrt(HEAD)
    for step in range(STEPS):
        unit = jnp.concatenate([main[:, :, :, step], bias[step][..., None]], axis=-1)
        unit = jnp.pad(unit, ((0, 0), (0, 0), (0, 0), (0, LANES - PF - 1)))
        n = jnp.einsum("hdk,hdl->hkl", unit[0], unit[1], preferred_element_type=F32)
        n = (n * fold_scale).astype(BF16)
        mvt = jnp.pad(unit[2], ((0, 0), (0, 8), (0, 0)))
        gate = mods[step, 2][:, None]
        noise = frame_block(patches, gram, n, mvt, full_in_t, full_o_t, full_out_t, gate)
        if step == 0:
            frames = jnp.stack([noise, shifted(noise, "tm", -1), shifted(noise, "tm", -2)])
            last = (frame == TM - 1).astype(jnp.int32)[None]
            latent, patches = middle(
                scale_in[1:2], last, with_rows(frames), marked, new_frames[0], mix
            )
            patches = tile_collect(patches)
        else:
            frames = jnp.stack([shifted(noise, "tm", 1), noise, shifted(noise, "tm", -1)])
            return finish(drop[1:2], with_rows(frames), latent, mix)[None]


def solution(mesh):
    in_specs = (
        P("tm", "tile", None, None),
        P(None, "tile", None, None),
        P(None, "tm"),
        P(),
        P("tm", "tile"),
        P("tm", "tile"),
        P("tm", "tile"),
        P("tm", "tile"),
        P("tm", "tile"),
        P("tm", "tile"),
        P(),
        P(),
        P(),
    )
    out_specs = P("tm", "tile", None, None)
    return jax.shard_map(
        per_device, mesh=mesh, in_specs=in_specs, out_specs=out_specs, check_vma=False
    )
```

```python
import functools
import math

import jax
import jax.numpy as jnp
import numpy as np
from jax import lax
from jax.experimental import pallas as pl
from jax.experimental.pallas import tpu as pltpu
from jax.sharding import PartitionSpec as P

D = 1152
HEADS = 16
HEAD = 72
C = 16
PF = 64
FREQ = 256
STEPS = 2
LEVELS = 64
TM = 32
TILE = 16
ROWS = 36
TOK = 128
LANES = 128
SPAN = TILE * TOK
WIDE = 32 * 40

SIGMA_LOW = 0.02
SIGMA_RATIO = 1000.0
NORM_EPS = 1e-06

F32 = jnp.float32
BF16 = jnp.bfloat16
HIGHEST = lax.Precision.HIGHEST


def swapped(block, axis, mask):
    size = lax.axis_size(axis)
    return lax.ppermute(block, axis, [(i, i ^ mask) for i in range(size)])


def shifted(block, axis, distance):
    devices = range(lax.axis_size(axis))
    route = [(i - distance, i) for i in devices if i - distance in devices]
    return lax.ppermute(block, axis, route)


def exchanged(copies, axis):
    return lax.all_to_all(copies, axis, split_axis=0, concat_axis=0, tiled=True)


def sigma_of(level_ids):
    scaled_level = level_ids.astype(F32) / LEVELS
    return jnp.where(
        level_ids > 0, SIGMA_LOW * jnp.exp(math.log(SIGMA_RATIO) * scaled_level), F32(0.0)
    )


def sinusoid(values):
    half_freq = FREQ // 2
    frequency = jnp.exp(-math.log(10000.0) * jnp.arange(half_freq, dtype=F32) / half_freq)
    angles = values[:, None] * frequency[None, :]
    return jnp.concatenate([jnp.cos(angles), jnp.sin(angles)], axis=1)


def nn(a, b, precision=None):
    return lax.dot_general(
        a, b, (((1,), (0,)), ((), ())), preferred_element_type=F32, precision=precision
    )


def nt(a, b):
    return lax.dot_general(a, b, (((1,), (1,)), ((), ())), preferred_element_type=F32)


def tn(a, b):
    return lax.dot_general(a, b, (((0,), (0,)), ((), ())), preferred_element_type=F32)


def lane_of(shape):
    return lax.broadcasted_iota(jnp.int32, shape, 1)


def spread_matrix(shape, token_dim, hp, b, dtype):
    token = lax.broadcasted_iota(jnp.int32, shape, token_dim)
    col = lax.broadcasted_iota(jnp.int32, shape, 1 - token_dim)
    hit = col + 128 * hp == 2 * token + b
    return jnp.where(hit, 1.0, 0.0).astype(dtype)


def patch_rows(scaled):
    halves = []
    for b in range(2):
        total = None
        for hp in range(2):
            rows = scaled[2 * hp : 2 * hp + 2].reshape(2 * C, LANES)
            term = nn(rows, spread_matrix((LANES, TOK), 1, hp, b, BF16))
            total = term if total is None else total + term
        halves.append(total)
    return jnp.concatenate(halves, axis=0).astype(BF16)


def prep_kernel(scalar_ref, lat_ref, out_ref):
    scaled = (lat_ref[...] * scalar_ref[0]).astype(BF16)
    rows = patch_rows(scaled)
    for t in range(TILE):
        out_ref[t] = rows


def refined_rows(noise_ref, mix_ref):
    lane = lax.broadcasted_iota(jnp.int32, (C, LANES), 1)
    tri = {}
    for td in range(3):
        for row in range(6):
            x = noise_ref[td, row]
            before = jnp.where(lane == 0, 0.0, pltpu.roll(x, 1, 1))
            after = jnp.where(lane == LANES - 1, 0.0, pltpu.roll(x, LANES - 1, 1))
            tri[td, row] = [before, x, after]
    columns = []
    for r in range(4):
        pieces = []
        for td in range(3):
            for dr in range(3):
                pieces += tri[td, r + dr]
        columns.append(jnp.concatenate(pieces, axis=0))
    cells = jnp.concatenate(columns, axis=1)
    mixed = nn(mix_ref[...], cells, HIGHEST)
    return [noise_ref[1, r + 1] + mixed[:, r * LANES : (r + 1) * LANES] for r in range(4)]


def middle_kernel(scalar_ref, flag_ref, noise_ref, lat_ref, new_ref, mix_ref, lat_out, patch_out):
    refined = refined_rows(noise_ref, mix_ref)
    last = flag_ref[0] == 1
    rows = []
    for r in range(4):
        moved = lat_ref[r] + lat_ref[4, 0:1, :] * refined[r]
        rows.append(jnp.where(last, new_ref[r], moved))
        lat_out[r] = rows[r]
    scaled = (jnp.stack(rows) * scalar_ref[0]).astype(BF16)
    patches = patch_rows(scaled)
    for t in range(TILE):
        patch_out[t] = patches


def final_kernel(scalar_ref, noise_ref, lat_ref, mix_ref, out_ref):
    refined = refined_rows(noise_ref, mix_ref)
    for r in range(4):
        out_ref[r] = lat_ref[r] + scalar_ref[0] * refined[r]


def spread_kernel(x_ref, pick_ref, emb_ref, mod_ref, order_ref, pay_ref, out_t_ref):
    out_t_ref[...] = nt(order_ref[...], x_ref[:, 256:384]).astype(BF16)
    cols = x_ref[:, 128:256]
    halves = []
    for h in range(2):
        found = jnp.concatenate(
            [nn(pick_ref[h], cols), nn(emb_ref[h], cols), jnp.zeros((48, LANES), F32)], axis=0
        )
        turned = pltpu.roll(found, 40, 1).T[0:40]
        mod = mod_ref[40 * h : 40 * h + 40]
        lane = lane_of((40, LANES))
        valid = lax.broadcasted_iota(jnp.int32, (40, LANES), 0) < ROWS
        block = jnp.where(lane < PF, turned, jnp.where(lane == 76, 1.0, 0.0))
        for step in range(STEPS):
            hidden = turned[:, PF + step : PF + step + 1]
            condition = hidden / (1.0 + jnp.exp(-hidden))
            for j, kind in enumerate((1, 0, 2)):
                value = condition * mod[:, kind : kind + 1] + mod[:, 3 + kind : 4 + kind]
                if kind == 1:
                    value = value + 1.0
                upper = value.astype(BF16).astype(F32)
                block = jnp.where(lane == PF + 3 * step + j, upper, block)
                block = jnp.where(lane == PF + 6 + 3 * step + j, value - upper, block)
        halves.append(jnp.where(valid, block, 0.0))
    pay = jnp.concatenate(halves, axis=0).astype(BF16)
    for t in range(TILE):
        pay_ref[t] = pay


def fold_kernel(feat_ref, x_ref, first_ref, second_ref, gram_ref):
    lane = lane_of((WIDE, LANES))
    feat = feat_ref[...].astype(F32)
    mods = feat + pltpu.roll(feat, LANES - 6, 1)
    wide = jnp.where(lane < PF, feat, 0.0)
    mean = jnp.sum(wide, axis=0, keepdims=True) * (1.0 / D)
    centred = (wide - mean) * feat[:, 76:77]
    upper = centred.astype(BF16)
    lower = (centred - upper.astype(F32)).astype(BF16)
    gram = tn(upper, upper) + tn(upper, lower) + tn(lower, upper)
    gram_ref[...] = gram[0:PF, 0:PF]
    for step, out_ref in enumerate((first_ref, second_ref)):
        at = PF + 3 * step
        lines = jnp.where(
            lane < PF,
            centred * mods[:, at : at + 1],
            jnp.where(lane == PF, mods[:, at + 1 : at + 2], 0.0),
        )
        upper = lines.astype(BF16)
        lower = (lines - upper.astype(F32)).astype(BF16)
        weights = x_ref[:, 0:256]
        folded = tn(weights, upper) + tn(weights, lower)
        unit = [folded[HEAD * j : HEAD * j + HEAD] for j in range(3)]
        spot = lane_of((HEAD, LANES))
        top = jnp.where(spot < PF, unit[0], pltpu.roll(unit[1], PF, 1))
        low = jnp.where(spot < PF, unit[2], 0.0)
        low = jnp.where(spot == PF, unit[0], low)
        low = jnp.where(spot == PF + 1, pltpu.roll(unit[1], 1, 1), low)
        low = jnp.where(spot == PF + 2, pltpu.roll(unit[2], 2, 1), low)
        packed = jnp.concatenate([top, low], axis=0).astype(BF16)
        for t in range(TILE):
            out_ref[t] = packed


def heads_kernel(folded_ref, widen_ref, n_ref, mvt_ref, units):
    spot = lane_of((HEAD, LANES))
    for t in range(TILE):
        both = folded_ref[t].astype(F32)
        top, low = both[0:HEAD], both[HEAD : 2 * HEAD]
        parts = (
            (top, low),
            (pltpu.roll(top, PF, 1), pltpu.roll(low, LANES - 1, 1)),
            (low, pltpu.roll(low, LANES - 2, 1)),
        )
        for j, (main, bias) in enumerate(parts):
            unit = jnp.where(spot < PF, main, jnp.where(spot == PF, bias, 0.0))
            units[3 * t + j] = unit
    fold_scale = math.log2(math.e) / math.sqrt(HEAD)
    for h in range(HEADS):
        q, k, v = (units[HEADS * kind + h].astype(BF16) for kind in range(3))
        n_ref[h] = (tn(q, k) * fold_scale).astype(BF16)
        mvt_ref[h] = nn(widen_ref[...], v).astype(BF16)


def block_kernel(
    step, spot_ref, pt_ref, gram_ref, n_ref, mvt_ref, feat_ref, wot_ref, wot2_ref, out_ref,
    keys_t, keys, att, stream_ref,
):
    me = spot_ref[0]
    row = lax.broadcasted_iota(jnp.int32, (PF, TOK), 0)
    ones = jnp.where(row == 0, 1.0, 0.0).astype(F32)
    for j in range(TILE):
        patches = pt_ref[j].astype(F32)
        spread = jnp.sum(patches * nn(gram_ref[...], patches, HIGHEST), axis=0, keepdims=True)
        unit = patches * lax.rsqrt(jnp.maximum(spread, 0.0) * (1.0 / D) + NORM_EPS)
        wide = jnp.concatenate([unit, ones], axis=0)
        keys_t[:, j * TOK : (j + 1) * TOK] = wide.astype(BF16)
        keys[j * TOK : (j + 1) * TOK, :] = wide.T.astype(BF16)

    def two_heads(pair):
        own = keys[pl.ds(pl.multiple_of(me * TOK, TOK), TOK), :]
        queries = jnp.concatenate(
            [nn(own, n_ref[2 * pair]), nn(own, n_ref[2 * pair + 1])], axis=0
        ).astype(BF16)
        scores = nn(queries, keys_t[...])
        highest = jnp.max(scores, axis=1, keepdims=True)
        weights = jnp.exp2(scores - highest).astype(BF16)
        summed = nn(weights, keys[...])
        mean = (summed / summed[:, PF : PF + 1]).astype(BF16)
        for k in range(2):
            head = 2 * pair + k
            value = nt(mvt_ref[head], mean[k * TOK : (k + 1) * TOK])
            att[pl.ds(pl.multiple_of(head * 80, 80), 80), :] = value

    @pl.loop(0, HEADS // 4)
    def _(i):
        two_heads(2 * i)
        two_heads(2 * i + 1)

    attended = att[...].astype(BF16)
    for c, ref in enumerate((wot_ref, wot2_ref)):
        delta = nn(ref[...], attended)
        for b in range(8):
            tile = me ^ (8 * (b % 2) + 2 * (b // 2) + c)
            rows = pl.ds(pl.multiple_of(tile * 80, 80), 80)
            stream_ref[rows, :] = delta[96 * b : 96 * b + 80]
    feat = feat_ref[...]
    own = jnp.concatenate([pt_ref[me], jnp.zeros((PF, TOK), BF16)], axis=0)
    at = PF + 3 * step + 2
    gate = feat[:, at : at + 1].astype(F32) + feat[:, at + 6 : at + 7].astype(F32)
    stream = nn(feat, own) + gate * stream_ref[...]
    mean = jnp.sum(stream, axis=0, keepdims=True) * (1.0 / D)
    center = (stream - mean) * feat[:, 76:77].astype(F32)
    spread = jnp.sum(center * center, axis=0, keepdims=True) * (1.0 / D)
    final = (center * lax.rsqrt(spread + NORM_EPS)).astype(BF16)
    out_rows = [
        ref[96 * b + 80 : 96 * b + 96, :] for ref in (wot_ref, wot2_ref) for b in range(8)
    ]
    noise = nn(jnp.concatenate(out_rows, axis=0), final)
    feature = lax.broadcasted_iota(jnp.int32, (PF, 256), 0)
    source = lane_of((PF, 256))
    block = source >> 4
    mask = ((block & 1) << 3) | (((block >> 1) & 3) << 1) | (block >> 3)
    q = source & 15
    wanted = ((q & 1) << 5) + ((q >> 1) << 4) + (mask ^ me)
    order = jnp.where((q < 4) & (feature == wanted), 1.0, 0.0).astype(F32)
    noise = nn(order, noise, HIGHEST)
    for hp in range(2):
        rows = None
        for b in range(2):
            term = nn(
                noise[b * 32 : (b + 1) * 32], spread_matrix((TOK, LANES), 0, hp, b, F32), HIGHEST
            )
            rows = term if rows is None else rows + term
        out_ref[2 * hp] = rows[0:C]
        out_ref[2 * hp + 1] = rows[C : 2 * C]


VMEM = pl.BlockSpec(memory_space=pltpu.VMEM)
SMEM = pl.BlockSpec(memory_space=pltpu.SMEM)


def spread(x, emb, mod):
    return pl.pallas_call(
        spread_kernel,
        out_shape=(
            jax.ShapeDtypeStruct((TILE, 80, LANES), BF16),
            jax.ShapeDtypeStruct((96, WIDE), BF16),
        ),
        in_specs=[VMEM] * 5,
        out_specs=(VMEM, VMEM),
        compiler_params=pltpu.CompilerParams(vmem_limit_bytes=32 * 1024 * 1024),
        name="spread",
    )(x, jnp.asarray(PICK, BF16), emb, mod, jnp.asarray(ORDER, BF16))


def fold(feat, x):
    folded = jax.ShapeDtypeStruct((TILE, 2 * HEAD, LANES), BF16)
    return pl.pallas_call(
        fold_kernel,
        out_shape=(folded, folded, jax.ShapeDtypeStruct((PF, PF), F32)),
        in_specs=[VMEM] * 2,
        out_specs=(VMEM,) * 3,
        compiler_params=pltpu.CompilerParams(vmem_limit_bytes=32 * 1024 * 1024),
        name="fold",
    )(feat, x)


def heads(folded):
    return pl.pallas_call(
        heads_kernel,
        out_shape=(
            jax.ShapeDtypeStruct((HEADS, LANES, LANES), BF16),
            jax.ShapeDtypeStruct((HEADS, 80, LANES), BF16),
        ),
        in_specs=[VMEM] * 2,
        out_specs=(VMEM,) * 2,
        scratch_shapes=[pltpu.VMEM((3 * HEADS, HEAD, LANES), F32)],
        compiler_params=pltpu.CompilerParams(vmem_limit_bytes=32 * 1024 * 1024),
        name="heads",
    )(folded, jnp.asarray(ORDER[0:80, 0:HEAD], BF16))


def frame_block(step, spot, pt, gram, n, mvt, feat, wot, wot2):
    return pl.pallas_call(
        functools.partial(block_kernel, step),
        out_shape=jax.ShapeDtypeStruct((4, C, LANES), F32),
        in_specs=[SMEM] + [VMEM] * 7,
        out_specs=VMEM,
        scratch_shapes=[
            pltpu.VMEM((LANES, SPAN), BF16),
            pltpu.VMEM((SPAN, LANES), BF16),
            pltpu.VMEM((WIDE, TOK), F32),
            pltpu.VMEM((WIDE, TOK), F32),
        ],
        compiler_params=pltpu.CompilerParams(vmem_limit_bytes=48 * 1024 * 1024),
        cost_estimate=pl.CostEstimate(
            flops=2 * 2 * SPAN * SPAN * LANES + 2 * D * D * TOK,
            bytes_accessed=2 * D * D + 4 * SPAN * LANES,
            transcendentals=SPAN * SPAN,
        ),
        name="frame_block",
    )(spot, pt, gram, n, mvt, feat, wot, wot2)


def prep(scale_in, latent):
    return pl.pallas_call(
        prep_kernel,
        out_shape=jax.ShapeDtypeStruct((TILE, PF, TOK), BF16),
        in_specs=[SMEM, VMEM],
        out_specs=VMEM,
        name="prep",
    )(scale_in, latent)


def middle(scale_in, last, noise, lat, new, mix):
    return pl.pallas_call(
        middle_kernel,
        out_shape=(
            jax.ShapeDtypeStruct((4, C, LANES), F32),
            jax.ShapeDtypeStruct((TILE, PF, TOK), BF16),
        ),
        in_specs=[SMEM, SMEM] + [VMEM] * 4,
        out_specs=(VMEM, VMEM),
        compiler_params=pltpu.CompilerParams(vmem_limit_bytes=32 * 1024 * 1024),
        name="middle",
    )(scale_in, last, noise, lat, new, mix)


def finish(drop, noise, lat, mix):
    return pl.pallas_call(
        final_kernel,
        out_shape=jax.ShapeDtypeStruct((4, C, LANES), F32),
        in_specs=[SMEM] + [VMEM] * 3,
        out_specs=VMEM,
        compiler_params=pltpu.CompilerParams(vmem_limit_bytes=32 * 1024 * 1024),
        name="finish",
    )(drop, noise, lat, mix)


def with_rows(frames):
    before = shifted(frames[:, 3:4], "tile", 1)
    after = shifted(frames[:, 0:1], "tile", -1)
    return jnp.concatenate([before, frames, after], axis=1)


def pick_matrix():
    pick = np.zeros((2, 2, 2, C, TM, 20, 2), np.float32)
    for h in range(2):
        for b in range(2):
            for a in range(2):
                for c in range(C):
                    pick[h, b, a, c, 2 * c + a, 16 + b, h] = 1.0
    return pick.reshape(2, PF, WIDE)


def order_matrix():
    order = np.zeros((96, LANES), np.float32)
    for j in range(ROWS):
        order[j, j] = 1.0
        order[40 + j, ROWS + j] = 1.0
    for j in range(4):
        order[80 + j, HEAD + j] = 1.0
    return order


PICK = pick_matrix()
ORDER = order_matrix()


def packed_weights(w_in, w_qkv, w_o, w_out, w_time, w_pos):
    small = jnp.concatenate([w_time, w_pos, w_in], axis=0).reshape(ROWS, ROWS)
    gap = jnp.zeros((ROWS, 4), BF16)
    tail = jnp.zeros((ROWS, 52), BF16)
    packed = jnp.concatenate([w_qkv, small, gap, w_o, w_out, tail], axis=1)
    return jnp.pad(packed, ((0, 4), (0, 0)))


def embeddings(level, position):
    level_emb = sinusoid(level.astype(F32)).reshape(STEPS, TM, 8)
    position_emb = sinusoid(position.astype(F32)).reshape(STEPS, TM, 8)
    rest = jnp.zeros((STEPS, TM, 4), F32)
    emb = jnp.concatenate([level_emb, position_emb, rest], axis=2).astype(BF16)
    half = jnp.eye(2, dtype=BF16)[:, None, None, None, :]
    emb = (emb[None, :, :, :, None] * half).reshape(2, STEPS, WIDE)
    return jnp.pad(emb, ((0, 0), (0, 14), (0, 0)))


def own_mods(mod_gain, mod_bias, tile):
    mods = jnp.concatenate([mod_gain, mod_bias, jnp.zeros((2, D), F32)], axis=0)
    mods = lax.dynamic_slice_in_dim(mods.reshape(8, TILE, HEAD), tile, 1, axis=1)
    return jnp.pad(mods.reshape(8, 2, ROWS), ((0, 0), (0, 0), (0, 4))).reshape(8, 80).T


def per_device(
    latents, new_frames, levels, offset, w_in, w_qkv, w_o, w_out, w_time, w_pos,
    mod_gain, mod_bias, refiner,
):
    frame = lax.axis_index("tm")
    tile = lax.axis_index("tile")
    spot = tile.astype(jnp.int32)[None]
    mix = refiner.reshape(C, 27 * C)
    latent = latents[0]
    level = levels[:, 0]
    sigma_now = sigma_of(level)
    drop = sigma_of(level - 1) - sigma_now
    scale_in = lax.rsqrt(1.0 + sigma_now * sigma_now)

    packed = packed_weights(w_in, w_qkv, w_o, w_out, w_time, w_pos)
    rows = exchanged(jnp.broadcast_to(packed[None], (TM,) + packed.shape), "tm")
    rows = rows.reshape(WIDE, 384)

    patches = exchanged(prep(scale_in[0:1], latent), "tile")
    marked = jnp.concatenate([latent, jnp.full((1, C, LANES), drop[0], F32)], axis=0)
    marked = shifted(marked, "tm", -1)

    steps = jnp.arange(STEPS, dtype=jnp.int32)
    emb = embeddings(level, offset + frame + steps)
    pay, out_t = spread(rows, emb, own_mods(mod_gain, mod_bias, tile))
    feat = exchanged(pay, "tile").reshape(WIDE, LANES)

    first, second, gram = fold(feat, rows)
    folded = [exchanged(first, "tile"), exchanged(second, "tile")]

    both = jnp.stack([out_t, swapped(out_t, "tile", 8)])
    four = jnp.concatenate([both] + [swapped(both, "tile", 2 * k) for k in (1, 2, 3)])
    other = swapped(four, "tile", 1)
    four = four.reshape(8 * 96, WIDE)
    other = other.reshape(8 * 96, WIDE)

    for step in range(STEPS):
        n, mvt = heads(folded[step])
        noise = frame_block(step, spot, patches, gram, n, mvt, feat, four, other)
        if step == 0:
            frames = jnp.stack([noise, shifted(noise, "tm", -1), shifted(noise, "tm", -2)])
            last = (frame == TM - 1).astype(jnp.int32)[None]
            latent, patches = middle(
                scale_in[1:2], last, with_rows(frames), marked, new_frames[0], mix
            )
            patches = exchanged(patches, "tile")
        else:
            frames = jnp.stack([shifted(noise, "tm", 1), noise, shifted(noise, "tm", -1)])
            return finish(drop[1:2], with_rows(frames), latent, mix)[None]


def solution(mesh):
    in_specs = (
        P("tm", "tile", None, None),
        P(None, "tile", None, None),
        P(None, "tm"),
        P(),
        P("tm", "tile"),
        P("tm", "tile"),
        P("tm", "tile"),
        P("tm", "tile"),
        P("tm", "tile"),
        P("tm", "tile"),
        P(),
        P(),
        P(),
    )
    out_specs = P("tm", "tile", None, None)
    return jax.shard_map(
        per_device, mesh=mesh, in_specs=in_specs, out_specs=out_specs, check_vma=False
    )
```

```python
import functools
import math

import jax
import jax.numpy as jnp
import numpy as np
from jax import lax
from jax.experimental import pallas as pl
from jax.experimental.pallas import tpu as pltpu
from jax.sharding import PartitionSpec as P

D = 1152
HEADS = 16
HEAD = 72
C = 16
PF = 64
FREQ = 256
STEPS = 2
LEVELS = 64
TM = 32
TILE = 16
ROWS = 36
TOK = 128
LANES = 128
SPAN = TILE * TOK
WIDE = 32 * 40

SIGMA_LOW = 0.02
SIGMA_RATIO = 1000.0
NORM_EPS = 1e-06

AXES = ("zl", "y", "zh", "x", "core")
SPLIT = (4, 8, 2, 4, 2)
TM_AXES = AXES[:2]
TILE_AXES = AXES[2:]

F32 = jnp.float32
BF16 = jnp.bfloat16
HIGHEST = lax.Precision.HIGHEST


def swapped(block, axis):
    return lax.ppermute(block, axis, [(0, 1), (1, 0)])


def shifted(block, axis, distance):
    devices = range(lax.axis_size(axis))
    route = [(i - distance, i) for i in devices if i - distance in devices]
    return lax.ppermute(block, axis, route)


def exchanged(copies, axis):
    return lax.all_to_all(copies, axis, split_axis=0, concat_axis=0, tiled=True)


def sigma_of(level_ids):
    scaled_level = level_ids.astype(F32) / LEVELS
    return jnp.where(
        level_ids > 0, SIGMA_LOW * jnp.exp(math.log(SIGMA_RATIO) * scaled_level), F32(0.0)
    )


def sinusoid(values):
    half_freq = FREQ // 2
    frequency = jnp.exp(-math.log(10000.0) * jnp.arange(half_freq, dtype=F32) / half_freq)
    angles = values[:, None] * frequency[None, :]
    return jnp.concatenate([jnp.cos(angles), jnp.sin(angles)], axis=1)


def nn(a, b, precision=None):
    return lax.dot_general(
        a, b, (((1,), (0,)), ((), ())), preferred_element_type=F32, precision=precision
    )


def nt(a, b):
    return lax.dot_general(a, b, (((1,), (1,)), ((), ())), preferred_element_type=F32)


def tn(a, b):
    return lax.dot_general(a, b, (((0,), (0,)), ((), ())), preferred_element_type=F32)


def lane_of(shape):
    return lax.broadcasted_iota(jnp.int32, shape, 1)


def spread_matrix(shape, token_dim, hp, b, dtype):
    token = lax.broadcasted_iota(jnp.int32, shape, token_dim)
    col = lax.broadcasted_iota(jnp.int32, shape, 1 - token_dim)
    hit = col + 128 * hp == 2 * token + b
    return jnp.where(hit, 1.0, 0.0).astype(dtype)


def patch_rows(scaled):
    halves = []
    for b in range(2):
        total = None
        for hp in range(2):
            rows = scaled[2 * hp : 2 * hp + 2].reshape(2 * C, LANES)
            term = nn(rows, spread_matrix((LANES, TOK), 1, hp, b, BF16))
            total = term if total is None else total + term
        halves.append(total)
    return jnp.concatenate(halves, axis=0).astype(BF16)


def prep_kernel(scalar_ref, lat_ref, out_ref):
    scaled = (lat_ref[...] * scalar_ref[0]).astype(BF16)
    rows = patch_rows(scaled)
    for t in range(TILE):
        out_ref[t] = rows


def columns_around(x):
    lane = lax.broadcasted_iota(jnp.int32, (C, LANES), 1)
    before = jnp.where(lane == 0, 0.0, pltpu.roll(x, 1, 1))
    after = jnp.where(lane == LANES - 1, 0.0, pltpu.roll(x, LANES - 1, 1))
    return jnp.concatenate([before, x, after], axis=0)


def convolved(frames, mix_ref):
    around = [[None if x is None else columns_around(x) for x in rows] for rows in frames]
    blank = jnp.zeros((3 * C, LANES), F32)
    columns = []
    for r in range(len(frames[0]) - 2):
        pieces = [
            blank if around[td][r + dr] is None else around[td][r + dr]
            for td in range(3)
            for dr in range(3)
        ]
        columns.append(jnp.concatenate(pieces, axis=0))
    mixed = nn(mix_ref[...], jnp.concatenate(columns, axis=1), HIGHEST)
    return [mixed[:, r * LANES : (r + 1) * LANES] for r in range(len(columns))]


def middle_kernel(
    scalar_ref, flag_ref, noise_ref, next_ref, after_ref, lat_ref, new_ref, mix_ref,
    lat_out, edge_out, patch_out,
):
    frames = [
        [None, None] + [ref[r] for r in range(4)] + [None, None]
        for ref in (noise_ref, next_ref, after_ref)
    ]
    mixed = convolved(frames, mix_ref)
    last = flag_ref[0] == 1
    drop = lat_ref[4, 0:1, :]
    rows = []
    for r in range(4):
        moved = lat_ref[r] + drop * (next_ref[r] + mixed[r + 1])
        rows.append(jnp.where(last, new_ref[r], moved))
        lat_out[r] = rows[r]
    above = jnp.where(last, 0.0, drop * mixed[0])
    below = jnp.where(last, 0.0, drop * mixed[5])
    edge_out[0] = above
    edge_out[1] = below
    patches = patch_rows((jnp.stack(rows) * scalar_ref[0]).astype(BF16))
    above = (above * scalar_ref[0]).astype(BF16)
    below = (below * scalar_ref[0]).astype(BF16)
    edges = [
        nn(above, spread_matrix((LANES, TOK), 1, 0, b, BF16))
        + nn(below, spread_matrix((LANES, TOK), 1, 1, b, BF16))
        for b in range(2)
    ]
    patches = jnp.concatenate([patches, jnp.concatenate(edges, axis=0).astype(BF16)], axis=0)
    for t in range(TILE):
        patch_out[t] = patches


def final_kernel(
    scalar_ref, before_ref, noise_ref, next_ref, up_ref, down_ref, lat_ref, above_ref, below_ref,
    mix_ref, out_ref,
):
    frames = [
        [up_ref[td]] + [ref[r] for r in range(4)] + [down_ref[td]]
        for td, ref in enumerate((before_ref, noise_ref, next_ref))
    ]
    mixed = convolved(frames, mix_ref)
    for r in range(4):
        latent = lat_ref[r]
        if r == 0:
            latent = latent + above_ref[...]
        if r == 3:
            latent = latent + below_ref[...]
        out_ref[r] = latent + scalar_ref[0] * (noise_ref[r] + mixed[r])


def spread_kernel(x_ref, pick_ref, emb_ref, mod_ref, order_ref, pay_ref, out_t_ref):
    out_t_ref[...] = nt(order_ref[...], x_ref[:, 256:384]).astype(BF16)
    cols = x_ref[:, 128:256]
    halves = []
    for h in range(2):
        found = jnp.concatenate(
            [nn(pick_ref[h], cols), nn(emb_ref[h], cols), jnp.zeros((48, LANES), F32)], axis=0
        )
        turned = pltpu.roll(found, 40, 1).T[0:40]
        mod = mod_ref[40 * h : 40 * h + 40]
        lane = lane_of((40, LANES))
        valid = lax.broadcasted_iota(jnp.int32, (40, LANES), 0) < ROWS
        block = jnp.where(lane < PF, turned, jnp.where(lane == 76, 1.0, 0.0))
        for step in range(STEPS):
            hidden = turned[:, PF + step : PF + step + 1]
            condition = hidden / (1.0 + jnp.exp(-hidden))
            for j, kind in enumerate((1, 0, 2)):
                value = condition * mod[:, kind : kind + 1] + mod[:, 3 + kind : 4 + kind]
                if kind == 1:
                    value = value + 1.0
                upper = value.astype(BF16).astype(F32)
                block = jnp.where(lane == PF + 3 * step + j, upper, block)
                block = jnp.where(lane == PF + 6 + 3 * step + j, value - upper, block)
        halves.append(jnp.where(valid, block, 0.0))
    pay = jnp.concatenate(halves, axis=0).astype(BF16)
    for t in range(TILE):
        pay_ref[t] = pay


def fold_kernel(feat_ref, x_ref, first_ref, second_ref, gram_ref):
    lane = lane_of((WIDE, LANES))
    feat = feat_ref[...].astype(F32)
    mods = feat + pltpu.roll(feat, LANES - 6, 1)
    wide = jnp.where(lane < PF, feat, 0.0)
    mean = jnp.sum(wide, axis=0, keepdims=True) * (1.0 / D)
    centred = (wide - mean) * feat[:, 76:77]
    upper = centred.astype(BF16)
    lower = (centred - upper.astype(F32)).astype(BF16)
    gram = tn(upper, upper) + tn(upper, lower) + tn(lower, upper)
    gram_ref[...] = gram[0:PF, 0:PF]
    for step, out_ref in enumerate((first_ref, second_ref)):
        at = PF + 3 * step
        lines = jnp.where(
            lane < PF,
            centred * mods[:, at : at + 1],
            jnp.where(lane == PF, mods[:, at + 1 : at + 2], 0.0),
        )
        upper = lines.astype(BF16)
        lower = (lines - upper.astype(F32)).astype(BF16)
        weights = x_ref[:, 0:256]
        folded = tn(weights, upper) + tn(weights, lower)
        unit = [folded[HEAD * j : HEAD * j + HEAD] for j in range(3)]
        spot = lane_of((HEAD, LANES))
        top = jnp.where(spot < PF, unit[0], pltpu.roll(unit[1], PF, 1))
        low = jnp.where(spot < PF, unit[2], 0.0)
        low = jnp.where(spot == PF, unit[0], low)
        low = jnp.where(spot == PF + 1, pltpu.roll(unit[1], 1, 1), low)
        low = jnp.where(spot == PF + 2, pltpu.roll(unit[2], 2, 1), low)
        packed = jnp.concatenate([top, low], axis=0).astype(BF16)
        for t in range(TILE):
            out_ref[t] = packed


def heads_kernel(folded_ref, widen_ref, n_ref, mvt_ref, units):
    spot = lane_of((HEAD, LANES))
    for t in range(TILE):
        both = folded_ref[t].astype(F32)
        top, low = both[0:HEAD], both[HEAD : 2 * HEAD]
        parts = (
            (top, low),
            (pltpu.roll(top, PF, 1), pltpu.roll(low, LANES - 1, 1)),
            (low, pltpu.roll(low, LANES - 2, 1)),
        )
        for j, (main, bias) in enumerate(parts):
            unit = jnp.where(spot < PF, main, jnp.where(spot == PF, bias, 0.0))
            units[3 * t + j] = unit
    fold_scale = math.log2(math.e) / math.sqrt(HEAD)
    for h in range(HEADS):
        q, k, v = (units[HEADS * kind + h].astype(BF16) for kind in range(3))
        n_ref[h] = (tn(q, k) * fold_scale).astype(BF16)
        mvt_ref[h] = nn(widen_ref[...], v).astype(BF16)


def with_edges(pt_ref, j):
    patches = pt_ref[j].astype(F32)[0:PF]
    lane = lane_of((2 * C, LANES))
    blank = jnp.zeros((2 * C, LANES), F32)
    first, last = blank, blank
    if j > 0:
        edge = pltpu.roll(pt_ref[j - 1].astype(F32)[PF : PF + 2 * C], PF, 1)
        first = jnp.where(lane < PF, edge, 0.0)
    if j < TILE - 1:
        edge = pltpu.roll(pt_ref[j + 1].astype(F32)[PF : PF + 2 * C], PF, 1)
        last = jnp.where(lane >= PF, edge, 0.0)
    added = jnp.concatenate([first[0:C], last[0:C], first[C:], last[C:]], axis=0)
    return (patches + added).astype(BF16)


def attend_kernel(
    edges, spot_ref, pt_ref, gram_ref, n_ref, mvt_ref, att_ref, own_ref, keys_t, keys, held
):
    me = spot_ref[0]
    row = lax.broadcasted_iota(jnp.int32, (PF, TOK), 0)
    ones = jnp.where(row == 0, 1.0, 0.0).astype(F32)
    for j in range(TILE):
        rounded = with_edges(pt_ref, j) if edges else pt_ref[j]
        held[j] = rounded
        patches = rounded.astype(F32)
        spread = jnp.sum(patches * nn(gram_ref[...], patches, HIGHEST), axis=0, keepdims=True)
        unit = patches * lax.rsqrt(jnp.maximum(spread, 0.0) * (1.0 / D) + NORM_EPS)
        wide = jnp.concatenate([unit, ones], axis=0)
        keys_t[:, j * TOK : (j + 1) * TOK] = wide.astype(BF16)
        keys[j * TOK : (j + 1) * TOK, :] = wide.T.astype(BF16)
    own_ref[...] = held[me]

    def two_heads(pair):
        own = keys[pl.ds(pl.multiple_of(me * TOK, TOK), TOK), :]
        queries = jnp.concatenate(
            [nn(own, n_ref[2 * pair]), nn(own, n_ref[2 * pair + 1])], axis=0
        ).astype(BF16)
        scores = nn(queries, keys_t[...])
        highest = jnp.max(scores, axis=1, keepdims=True)
        weights = jnp.exp2(scores - highest).astype(BF16)
        summed = nn(weights, keys[...])
        mean = (summed / summed[:, PF : PF + 1]).astype(BF16)
        for k in range(2):
            head = 2 * pair + k
            value = nt(mvt_ref[head], mean[k * TOK : (k + 1) * TOK])
            att_ref[pl.ds(pl.multiple_of(head * 80, 80), 80), :] = value.astype(BF16)

    @pl.loop(0, HEADS // 4)
    def _(i):
        two_heads(2 * i)
        two_heads(2 * i + 1)


def output_kernel(
    step, spot_ref, att_ref, own_ref, feat_ref, wot_ref, wot2_ref, out_ref, stream_ref
):
    me = spot_ref[0]
    attended = att_ref[...]
    for c, ref in enumerate((wot_ref, wot2_ref)):
        delta = nn(ref[...], attended)
        for b in range(8):
            tile = ((me ^ (8 * (b % 2))) & 8) + 2 * (b // 2) + ((me & 1) ^ c)
            rows = pl.ds(pl.multiple_of(tile * 80, 80), 80)
            stream_ref[rows, :] = delta[80 * b : 80 * b + 80]
    feat = feat_ref[...]
    own = jnp.concatenate([own_ref[...], jnp.zeros((PF, TOK), BF16)], axis=0)
    at = PF + 3 * step + 2
    gate = feat[:, at : at + 1].astype(F32) + feat[:, at + 6 : at + 7].astype(F32)
    valid = feat[:, 76:77].astype(F32)
    stream = (nn(feat, own) + gate * stream_ref[...]) * valid
    mean = jnp.sum(stream, axis=0, keepdims=True) * (1.0 / D)
    center = (stream - mean) * valid
    spread = jnp.sum(center * center, axis=0, keepdims=True) * (1.0 / D)
    final = (center * lax.rsqrt(spread + NORM_EPS)).astype(BF16)
    out_rows = [
        ref[80 * b + 32 : 80 * b + 48, :] for ref in (wot_ref, wot2_ref) for b in range(8)
    ]
    noise = nn(jnp.concatenate(out_rows, axis=0), final)
    feature = lax.broadcasted_iota(jnp.int32, (PF, 256), 0)
    source = lane_of((PF, 256))
    block = source >> 4
    tile = ((me ^ ((block & 1) << 3)) & 8) + (block & 6) + ((me & 1) ^ (block >> 3))
    q = (source & 15) - 4
    wanted = ((q & 1) << 5) + ((q >> 1) << 4) + tile
    order = jnp.where((q >= 0) & (q < 4) & (feature == wanted), 1.0, 0.0).astype(F32)
    noise = nn(order, noise, HIGHEST)
    for hp in range(2):
        rows = None
        for b in range(2):
            term = nn(
                noise[b * 32 : (b + 1) * 32], spread_matrix((TOK, LANES), 0, hp, b, F32), HIGHEST
            )
            rows = term if rows is None else rows + term
        out_ref[2 * hp] = rows[0:C]
        out_ref[2 * hp + 1] = rows[C : 2 * C]


VMEM = pl.BlockSpec(memory_space=pltpu.VMEM)
SMEM = pl.BlockSpec(memory_space=pltpu.SMEM)


def spread(x, emb, mod):
    return pl.pallas_call(
        spread_kernel,
        out_shape=(
            jax.ShapeDtypeStruct((TILE, 80, LANES), BF16),
            jax.ShapeDtypeStruct((80, WIDE), BF16),
        ),
        in_specs=[VMEM] * 5,
        out_specs=(VMEM, VMEM),
        compiler_params=pltpu.CompilerParams(vmem_limit_bytes=32 * 1024 * 1024),
        name="spread",
    )(x, jnp.asarray(PICK, BF16), emb, mod, jnp.asarray(ORDER, BF16))


def fold(feat, x):
    folded = jax.ShapeDtypeStruct((TILE, 2 * HEAD, LANES), BF16)
    return pl.pallas_call(
        fold_kernel,
        out_shape=(folded, folded, jax.ShapeDtypeStruct((PF, PF), F32)),
        in_specs=[VMEM] * 2,
        out_specs=(VMEM,) * 3,
        compiler_params=pltpu.CompilerParams(vmem_limit_bytes=32 * 1024 * 1024),
        name="fold",
    )(feat, x)


def heads(folded):
    return pl.pallas_call(
        heads_kernel,
        out_shape=(
            jax.ShapeDtypeStruct((HEADS, LANES, LANES), BF16),
            jax.ShapeDtypeStruct((HEADS, 80, LANES), BF16),
        ),
        in_specs=[VMEM] * 2,
        out_specs=(VMEM,) * 2,
        scratch_shapes=[pltpu.VMEM((3 * HEADS, HEAD, LANES), F32)],
        compiler_params=pltpu.CompilerParams(vmem_limit_bytes=32 * 1024 * 1024),
        name="heads",
    )(folded, jnp.asarray(ORDER[:, 0:HEAD], BF16))


def attend(edges, spot, pt, gram, n, mvt):
    return pl.pallas_call(
        functools.partial(attend_kernel, edges),
        out_shape=(
            jax.ShapeDtypeStruct((WIDE, TOK), BF16),
            jax.ShapeDtypeStruct((PF, TOK), BF16),
        ),
        in_specs=[SMEM] + [VMEM] * 4,
        out_specs=(VMEM, VMEM),
        scratch_shapes=[
            pltpu.VMEM((LANES, SPAN), BF16),
            pltpu.VMEM((SPAN, LANES), BF16),
            pltpu.VMEM((TILE, PF, TOK), BF16),
        ],
        compiler_params=pltpu.CompilerParams(vmem_limit_bytes=40 * 1024 * 1024),
        cost_estimate=pl.CostEstimate(
            flops=4 * 2 * SPAN * SPAN * LANES,
            bytes_accessed=8 * SPAN * LANES,
            transcendentals=SPAN * SPAN,
        ),
        name="attend",
    )(spot, pt, gram, n, mvt)


def output(step, spot, att, own, feat, wot, wot2):
    return pl.pallas_call(
        functools.partial(output_kernel, step),
        out_shape=jax.ShapeDtypeStruct((4, C, LANES), F32),
        in_specs=[SMEM] + [VMEM] * 5,
        out_specs=VMEM,
        scratch_shapes=[pltpu.VMEM((WIDE, TOK), F32)],
        compiler_params=pltpu.CompilerParams(vmem_limit_bytes=32 * 1024 * 1024),
        name="output",
    )(spot, att, own, feat, wot, wot2)


def prep(scale_in, latent):
    return pl.pallas_call(
        prep_kernel,
        out_shape=jax.ShapeDtypeStruct((TILE, PF, TOK), BF16),
        in_specs=[SMEM, VMEM],
        out_specs=VMEM,
        name="prep",
    )(scale_in, latent)


def middle(scale_in, last, noise, following, after, lat, new, mix):
    return pl.pallas_call(
        middle_kernel,
        out_shape=(
            jax.ShapeDtypeStruct((4, C, LANES), F32),
            jax.ShapeDtypeStruct((2, C, LANES), F32),
            jax.ShapeDtypeStruct((TILE, PF + 2 * C, TOK), BF16),
        ),
        in_specs=[SMEM, SMEM] + [VMEM] * 6,
        out_specs=(VMEM,) * 3,
        compiler_params=pltpu.CompilerParams(vmem_limit_bytes=32 * 1024 * 1024),
        name="middle",
    )(scale_in, last, noise, following, after, lat, new, mix)


def finish(drop, before, noise, following, up, down, lat, above, below, mix):
    return pl.pallas_call(
        final_kernel,
        out_shape=jax.ShapeDtypeStruct((4, C, LANES), F32),
        in_specs=[SMEM] + [VMEM] * 9,
        out_specs=VMEM,
        compiler_params=pltpu.CompilerParams(vmem_limit_bytes=32 * 1024 * 1024),
        name="finish",
    )(drop, before, noise, following, up, down, lat, above, below, mix)


def pick_matrix():
    pick = np.zeros((2, 2, 2, C, TM, 20, 2), np.float32)
    for h in range(2):
        for b in range(2):
            for a in range(2):
                for c in range(C):
                    pick[h, b, a, c, 2 * c + a, 16 + b, h] = 1.0
    return pick.reshape(2, PF, WIDE)


def order_matrix():
    order = np.zeros((80, LANES), np.float32)
    for j in range(ROWS):
        order[j, j] = 1.0
        order[40 + j, ROWS + j] = 1.0
    for j in range(4):
        order[ROWS + j, HEAD + j] = 1.0
    return order


PICK = pick_matrix()
ORDER = order_matrix()


def packed_weights(w_in, w_qkv, w_o, w_out, w_time, w_pos):
    small = jnp.concatenate([w_time, w_pos, w_in], axis=0).reshape(ROWS, ROWS)
    gap = jnp.zeros((ROWS, 4), BF16)
    tail = jnp.zeros((ROWS, 52), BF16)
    packed = jnp.concatenate([w_qkv, small, gap, w_o, w_out, tail], axis=1)
    return jnp.pad(packed, ((0, 4), (0, 0)))


def embeddings(level, position):
    level_emb = sinusoid(level.astype(F32)).reshape(STEPS, TM, 8)
    position_emb = sinusoid(position.astype(F32)).reshape(STEPS, TM, 8)
    rest = jnp.zeros((STEPS, TM, 4), F32)
    emb = jnp.concatenate([level_emb, position_emb, rest], axis=2).astype(BF16)
    half = jnp.eye(2, dtype=BF16)[:, None, None, None, :]
    emb = (emb[None, :, :, :, None] * half).reshape(2, STEPS, WIDE)
    return jnp.pad(emb, ((0, 0), (0, 14), (0, 0)))


def own_mods(mod_gain, mod_bias, tile):
    mods = jnp.concatenate([mod_gain, mod_bias, jnp.zeros((2, D), F32)], axis=0)
    mods = lax.dynamic_slice_in_dim(mods.reshape(8, TILE, HEAD), tile, 1, axis=1)
    return jnp.pad(mods.reshape(8, 2, ROWS), ((0, 0), (0, 0), (0, 4))).reshape(8, 80).T


def per_device(
    latents, new_frames, levels, offset, w_in, w_qkv, w_o, w_out, w_time, w_pos,
    mod_gain, mod_bias, refiner,
):
    frame = lax.axis_index(TM_AXES)
    tile = lax.axis_index(TILE_AXES)
    spot = tile.astype(jnp.int32)[None]
    mix = refiner.reshape(C, 27 * C)
    latent = latents[0]
    level = levels[:, 0]
    sigma_now = sigma_of(level)
    drop = sigma_of(level - 1) - sigma_now
    scale_in = lax.rsqrt(1.0 + sigma_now * sigma_now)

    packed = packed_weights(w_in, w_qkv, w_o, w_out, w_time, w_pos)
    rows = exchanged(jnp.broadcast_to(packed[None], (TM,) + packed.shape), TM_AXES)
    rows = rows.reshape(WIDE, 384)

    patches = exchanged(prep(scale_in[0:1], latent), TILE_AXES)
    marked = jnp.concatenate([latent, jnp.full((1, C, LANES), drop[0], F32)], axis=0)
    marked = shifted(marked, TM_AXES, -1)
    steps = jnp.arange(STEPS, dtype=jnp.int32)
    emb = embeddings(level, offset + frame + steps)
    mods = own_mods(mod_gain, mod_bias, tile)
    rows, patches, marked, mix = lax.optimization_barrier((rows, patches, marked, mix))

    pay, out_t = spread(rows, emb, mods)
    feat = exchanged(pay, TILE_AXES).reshape(WIDE, LANES)
    feat, out_t = lax.optimization_barrier((feat, out_t))

    first, second, gram = fold(feat, rows)
    n, mvt = heads(exchanged(first, TILE_AXES))

    both = jnp.stack([out_t, swapped(out_t, "zh")])
    four = exchanged(jnp.broadcast_to(both[None], (4,) + both.shape), "x")
    other = swapped(four, "core").reshape(8 * 80, WIDE)
    four = four.reshape(8 * 80, WIDE)

    att, own = attend(False, spot, patches, gram, n, mvt)
    noise = output(0, spot, att, own, feat, four, other)

    following, after = shifted(noise, TM_AXES, -1), shifted(noise, TM_AXES, -2)
    last = (frame == TM - 1).astype(jnp.int32)[None]
    latent, edges, patches = middle(
        scale_in[1:2], last, noise, following, after, marked, new_frames[0], mix
    )
    patches, second = lax.optimization_barrier((patches, second))
    patches = exchanged(patches, TILE_AXES)
    n, mvt = heads(exchanged(second, TILE_AXES))
    above = shifted(edges[1], TILE_AXES, 1)
    below = shifted(edges[0], TILE_AXES, -1)

    att, own = attend(True, spot, patches, gram, n, mvt)
    noise = output(1, spot, att, own, feat, four, other)
    frames = [shifted(noise, TM_AXES, 1), noise, shifted(noise, TM_AXES, -1)]
    up = shifted(jnp.stack([x[3] for x in frames]), TILE_AXES, 1)
    down = shifted(jnp.stack([x[0] for x in frames]), TILE_AXES, -1)
    return finish(drop[1:2], *frames, up, down, latent, above, below, mix)[None]


def solution(mesh):
    mesh = jax.sharding.Mesh(mesh.devices.reshape(SPLIT), AXES)
    rows, cols = TM_AXES, TILE_AXES
    in_specs = (
        P(rows, cols, None, None),
        P(None, cols, None, None),
        P(None, rows),
        P(),
        P(rows, cols),
        P(rows, cols),
        P(rows, cols),
        P(rows, cols),
        P(rows, cols),
        P(rows, cols),
        P(),
        P(),
        P(),
    )
    out_specs = P(rows, cols, None, None)
    return jax.shard_map(
        per_device, mesh=mesh, in_specs=in_specs, out_specs=out_specs, check_vma=False
    )
```

```python
import functools
import math

import jax
import jax.numpy as jnp
import numpy as np
from jax import lax
from jax.experimental import pallas as pl
from jax.experimental.pallas import tpu as pltpu
from jax.sharding import PartitionSpec as P

D = 1152
HEADS = 16
HEAD = 72
C = 16
PF = 64
FREQ = 256
STEPS = 2
LEVELS = 64
TM = 32
TILE = 16
ROWS = 36
TOK = 128
LANES = 128
SPAN = TILE * TOK
WIDE = 32 * 40

SIGMA_LOW = 0.02
SIGMA_RATIO = 1000.0
NORM_EPS = 1e-06

AXES = ("zl", "y", "zh", "x", "core")
SPLIT = (4, 8, 2, 4, 2)
TM_AXES = AXES[:2]
TILE_AXES = AXES[2:]

F32 = jnp.float32
BF16 = jnp.bfloat16
HIGHEST = lax.Precision.HIGHEST


def swapped(block, axis):
    return lax.ppermute(block, axis, [(0, 1), (1, 0)])


def shifted(block, axis, distance):
    devices = range(lax.axis_size(axis))
    route = [(i - distance, i) for i in devices if i - distance in devices]
    return lax.ppermute(block, axis, route)


def exchanged(copies, axis):
    return lax.all_to_all(copies, axis, split_axis=0, concat_axis=0, tiled=True)


def sigma_of(level_ids):
    scaled_level = level_ids.astype(F32) / LEVELS
    return jnp.where(
        level_ids > 0, SIGMA_LOW * jnp.exp(math.log(SIGMA_RATIO) * scaled_level), F32(0.0)
    )


def sinusoid(values):
    half_freq = FREQ // 2
    frequency = jnp.exp(-math.log(10000.0) * jnp.arange(half_freq, dtype=F32) / half_freq)
    angles = values[:, None] * frequency[None, :]
    return jnp.concatenate([jnp.cos(angles), jnp.sin(angles)], axis=1)


def nn(a, b, precision=None):
    return lax.dot_general(
        a, b, (((1,), (0,)), ((), ())), preferred_element_type=F32, precision=precision
    )


def nt(a, b):
    return lax.dot_general(a, b, (((1,), (1,)), ((), ())), preferred_element_type=F32)


def tn(a, b):
    return lax.dot_general(a, b, (((0,), (0,)), ((), ())), preferred_element_type=F32)


def lane_of(shape):
    return lax.broadcasted_iota(jnp.int32, shape, 1)


def spread_matrix(shape, token_dim, hp, b, dtype):
    token = lax.broadcasted_iota(jnp.int32, shape, token_dim)
    col = lax.broadcasted_iota(jnp.int32, shape, 1 - token_dim)
    hit = col + 128 * hp == 2 * token + b
    return jnp.where(hit, 1.0, 0.0).astype(dtype)


def patch_rows(scaled):
    halves = []
    for b in range(2):
        total = None
        for hp in range(2):
            rows = scaled[2 * hp : 2 * hp + 2].reshape(2 * C, LANES)
            term = nn(rows, spread_matrix((LANES, TOK), 1, hp, b, BF16))
            total = term if total is None else total + term
        halves.append(total)
    return jnp.concatenate(halves, axis=0).astype(BF16)


def prep_kernel(scalar_ref, lat_ref, out_ref):
    scaled = (lat_ref[...] * scalar_ref[0]).astype(BF16)
    out_ref[...] = patch_rows(scaled)


def columns_around(x):
    lane = lax.broadcasted_iota(jnp.int32, (C, LANES), 1)
    before = jnp.where(lane == 0, 0.0, pltpu.roll(x, 1, 1))
    after = jnp.where(lane == LANES - 1, 0.0, pltpu.roll(x, LANES - 1, 1))
    return jnp.concatenate([before, x, after], axis=0)


def convolved(frames, mix_ref):
    around = [[None if x is None else columns_around(x) for x in rows] for rows in frames]
    blank = jnp.zeros((3 * C, LANES), F32)
    columns = []
    for r in range(len(frames[0]) - 2):
        pieces = [
            blank if around[td][r + dr] is None else around[td][r + dr]
            for td in range(3)
            for dr in range(3)
        ]
        columns.append(jnp.concatenate(pieces, axis=0))
    mixed = nn(mix_ref[...], jnp.concatenate(columns, axis=1), HIGHEST)
    return [mixed[:, r * LANES : (r + 1) * LANES] for r in range(len(columns))]


def middle_kernel(
    scalar_ref, flag_ref, noise_ref, next_ref, after_ref, lat_ref, new_ref, mix_ref,
    lat_out, edge_out, patch_out,
):
    frames = [
        [None, None] + [ref[r] for r in range(4)] + [None, None]
        for ref in (noise_ref, next_ref, after_ref)
    ]
    mixed = convolved(frames, mix_ref)
    last = flag_ref[0] == 1
    drop = lat_ref[4, 0:1, :]
    rows = []
    for r in range(4):
        moved = lat_ref[r] + drop * (next_ref[r] + mixed[r + 1])
        rows.append(jnp.where(last, new_ref[r], moved))
        lat_out[r] = rows[r]
    above = jnp.where(last, 0.0, drop * mixed[0])
    below = jnp.where(last, 0.0, drop * mixed[5])
    edge_out[0] = above
    edge_out[1] = below
    patches = patch_rows((jnp.stack(rows) * scalar_ref[0]).astype(BF16))
    above = (above * scalar_ref[0]).astype(BF16)
    below = (below * scalar_ref[0]).astype(BF16)
    edges = [
        nn(above, spread_matrix((LANES, TOK), 1, 0, b, BF16))
        + nn(below, spread_matrix((LANES, TOK), 1, 1, b, BF16))
        for b in range(2)
    ]
    patches = jnp.concatenate([patches, jnp.concatenate(edges, axis=0).astype(BF16)], axis=0)
    for t in range(TILE):
        patch_out[t] = patches


def final_kernel(
    scalar_ref, before_ref, noise_ref, next_ref, up_ref, down_ref, lat_ref, mix_ref, out_ref
):
    frames = [
        [up_ref[td]] + [ref[r] for r in range(4)] + [down_ref[td]]
        for td, ref in enumerate((before_ref, noise_ref, next_ref))
    ]
    mixed = convolved(frames, mix_ref)
    for r in range(4):
        latent = lat_ref[r]
        if r == 0:
            latent = latent + up_ref[3]
        if r == 3:
            latent = latent + down_ref[3]
        out_ref[r] = latent + scalar_ref[0] * (noise_ref[r] + mixed[r])


def spread_kernel(x_ref, pick_ref, emb_ref, mod_ref, order_ref, patch_ref, pay_ref, out_t_ref):
    out_t_ref[...] = nt(order_ref[...], x_ref[:, 256:384]).astype(BF16)
    cols = x_ref[:, 128:256]
    halves = []
    for h in range(2):
        found = jnp.concatenate(
            [nn(pick_ref[h], cols), nn(emb_ref[h], cols), jnp.zeros((48, LANES), F32)], axis=0
        )
        turned = pltpu.roll(found, 40, 1).T[0:40]
        mod = mod_ref[40 * h : 40 * h + 40]
        lane = lane_of((40, LANES))
        valid = lax.broadcasted_iota(jnp.int32, (40, LANES), 0) < ROWS
        block = jnp.where(lane < PF, turned, jnp.where(lane == 76, 1.0, 0.0))
        for step in range(STEPS):
            hidden = turned[:, PF + step : PF + step + 1]
            condition = hidden / (1.0 + jnp.exp(-hidden))
            for j, kind in enumerate((1, 0, 2)):
                value = condition * mod[:, kind : kind + 1] + mod[:, 3 + kind : 4 + kind]
                if kind == 1:
                    value = value + 1.0
                upper = value.astype(BF16).astype(F32)
                block = jnp.where(lane == PF + 3 * step + j, upper, block)
                block = jnp.where(lane == PF + 6 + 3 * step + j, value - upper, block)
        halves.append(jnp.where(valid, block, 0.0))
    pay = jnp.concatenate(halves, axis=0).astype(BF16)
    pay = jnp.concatenate([patch_ref[...], pay], axis=0)
    for t in range(TILE):
        pay_ref[t] = pay


def fold_kernel(step, feat_ref, x_ref, out_ref, *gram_refs):
    lane = lane_of((WIDE, LANES))
    feat = jnp.concatenate([feat_ref[t, PF:].astype(F32) for t in range(TILE)], axis=0)
    mods = feat + pltpu.roll(feat, LANES - 6, 1)
    wide = jnp.where(lane < PF, feat, 0.0)
    mean = jnp.sum(wide, axis=0, keepdims=True) * (1.0 / D)
    centred = (wide - mean) * feat[:, 76:77]
    for gram_ref in gram_refs:
        upper = centred.astype(BF16)
        lower = (centred - upper.astype(F32)).astype(BF16)
        gram = tn(upper, upper) + tn(upper, lower) + tn(lower, upper)
        gram_ref[...] = gram[0:PF, 0:PF]
    at = PF + 3 * step
    lines = jnp.where(
        lane < PF,
        centred * mods[:, at : at + 1],
        jnp.where(lane == PF, mods[:, at + 1 : at + 2], 0.0),
    )
    upper = lines.astype(BF16)
    lower = (lines - upper.astype(F32)).astype(BF16)
    weights = x_ref[:, 0:256]
    folded = tn(weights, upper) + tn(weights, lower)
    unit = [folded[HEAD * j : HEAD * j + HEAD] for j in range(3)]
    spot = lane_of((HEAD, LANES))
    top = jnp.where(spot < PF, unit[0], pltpu.roll(unit[1], PF, 1))
    low = jnp.where(spot < PF, unit[2], 0.0)
    low = jnp.where(spot == PF, unit[0], low)
    low = jnp.where(spot == PF + 1, pltpu.roll(unit[1], 1, 1), low)
    low = jnp.where(spot == PF + 2, pltpu.roll(unit[2], 2, 1), low)
    packed = jnp.concatenate([top, low], axis=0).astype(BF16)
    for t in range(TILE):
        out_ref[t] = packed


def heads_kernel(folded_ref, widen_ref, n_ref, mvt_ref, units):
    spot = lane_of((HEAD, LANES))
    for t in range(TILE):
        both = folded_ref[t].astype(F32)
        top, low = both[0:HEAD], both[HEAD : 2 * HEAD]
        parts = (
            (top, low),
            (pltpu.roll(top, PF, 1), pltpu.roll(low, LANES - 1, 1)),
            (low, pltpu.roll(low, LANES - 2, 1)),
        )
        for j, (main, bias) in enumerate(parts):
            unit = jnp.where(spot < PF, main, jnp.where(spot == PF, bias, 0.0))
            units[3 * t + j] = unit
    fold_scale = math.log2(math.e) / math.sqrt(HEAD)
    for h in range(HEADS):
        q, k, v = (units[HEADS * kind + h].astype(BF16) for kind in range(3))
        n_ref[h] = (tn(q, k) * fold_scale).astype(BF16)
        mvt_ref[h] = nn(widen_ref[...], v).astype(BF16)


def with_edges(pt_ref, j):
    patches = pt_ref[j].astype(F32)[0:PF]
    lane = lane_of((2 * C, LANES))
    blank = jnp.zeros((2 * C, LANES), F32)
    first, last = blank, blank
    if j > 0:
        edge = pltpu.roll(pt_ref[j - 1].astype(F32)[PF : PF + 2 * C], PF, 1)
        first = jnp.where(lane < PF, edge, 0.0)
    if j < TILE - 1:
        edge = pltpu.roll(pt_ref[j + 1].astype(F32)[PF : PF + 2 * C], PF, 1)
        last = jnp.where(lane >= PF, edge, 0.0)
    added = jnp.concatenate([first[0:C], last[0:C], first[C:], last[C:]], axis=0)
    return (patches + added).astype(BF16)


def attend_kernel(
    edges, spot_ref, pt_ref, gram_ref, n_ref, mvt_ref, att_ref, own_ref, keys_t, keys, held
):
    me = spot_ref[0]
    row = lax.broadcasted_iota(jnp.int32, (PF, TOK), 0)
    ones = jnp.where(row == 0, 1.0, 0.0).astype(F32)
    for j in range(TILE):
        rounded = with_edges(pt_ref, j) if edges else pt_ref[j, 0:PF]
        held[j] = rounded
        patches = rounded.astype(F32)
        spread = jnp.sum(patches * nn(gram_ref[...], patches, HIGHEST), axis=0, keepdims=True)
        unit = patches * lax.rsqrt(jnp.maximum(spread, 0.0) * (1.0 / D) + NORM_EPS)
        wide = jnp.concatenate([unit, ones], axis=0)
        keys_t[:, j * TOK : (j + 1) * TOK] = wide.astype(BF16)
        keys[j * TOK : (j + 1) * TOK, :] = wide.T.astype(BF16)
    own_ref[...] = held[me]

    def two_heads(pair):
        own = keys[pl.ds(pl.multiple_of(me * TOK, TOK), TOK), :]
        queries = jnp.concatenate(
            [nn(own, n_ref[2 * pair]), nn(own, n_ref[2 * pair + 1])], axis=0
        ).astype(BF16)
        scores = nn(queries, keys_t[...])
        highest = jnp.max(scores, axis=1, keepdims=True)
        weights = jnp.exp2(scores - highest).astype(BF16)
        summed = nn(weights, keys[...])
        mean = (summed / summed[:, PF : PF + 1]).astype(BF16)
        for k in range(2):
            head = 2 * pair + k
            value = nt(mvt_ref[head], mean[k * TOK : (k + 1) * TOK])
            att_ref[pl.ds(pl.multiple_of(head * 80, 80), 80), :] = value.astype(BF16)

    @pl.loop(0, HEADS // 4)
    def _(i):
        two_heads(2 * i)
        two_heads(2 * i + 1)


def output_kernel(
    step, spot_ref, att_ref, own_ref, feat_ref, wot_ref, wot2_ref, out_ref, stream_ref
):
    me = spot_ref[0]
    attended = att_ref[...]
    for c, ref in enumerate((wot_ref, wot2_ref)):
        delta = nn(ref[...], attended)
        for b in range(8):
            tile = ((me ^ (8 * (b % 2))) & 8) + 2 * (b // 2) + ((me & 1) ^ c)
            rows = pl.ds(pl.multiple_of(tile * 80, 80), 80)
            stream_ref[rows, :] = delta[80 * b : 80 * b + 80]
    feat = jnp.concatenate([feat_ref[t, PF:] for t in range(TILE)], axis=0)
    own = jnp.concatenate([own_ref[...], jnp.zeros((PF, TOK), BF16)], axis=0)
    at = PF + 3 * step + 2
    gate = feat[:, at : at + 1].astype(F32) + feat[:, at + 6 : at + 7].astype(F32)
    valid = feat[:, 76:77].astype(F32)
    stream = (nn(feat, own) + gate * stream_ref[...]) * valid
    mean = jnp.sum(stream, axis=0, keepdims=True) * (1.0 / D)
    center = (stream - mean) * valid
    spread = jnp.sum(center * center, axis=0, keepdims=True) * (1.0 / D)
    final = (center * lax.rsqrt(spread + NORM_EPS)).astype(BF16)
    out_rows = [
        ref[80 * b + 32 : 80 * b + 48, :] for ref in (wot_ref, wot2_ref) for b in range(8)
    ]
    noise = nn(jnp.concatenate(out_rows, axis=0), final)
    feature = lax.broadcasted_iota(jnp.int32, (PF, 256), 0)
    source = lane_of((PF, 256))
    block = source >> 4
    tile = ((me ^ ((block & 1) << 3)) & 8) + (block & 6) + ((me & 1) ^ (block >> 3))
    q = (source & 15) - 4
    wanted = ((q & 1) << 5) + ((q >> 1) << 4) + tile
    order = jnp.where((q >= 0) & (q < 4) & (feature == wanted), 1.0, 0.0).astype(F32)
    noise = nn(order, noise, HIGHEST)
    for hp in range(2):
        rows = None
        for b in range(2):
            term = nn(
                noise[b * 32 : (b + 1) * 32], spread_matrix((TOK, LANES), 0, hp, b, F32), HIGHEST
            )
            rows = term if rows is None else rows + term
        out_ref[2 * hp] = rows[0:C]
        out_ref[2 * hp + 1] = rows[C : 2 * C]


VMEM = pl.BlockSpec(memory_space=pltpu.VMEM)
SMEM = pl.BlockSpec(memory_space=pltpu.SMEM)


def spread(x, emb, mod, patches):
    return pl.pallas_call(
        spread_kernel,
        out_shape=(
            jax.ShapeDtypeStruct((TILE, PF + 80, LANES), BF16),
            jax.ShapeDtypeStruct((80, WIDE), BF16),
        ),
        in_specs=[VMEM] * 6,
        out_specs=(VMEM, VMEM),
        compiler_params=pltpu.CompilerParams(vmem_limit_bytes=32 * 1024 * 1024),
        name="spread",
    )(x, jnp.asarray(PICK, BF16), emb, mod, jnp.asarray(ORDER, BF16), patches)


def fold(step, feat, x):
    shapes = [jax.ShapeDtypeStruct((TILE, 2 * HEAD, LANES), BF16)]
    if step == 0:
        shapes.append(jax.ShapeDtypeStruct((PF, PF), F32))
    return pl.pallas_call(
        functools.partial(fold_kernel, step),
        out_shape=tuple(shapes),
        in_specs=[VMEM] * 2,
        out_specs=(VMEM,) * len(shapes),
        compiler_params=pltpu.CompilerParams(vmem_limit_bytes=32 * 1024 * 1024),
        cost_estimate=pl.CostEstimate(
            flops=4 * WIDE * 256 * LANES, bytes_accessed=8 * WIDE * LANES, transcendentals=0
        ),
        name="fold",
    )(feat, x)


def heads(folded):
    return pl.pallas_call(
        heads_kernel,
        out_shape=(
            jax.ShapeDtypeStruct((HEADS, LANES, LANES), BF16),
            jax.ShapeDtypeStruct((HEADS, 80, LANES), BF16),
        ),
        in_specs=[VMEM] * 2,
        out_specs=(VMEM,) * 2,
        scratch_shapes=[pltpu.VMEM((3 * HEADS, HEAD, LANES), F32)],
        compiler_params=pltpu.CompilerParams(vmem_limit_bytes=32 * 1024 * 1024),
        name="heads",
    )(folded, jnp.asarray(ORDER[:, 0:HEAD], BF16))


def attend(edges, spot, pt, gram, n, mvt):
    return pl.pallas_call(
        functools.partial(attend_kernel, edges),
        out_shape=(
            jax.ShapeDtypeStruct((WIDE, TOK), BF16),
            jax.ShapeDtypeStruct((PF, TOK), BF16),
        ),
        in_specs=[SMEM] + [VMEM] * 4,
        out_specs=(VMEM, VMEM),
        scratch_shapes=[
            pltpu.VMEM((LANES, SPAN), BF16),
            pltpu.VMEM((SPAN, LANES), BF16),
            pltpu.VMEM((TILE, PF, TOK), BF16),
        ],
        compiler_params=pltpu.CompilerParams(vmem_limit_bytes=40 * 1024 * 1024),
        cost_estimate=pl.CostEstimate(
            flops=4 * 2 * SPAN * SPAN * LANES,
            bytes_accessed=8 * SPAN * LANES,
            transcendentals=SPAN * SPAN,
        ),
        name="attend",
    )(spot, pt, gram, n, mvt)


def output(step, spot, att, own, feat, wot, wot2):
    return pl.pallas_call(
        functools.partial(output_kernel, step),
        out_shape=jax.ShapeDtypeStruct((4, C, LANES), F32),
        in_specs=[SMEM] + [VMEM] * 5,
        out_specs=VMEM,
        scratch_shapes=[pltpu.VMEM((WIDE, TOK), F32)],
        compiler_params=pltpu.CompilerParams(vmem_limit_bytes=32 * 1024 * 1024),
        name="output",
    )(spot, att, own, feat, wot, wot2)


def prep(scale_in, latent):
    return pl.pallas_call(
        prep_kernel,
        out_shape=jax.ShapeDtypeStruct((PF, TOK), BF16),
        in_specs=[SMEM, VMEM],
        out_specs=VMEM,
        name="prep",
    )(scale_in, latent)


def middle(scale_in, last, noise, following, after, lat, new, mix):
    return pl.pallas_call(
        middle_kernel,
        out_shape=(
            jax.ShapeDtypeStruct((4, C, LANES), F32),
            jax.ShapeDtypeStruct((2, C, LANES), F32),
            jax.ShapeDtypeStruct((TILE, PF + 2 * C, TOK), BF16),
        ),
        in_specs=[SMEM, SMEM] + [VMEM] * 6,
        out_specs=(VMEM,) * 3,
        compiler_params=pltpu.CompilerParams(vmem_limit_bytes=32 * 1024 * 1024),
        name="middle",
    )(scale_in, last, noise, following, after, lat, new, mix)


def finish(drop, before, noise, following, up, down, lat, mix):
    return pl.pallas_call(
        final_kernel,
        out_shape=jax.ShapeDtypeStruct((4, C, LANES), F32),
        in_specs=[SMEM] + [VMEM] * 7,
        out_specs=VMEM,
        compiler_params=pltpu.CompilerParams(vmem_limit_bytes=32 * 1024 * 1024),
        name="finish",
    )(drop, before, noise, following, up, down, lat, mix)


def pick_matrix():
    pick = np.zeros((2, 2, 2, C, TM, 20, 2), np.float32)
    for h in range(2):
        for b in range(2):
            for a in range(2):
                for c in range(C):
                    pick[h, b, a, c, 2 * c + a, 16 + b, h] = 1.0
    return pick.reshape(2, PF, WIDE)


def order_matrix():
    order = np.zeros((80, LANES), np.float32)
    for j in range(ROWS):
        order[j, j] = 1.0
        order[40 + j, ROWS + j] = 1.0
    for j in range(4):
        order[ROWS + j, HEAD + j] = 1.0
    return order


PICK = pick_matrix()
ORDER = order_matrix()


def packed_weights(w_in, w_qkv, w_o, w_out, w_time, w_pos):
    small = jnp.concatenate([w_time, w_pos, w_in], axis=0).reshape(ROWS, ROWS)
    gap = jnp.zeros((ROWS, 4), BF16)
    tail = jnp.zeros((ROWS, 52), BF16)
    packed = jnp.concatenate([w_qkv, small, gap, w_o, w_out, tail], axis=1)
    return jnp.pad(packed, ((0, 4), (0, 0)))


def embeddings(level, position):
    level_emb = sinusoid(level.astype(F32)).reshape(STEPS, TM, 8)
    position_emb = sinusoid(position.astype(F32)).reshape(STEPS, TM, 8)
    rest = jnp.zeros((STEPS, TM, 4), F32)
    emb = jnp.concatenate([level_emb, position_emb, rest], axis=2).astype(BF16)
    half = jnp.eye(2, dtype=BF16)[:, None, None, None, :]
    emb = (emb[None, :, :, :, None] * half).reshape(2, STEPS, WIDE)
    return jnp.pad(emb, ((0, 0), (0, 14), (0, 0)))


def own_mods(mod_gain, mod_bias, tile):
    mods = jnp.concatenate([mod_gain, mod_bias, jnp.zeros((2, D), F32)], axis=0)
    mods = lax.dynamic_slice_in_dim(mods.reshape(8, TILE, HEAD), tile, 1, axis=1)
    return jnp.pad(mods.reshape(8, 2, ROWS), ((0, 0), (0, 0), (0, 4))).reshape(8, 80).T


def per_device(
    latents, new_frames, levels, offset, w_in, w_qkv, w_o, w_out, w_time, w_pos,
    mod_gain, mod_bias, refiner,
):
    frame = lax.axis_index(TM_AXES)
    tile = lax.axis_index(TILE_AXES)
    spot = tile.astype(jnp.int32)[None]
    mix = refiner.reshape(C, 27 * C)
    latent = latents[0]
    level = levels[:, 0]
    sigma_now = sigma_of(level)
    drop = sigma_of(level - 1) - sigma_now
    scale_in = lax.rsqrt(1.0 + sigma_now * sigma_now)

    packed = packed_weights(w_in, w_qkv, w_o, w_out, w_time, w_pos)
    rows = exchanged(jnp.broadcast_to(packed[None], (TM,) + packed.shape), TM_AXES)
    rows = rows.reshape(WIDE, 384)

    own = prep(scale_in[0:1], latent)
    marked = jnp.concatenate([latent, jnp.full((1, C, LANES), drop[0], F32)], axis=0)
    marked = shifted(marked, TM_AXES, -1)
    steps = jnp.arange(STEPS, dtype=jnp.int32)
    emb = embeddings(level, offset + frame + steps)
    mods = own_mods(mod_gain, mod_bias, tile)
    rows, marked, mix = lax.optimization_barrier((rows, marked, mix))

    pay, out_t = spread(rows, emb, mods, own)
    feat = exchanged(pay, TILE_AXES)

    first, gram = fold(0, feat, rows)
    first, feat, rows, out_t = lax.optimization_barrier((first, feat, rows, out_t))
    first = exchanged(first, TILE_AXES)

    (second,) = fold(1, feat, rows)
    both = jnp.stack([out_t, swapped(out_t, "zh")])
    first, both, second = lax.optimization_barrier((first, both, second))
    n, mvt = heads(first)
    four = exchanged(jnp.broadcast_to(both[None], (4,) + both.shape), "x")
    other = swapped(four, "core").reshape(8 * 80, WIDE)
    four = four.reshape(8 * 80, WIDE)
    second = exchanged(second, TILE_AXES)

    att, own = attend(False, spot, feat, gram, n, mvt)
    att, second = lax.optimization_barrier((att, second))
    noise = output(0, spot, att, own, feat, four, other)

    following, after = shifted(noise, TM_AXES, -1), shifted(noise, TM_AXES, -2)
    last = (frame == TM - 1).astype(jnp.int32)[None]
    latent, edges, patches = middle(
        scale_in[1:2], last, noise, following, after, marked, new_frames[0], mix
    )
    patches = exchanged(patches, TILE_AXES)
    n, mvt = heads(second)

    att, own = attend(True, spot, patches, gram, n, mvt)
    noise = output(1, spot, att, own, feat, four, other)
    frames = [shifted(noise, TM_AXES, 1), noise, shifted(noise, TM_AXES, -1)]
    up = jnp.stack([x[3] for x in frames] + [edges[1]])
    down = jnp.stack([x[0] for x in frames] + [edges[0]])
    up, down = shifted(up, TILE_AXES, 1), shifted(down, TILE_AXES, -1)
    return finish(drop[1:2], *frames, up, down, latent, mix)[None]


def solution(mesh):
    mesh = jax.sharding.Mesh(mesh.devices.reshape(SPLIT), AXES)
    rows, cols = TM_AXES, TILE_AXES
    in_specs = (
        P(rows, cols, None, None),
        P(None, cols, None, None),
        P(None, rows),
        P(),
        P(rows, cols),
        P(rows, cols),
        P(rows, cols),
        P(rows, cols),
        P(rows, cols),
        P(rows, cols),
        P(),
        P(),
        P(),
    )
    out_specs = P(rows, cols, None, None)
    return jax.shard_map(
        per_device, mesh=mesh, in_specs=in_specs, out_specs=out_specs, check_vma=False
    )
```

```python
import functools
import math

import jax
import jax.numpy as jnp
import numpy as np
from jax import lax
from jax.experimental import pallas as pl
from jax.experimental.pallas import tpu as pltpu
from jax.sharding import PartitionSpec as P

D = 1152
HEADS = 16
HEAD = 72
C = 16
PF = 64
FREQ = 256
STEPS = 2
LEVELS = 64
TM = 32
TILE = 16
ROWS = 36
TOK = 128
LANES = 128
SPAN = TILE * TOK
WIDE = 32 * 40

SIGMA_LOW = 0.02
SIGMA_RATIO = 1000.0
NORM_EPS = 1e-06

AXES = ("zl", "y", "zh", "x", "core")
SPLIT = (4, 8, 2, 4, 2)
TM_AXES = AXES[:2]
TILE_AXES = AXES[2:]

F32 = jnp.float32
BF16 = jnp.bfloat16
HIGHEST = lax.Precision.HIGHEST


def swapped(block, axis):
    return lax.ppermute(block, axis, [(0, 1), (1, 0)])


def shifted(block, axis, distance):
    devices = range(lax.axis_size(axis))
    route = [(i - distance, i) for i in devices if i - distance in devices]
    return lax.ppermute(block, axis, route)


def exchanged(copies, axis):
    return lax.all_to_all(copies, axis, split_axis=0, concat_axis=0, tiled=True)


def sigma_of(level_ids):
    scaled_level = level_ids.astype(F32) / LEVELS
    return jnp.where(
        level_ids > 0, SIGMA_LOW * jnp.exp(math.log(SIGMA_RATIO) * scaled_level), F32(0.0)
    )


def sinusoid(values):
    half_freq = FREQ // 2
    frequency = jnp.exp(-math.log(10000.0) * jnp.arange(half_freq, dtype=F32) / half_freq)
    angles = values[:, None] * frequency[None, :]
    return jnp.concatenate([jnp.cos(angles), jnp.sin(angles)], axis=1)


def nn(a, b, precision=None):
    return lax.dot_general(
        a, b, (((1,), (0,)), ((), ())), preferred_element_type=F32, precision=precision
    )


def nt(a, b):
    return lax.dot_general(a, b, (((1,), (1,)), ((), ())), preferred_element_type=F32)


def tn(a, b):
    return lax.dot_general(a, b, (((0,), (0,)), ((), ())), preferred_element_type=F32)


def lane_of(shape):
    return lax.broadcasted_iota(jnp.int32, shape, 1)


def spread_matrix(shape, token_dim, hp, b, dtype):
    token = lax.broadcasted_iota(jnp.int32, shape, token_dim)
    col = lax.broadcasted_iota(jnp.int32, shape, 1 - token_dim)
    hit = col + 128 * hp == 2 * token + b
    return jnp.where(hit, 1.0, 0.0).astype(dtype)


def patch_rows(scaled):
    halves = []
    for b in range(2):
        total = None
        for hp in range(2):
            rows = scaled[2 * hp : 2 * hp + 2].reshape(2 * C, LANES)
            term = nn(rows, spread_matrix((LANES, TOK), 1, hp, b, BF16))
            total = term if total is None else total + term
        halves.append(total)
    return jnp.concatenate(halves, axis=0).astype(BF16)


def prep_kernel(scalar_ref, lat_ref, out_ref):
    scaled = (lat_ref[...] * scalar_ref[0]).astype(BF16)
    out_ref[...] = patch_rows(scaled)


def columns_around(x):
    lane = lax.broadcasted_iota(jnp.int32, (C, LANES), 1)
    before = jnp.where(lane == 0, 0.0, pltpu.roll(x, 1, 1))
    after = jnp.where(lane == LANES - 1, 0.0, pltpu.roll(x, LANES - 1, 1))
    return jnp.concatenate([before, x, after], axis=0)


def convolved(frames, mix_ref):
    around = [[None if x is None else columns_around(x) for x in rows] for rows in frames]
    blank = jnp.zeros((3 * C, LANES), F32)
    columns = []
    for r in range(len(frames[0]) - 2):
        pieces = [
            blank if around[td][r + dr] is None else around[td][r + dr]
            for td in range(3)
            for dr in range(3)
        ]
        columns.append(jnp.concatenate(pieces, axis=0))
    mixed = nn(mix_ref[...], jnp.concatenate(columns, axis=1), HIGHEST)
    return [mixed[:, r * LANES : (r + 1) * LANES] for r in range(len(columns))]


def middle_kernel(
    scalar_ref, flag_ref, noise_ref, next_ref, after_ref, lat_ref, new_ref, mix_ref,
    lat_out, edge_out, patch_out,
):
    frames = [
        [None, None] + [ref[r] for r in range(4)] + [None, None]
        for ref in (noise_ref, next_ref, after_ref)
    ]
    mixed = convolved(frames, mix_ref)
    last = flag_ref[0] == 1
    drop = lat_ref[4, 0:1, :]
    rows = []
    for r in range(4):
        moved = lat_ref[r] + drop * (next_ref[r] + mixed[r + 1])
        rows.append(jnp.where(last, new_ref[r], moved))
        lat_out[r] = rows[r]
    above = jnp.where(last, 0.0, drop * mixed[0])
    below = jnp.where(last, 0.0, drop * mixed[5])
    edge_out[0] = above
    edge_out[1] = below
    patches = patch_rows((jnp.stack(rows) * scalar_ref[0]).astype(BF16))
    above = (above * scalar_ref[0]).astype(BF16)
    below = (below * scalar_ref[0]).astype(BF16)
    edges = [
        nn(above, spread_matrix((LANES, TOK), 1, 0, b, BF16))
        + nn(below, spread_matrix((LANES, TOK), 1, 1, b, BF16))
        for b in range(2)
    ]
    patches = jnp.concatenate([patches, jnp.concatenate(edges, axis=0).astype(BF16)], axis=0)
    for t in range(TILE):
        patch_out[t] = patches


def final_kernel(
    scalar_ref, before_ref, noise_ref, next_ref, up_ref, down_ref, lat_ref, mix_ref, out_ref
):
    frames = [
        [up_ref[td]] + [ref[r] for r in range(4)] + [down_ref[td]]
        for td, ref in enumerate((before_ref, noise_ref, next_ref))
    ]
    mixed = convolved(frames, mix_ref)
    for r in range(4):
        latent = lat_ref[r]
        if r == 0:
            latent = latent + up_ref[3]
        if r == 3:
            latent = latent + down_ref[3]
        out_ref[r] = latent + scalar_ref[0] * (noise_ref[r] + mixed[r])


def spread_kernel(x_ref, pick_ref, emb_ref, mod_ref, order_ref, patch_ref, pay_ref, out_t_ref):
    out_t_ref[...] = nt(order_ref[...], x_ref[:, 256:384]).astype(BF16)
    cols = x_ref[:, 128:256]
    halves = []
    for h in range(2):
        found = jnp.concatenate(
            [nn(pick_ref[h], cols), nn(emb_ref[h], cols), jnp.zeros((48, LANES), F32)], axis=0
        )
        turned = pltpu.roll(found, 40, 1).T[0:40]
        mod = mod_ref[40 * h : 40 * h + 40]
        lane = lane_of((40, LANES))
        valid = lax.broadcasted_iota(jnp.int32, (40, LANES), 0) < ROWS
        block = jnp.where(lane < PF, turned, jnp.where(lane == 76, 1.0, 0.0))
        for step in range(STEPS):
            hidden = turned[:, PF + step : PF + step + 1]
            condition = hidden / (1.0 + jnp.exp(-hidden))
            for j, kind in enumerate((1, 0, 2)):
                value = condition * mod[:, kind : kind + 1] + mod[:, 3 + kind : 4 + kind]
                if kind == 1:
                    value = value + 1.0
                upper = value.astype(BF16).astype(F32)
                block = jnp.where(lane == PF + 3 * step + j, upper, block)
                block = jnp.where(lane == PF + 6 + 3 * step + j, value - upper, block)
        halves.append(jnp.where(valid, block, 0.0))
    pay = jnp.concatenate(halves, axis=0).astype(BF16)
    pay = jnp.concatenate([patch_ref[...], pay], axis=0)
    for t in range(TILE):
        pay_ref[t] = pay


def fold_kernel(step, feat_ref, x_ref, out_ref, *gram_refs):
    lane = lane_of((WIDE, LANES))
    feat = jnp.concatenate([feat_ref[t, PF:].astype(F32) for t in range(TILE)], axis=0)
    mods = feat + pltpu.roll(feat, LANES - 6, 1)
    wide = jnp.where(lane < PF, feat, 0.0)
    mean = jnp.sum(wide, axis=0, keepdims=True) * (1.0 / D)
    centred = (wide - mean) * feat[:, 76:77]
    for gram_ref in gram_refs:
        upper = centred.astype(BF16)
        lower = (centred - upper.astype(F32)).astype(BF16)
        gram = tn(upper, upper) + tn(upper, lower) + tn(lower, upper)
        gram = gram[0:PF, 0:PF]
        upper = gram.astype(BF16)
        gram_ref[0:PF] = upper
        gram_ref[PF : 2 * PF] = (gram - upper.astype(F32)).astype(BF16)
    at = PF + 3 * step
    lines = jnp.where(
        lane < PF,
        centred * mods[:, at : at + 1],
        jnp.where(lane == PF, mods[:, at + 1 : at + 2], 0.0),
    )
    upper = lines.astype(BF16)
    lower = (lines - upper.astype(F32)).astype(BF16)
    weights = x_ref[:, 0:256]
    folded = tn(weights, upper) + tn(weights, lower)
    unit = [folded[HEAD * j : HEAD * j + HEAD] for j in range(3)]
    spot = lane_of((HEAD, LANES))
    top = jnp.where(spot < PF, unit[0], pltpu.roll(unit[1], PF, 1))
    low = jnp.where(spot < PF, unit[2], 0.0)
    low = jnp.where(spot == PF, unit[0], low)
    low = jnp.where(spot == PF + 1, pltpu.roll(unit[1], 1, 1), low)
    low = jnp.where(spot == PF + 2, pltpu.roll(unit[2], 2, 1), low)
    packed = jnp.concatenate([top, low], axis=0).astype(BF16)
    for t in range(TILE):
        out_ref[t] = packed


def heads_kernel(folded_ref, widen_ref, n_ref, mvt_ref, units):
    spot = lane_of((HEAD, LANES))
    for t in range(TILE):
        both = folded_ref[t].astype(F32)
        top, low = both[0:HEAD], both[HEAD : 2 * HEAD]
        parts = (
            (top, low),
            (pltpu.roll(top, PF, 1), pltpu.roll(low, LANES - 1, 1)),
            (low, pltpu.roll(low, LANES - 2, 1)),
        )
        for j, (main, bias) in enumerate(parts):
            unit = jnp.where(spot < PF, main, jnp.where(spot == PF, bias, 0.0))
            units[3 * t + j] = unit
    fold_scale = math.log2(math.e) / math.sqrt(HEAD)
    for h in range(HEADS):
        q, k, v = (units[HEADS * kind + h].astype(BF16) for kind in range(3))
        n_ref[h] = (tn(q, k) * fold_scale).astype(BF16)
        mvt_ref[h] = nn(widen_ref[...], v).astype(BF16)


def with_edges(pt_ref, j):
    patches = pt_ref[j].astype(F32)[0:PF]
    lane = lane_of((2 * C, LANES))
    blank = jnp.zeros((2 * C, LANES), F32)
    first, last = blank, blank
    if j > 0:
        edge = pltpu.roll(pt_ref[j - 1].astype(F32)[PF : PF + 2 * C], PF, 1)
        first = jnp.where(lane < PF, edge, 0.0)
    if j < TILE - 1:
        edge = pltpu.roll(pt_ref[j + 1].astype(F32)[PF : PF + 2 * C], PF, 1)
        last = jnp.where(lane >= PF, edge, 0.0)
    added = jnp.concatenate([first[0:C], last[0:C], first[C:], last[C:]], axis=0)
    return (patches + added).astype(BF16)


def attend_kernel(
    edges, spot_ref, pt_ref, gram_ref, n_ref, mvt_ref, att_ref, own_ref, keys_t, keys, held
):
    me = spot_ref[0]
    row = lax.broadcasted_iota(jnp.int32, (PF, TOK), 0)
    ones = jnp.where(row == 0, 1.0, 0.0).astype(F32)
    blocks = []
    for j in range(TILE):
        rounded = with_edges(pt_ref, j) if edges else pt_ref[j, 0:PF]
        held[j] = rounded
        blocks.append(rounded)
    patches = jnp.concatenate(blocks, axis=1)
    product = nn(gram_ref[...], patches)
    patches = patches.astype(F32)
    product = patches * (product[0:PF] + product[PF : 2 * PF])
    spread = jnp.maximum(jnp.sum(product, axis=0, keepdims=True), 0.0)
    unit = patches * lax.rsqrt(spread * (1.0 / D) + NORM_EPS)
    for j in range(TILE):
        wide = jnp.concatenate([unit[:, j * TOK : (j + 1) * TOK], ones], axis=0)
        keys_t[:, j * TOK : (j + 1) * TOK] = wide.astype(BF16)
        keys[j * TOK : (j + 1) * TOK, :] = wide.T.astype(BF16)
    own_ref[...] = held[me]

    def two_heads(pair):
        own = keys[pl.ds(pl.multiple_of(me * TOK, TOK), TOK), :]
        queries = jnp.concatenate(
            [nn(own, n_ref[2 * pair]), nn(own, n_ref[2 * pair + 1])], axis=0
        ).astype(BF16)
        scores = nn(queries, keys_t[...])
        highest = jnp.max(scores, axis=1, keepdims=True)
        weights = jnp.exp2(scores - highest).astype(BF16)
        summed = nn(weights, keys[...])
        mean = (summed / summed[:, PF : PF + 1]).astype(BF16)
        for k in range(2):
            head = 2 * pair + k
            value = nt(mvt_ref[head], mean[k * TOK : (k + 1) * TOK])
            att_ref[pl.ds(pl.multiple_of(head * 80, 80), 80), :] = value.astype(BF16)

    @pl.loop(0, HEADS // 8)
    def _(i):
        for k in range(4):
            two_heads(4 * i + k)


def output_kernel(
    step, spot_ref, att_ref, own_ref, feat_ref, wot_ref, out_ref, stream_ref
):
    me = spot_ref[0]
    delta = nn(wot_ref[...], att_ref[...])
    for b in range(TILE):
        tile = ((me ^ (8 * (b % 2))) & 8) + b // 2
        rows = pl.ds(pl.multiple_of(tile * 80, 80), 80)
        stream_ref[rows, :] = delta[80 * b : 80 * b + 80]
    feat = jnp.concatenate([feat_ref[t, PF:] for t in range(TILE)], axis=0)
    own = jnp.concatenate([own_ref[...], jnp.zeros((PF, TOK), BF16)], axis=0)
    at = PF + 3 * step + 2
    gate = feat[:, at : at + 1].astype(F32) + feat[:, at + 6 : at + 7].astype(F32)
    valid = feat[:, 76:77].astype(F32)
    stream = (nn(feat, own) + gate * stream_ref[...]) * valid
    mean = jnp.sum(stream, axis=0, keepdims=True) * (1.0 / D)
    center = (stream - mean) * valid
    spread = jnp.sum(center * center, axis=0, keepdims=True) * (1.0 / D)
    final = (center * lax.rsqrt(spread + NORM_EPS)).astype(BF16)
    out_rows = [wot_ref[80 * b + 32 : 80 * b + 48, :] for b in range(TILE)]
    noise = nn(jnp.concatenate(out_rows, axis=0), final)
    feature = lax.broadcasted_iota(jnp.int32, (PF, 256), 0)
    source = lane_of((PF, 256))
    block = source >> 4
    tile = ((me ^ ((block & 1) << 3)) & 8) + (block >> 1)
    q = (source & 15) - 4
    wanted = ((q & 1) << 5) + ((q >> 1) << 4) + tile
    order = jnp.where((q >= 0) & (q < 4) & (feature == wanted), 1.0, 0.0).astype(F32)
    noise = nn(order, noise, HIGHEST)
    for hp in range(2):
        rows = None
        for b in range(2):
            term = nn(
                noise[b * 32 : (b + 1) * 32], spread_matrix((TOK, LANES), 0, hp, b, F32), HIGHEST
            )
            rows = term if rows is None else rows + term
        out_ref[2 * hp] = rows[0:C]
        out_ref[2 * hp + 1] = rows[C : 2 * C]


VMEM = pl.BlockSpec(memory_space=pltpu.VMEM)
SMEM = pl.BlockSpec(memory_space=pltpu.SMEM)
BLOCK = pl.BlockSpec()


def spread(x, emb, mod, patches):
    return pl.pallas_call(
        spread_kernel,
        out_shape=(
            jax.ShapeDtypeStruct((TILE, PF + 80, LANES), BF16),
            jax.ShapeDtypeStruct((80, WIDE), BF16),
        ),
        in_specs=[VMEM] * 6,
        out_specs=(VMEM, VMEM),
        compiler_params=pltpu.CompilerParams(vmem_limit_bytes=32 * 1024 * 1024),
        name="spread",
    )(x, jnp.asarray(PICK, BF16), emb, mod, jnp.asarray(ORDER, BF16), patches)


def fold(step, feat, x):
    shapes = [jax.ShapeDtypeStruct((TILE, 2 * HEAD, LANES), BF16)]
    if step == 0:
        shapes.append(jax.ShapeDtypeStruct((2 * PF, PF), BF16))
    return pl.pallas_call(
        functools.partial(fold_kernel, step),
        out_shape=tuple(shapes),
        in_specs=[VMEM] * 2,
        out_specs=(VMEM,) * len(shapes),
        compiler_params=pltpu.CompilerParams(vmem_limit_bytes=32 * 1024 * 1024),
        cost_estimate=pl.CostEstimate(
            flops=4 * WIDE * 256 * LANES, bytes_accessed=8 * WIDE * LANES, transcendentals=0
        ),
        name="fold",
    )(feat, x)


def heads(folded):
    return pl.pallas_call(
        heads_kernel,
        out_shape=(
            jax.ShapeDtypeStruct((HEADS, LANES, LANES), BF16),
            jax.ShapeDtypeStruct((HEADS, 80, LANES), BF16),
        ),
        in_specs=[VMEM] * 2,
        out_specs=(VMEM,) * 2,
        scratch_shapes=[pltpu.VMEM((3 * HEADS, HEAD, LANES), F32)],
        compiler_params=pltpu.CompilerParams(vmem_limit_bytes=32 * 1024 * 1024),
        name="heads",
    )(folded, jnp.asarray(ORDER[:, 0:HEAD], BF16))


def attend(edges, spot, pt, gram, n, mvt):
    return pl.pallas_call(
        functools.partial(attend_kernel, edges),
        out_shape=(
            jax.ShapeDtypeStruct((WIDE, TOK), BF16),
            jax.ShapeDtypeStruct((PF, TOK), BF16),
        ),
        in_specs=[SMEM] + [BLOCK] * 4,
        out_specs=(VMEM, VMEM),
        scratch_shapes=[
            pltpu.VMEM((LANES, SPAN), BF16),
            pltpu.VMEM((SPAN, LANES), BF16),
            pltpu.VMEM((TILE, PF, TOK), BF16),
        ],
        compiler_params=pltpu.CompilerParams(vmem_limit_bytes=40 * 1024 * 1024),
        cost_estimate=pl.CostEstimate(
            flops=4 * 2 * SPAN * SPAN * LANES,
            bytes_accessed=8 * SPAN * LANES,
            transcendentals=SPAN * SPAN,
        ),
        name="attend",
    )(spot, pt, gram, n, mvt)


def output(step, spot, att, own, feat, wot):
    return pl.pallas_call(
        functools.partial(output_kernel, step),
        out_shape=jax.ShapeDtypeStruct((4, C, LANES), F32),
        in_specs=[SMEM] + [VMEM] * 4,
        out_specs=VMEM,
        scratch_shapes=[pltpu.VMEM((WIDE, TOK), F32)],
        compiler_params=pltpu.CompilerParams(vmem_limit_bytes=32 * 1024 * 1024),
        name="output",
    )(spot, att, own, feat, wot)


def prep(scale_in, latent):
    return pl.pallas_call(
        prep_kernel,
        out_shape=jax.ShapeDtypeStruct((PF, TOK), BF16),
        in_specs=[SMEM, VMEM],
        out_specs=VMEM,
        name="prep",
    )(scale_in, latent)


def middle(scale_in, last, noise, following, after, lat, new, mix):
    return pl.pallas_call(
        middle_kernel,
        out_shape=(
            jax.ShapeDtypeStruct((4, C, LANES), F32),
            jax.ShapeDtypeStruct((2, C, LANES), F32),
            jax.ShapeDtypeStruct((TILE, PF + 2 * C, TOK), BF16),
        ),
        in_specs=[SMEM, SMEM] + [BLOCK] * 6,
        out_specs=(VMEM,) * 3,
        compiler_params=pltpu.CompilerParams(vmem_limit_bytes=32 * 1024 * 1024),
        name="middle",
    )(scale_in, last, noise, following, after, lat, new, mix)


def finish(drop, before, noise, following, up, down, lat, mix):
    return pl.pallas_call(
        final_kernel,
        out_shape=jax.ShapeDtypeStruct((4, C, LANES), F32),
        in_specs=[SMEM] + [BLOCK] * 7,
        out_specs=VMEM,
        compiler_params=pltpu.CompilerParams(vmem_limit_bytes=32 * 1024 * 1024),
        name="finish",
    )(drop, before, noise, following, up, down, lat, mix)


def pick_matrix():
    pick = np.zeros((2, 2, 2, C, TM, 20, 2), np.float32)
    for h in range(2):
        for b in range(2):
            for a in range(2):
                for c in range(C):
                    pick[h, b, a, c, 2 * c + a, 16 + b, h] = 1.0
    return pick.reshape(2, PF, WIDE)


def order_matrix():
    order = np.zeros((80, LANES), np.float32)
    for j in range(ROWS):
        order[j, j] = 1.0
        order[40 + j, ROWS + j] = 1.0
    for j in range(4):
        order[ROWS + j, HEAD + j] = 1.0
    return order


PICK = pick_matrix()
ORDER = order_matrix()


def packed_weights(w_in, w_qkv, w_o, w_out, w_time, w_pos):
    small = jnp.concatenate([w_time, w_pos, w_in], axis=0).reshape(ROWS, ROWS)
    gap = jnp.zeros((ROWS, 4), BF16)
    tail = jnp.zeros((ROWS, 52), BF16)
    packed = jnp.concatenate([w_qkv, small, gap, w_o, w_out, tail], axis=1)
    return jnp.pad(packed, ((0, 4), (0, 0)))


def embeddings(level, position):
    level_emb = sinusoid(level.astype(F32)).reshape(STEPS, TM, 8)
    position_emb = sinusoid(position.astype(F32)).reshape(STEPS, TM, 8)
    rest = jnp.zeros((STEPS, TM, 4), F32)
    emb = jnp.concatenate([level_emb, position_emb, rest], axis=2).astype(BF16)
    half = jnp.eye(2, dtype=BF16)[:, None, None, None, :]
    emb = (emb[None, :, :, :, None] * half).reshape(2, STEPS, WIDE)
    return jnp.pad(emb, ((0, 0), (0, 14), (0, 0)))


def own_mods(mod_gain, mod_bias, tile):
    mods = jnp.concatenate([mod_gain, mod_bias, jnp.zeros((2, D), F32)], axis=0)
    mods = lax.dynamic_slice_in_dim(mods.reshape(8, TILE, HEAD), tile, 1, axis=1)
    return jnp.pad(mods.reshape(8, 2, ROWS), ((0, 0), (0, 0), (0, 4))).reshape(8, 80).T


def per_device(
    latents, new_frames, levels, offset, w_in, w_qkv, w_o, w_out, w_time, w_pos,
    mod_gain, mod_bias, refiner,
):
    frame = lax.axis_index(TM_AXES)
    tile = lax.axis_index(TILE_AXES)
    spot = tile.astype(jnp.int32)[None]
    mix = refiner.reshape(C, 27 * C)
    latent = latents[0]
    level = levels[:, 0]
    sigma_now = sigma_of(level)
    drop = sigma_of(level - 1) - sigma_now
    scale_in = lax.rsqrt(1.0 + sigma_now * sigma_now)

    packed = packed_weights(w_in, w_qkv, w_o, w_out, w_time, w_pos)
    rows = exchanged(jnp.broadcast_to(packed[None], (TM,) + packed.shape), TM_AXES)
    rows = rows.reshape(WIDE, 384)

    own = prep(scale_in[0:1], latent)
    marked = jnp.concatenate([latent, jnp.full((1, C, LANES), drop[0], F32)], axis=0)
    marked = shifted(marked, TM_AXES, -1)
    steps = jnp.arange(STEPS, dtype=jnp.int32)
    emb = embeddings(level, offset + frame + steps)
    mods = own_mods(mod_gain, mod_bias, tile)
    rows, marked, mix = lax.optimization_barrier((rows, marked, mix))

    pay, out_t = spread(rows, emb, mods, own)
    feat = exchanged(pay, TILE_AXES)

    first, gram = fold(0, feat, rows)
    first, feat, rows = lax.optimization_barrier((first, feat, rows))
    first = exchanged(first, TILE_AXES)

    (second,) = fold(1, feat, rows)
    first, second = lax.optimization_barrier((first, second))
    n, mvt = heads(first)
    second = exchanged(second, TILE_AXES)

    both = jnp.stack([out_t, swapped(out_t, "zh")])
    full_o = lax.all_gather(both, ("x", "core")).reshape(WIDE, WIDE)

    att, own = attend(False, spot, feat, gram, n, mvt)
    att, second = lax.optimization_barrier((att, second))
    noise = output(0, spot, att, own, feat, full_o)

    following, after = shifted(noise, TM_AXES, -1), shifted(noise, TM_AXES, -2)
    last = (frame == TM - 1).astype(jnp.int32)[None]
    latent, edges, patches = middle(
        scale_in[1:2], last, noise, following, after, marked, new_frames[0], mix
    )
    patches = exchanged(patches, TILE_AXES)
    n, mvt = heads(second)

    att, own = attend(True, spot, patches, gram, n, mvt)
    noise = output(1, spot, att, own, feat, full_o)
    frames = [shifted(noise, TM_AXES, 1), noise, shifted(noise, TM_AXES, -1)]
    up = jnp.stack([x[3] for x in frames] + [edges[1]])
    down = jnp.stack([x[0] for x in frames] + [edges[0]])
    up, down = shifted(up, TILE_AXES, 1), shifted(down, TILE_AXES, -1)
    return finish(drop[1:2], *frames, up, down, latent, mix)[None]


def solution(mesh):
    mesh = jax.sharding.Mesh(mesh.devices.reshape(SPLIT), AXES)
    rows, cols = TM_AXES, TILE_AXES
    in_specs = (
        P(rows, cols, None, None),
        P(None, cols, None, None),
        P(None, rows),
        P(),
        P(rows, cols),
        P(rows, cols),
        P(rows, cols),
        P(rows, cols),
        P(rows, cols),
        P(rows, cols),
        P(),
        P(),
        P(),
    )
    out_specs = P(rows, cols, None, None)
    return jax.shard_map(
        per_device, mesh=mesh, in_specs=in_specs, out_specs=out_specs, check_vma=False
    )
```

```python
import functools
import math

import jax
import jax.numpy as jnp
import numpy as np
from jax import lax
from jax.experimental import pallas as pl
from jax.experimental.pallas import tpu as pltpu
from jax.sharding import PartitionSpec as P

D = 1152
HEADS = 16
HEAD = 72
C = 16
PF = 64
FREQ = 256
STEPS = 2
LEVELS = 64
TM = 32
TILE = 16
ROWS = 36
TOK = 128
LANES = 128
SPAN = TILE * TOK
WIDE = 32 * 40

SIGMA_LOW = 0.02
SIGMA_RATIO = 1000.0
NORM_EPS = 1e-06

AXES = ("zl", "y", "zh", "x", "core")
SPLIT = (4, 8, 2, 4, 2)
TM_AXES = AXES[:2]
TILE_AXES = AXES[2:]

F32 = jnp.float32
BF16 = jnp.bfloat16
HIGHEST = lax.Precision.HIGHEST


def shifted(block, axis, distance):
    devices = range(lax.axis_size(axis))
    route = [(i - distance, i) for i in devices if i - distance in devices]
    return lax.ppermute(block, axis, route)


def exchanged(copies, axis):
    return lax.all_to_all(copies, axis, split_axis=0, concat_axis=0, tiled=True)


def sigma_of(level_ids):
    scaled_level = level_ids.astype(F32) / LEVELS
    return jnp.where(
        level_ids > 0, SIGMA_LOW * jnp.exp(math.log(SIGMA_RATIO) * scaled_level), F32(0.0)
    )


def sinusoid(values):
    half_freq = FREQ // 2
    frequency = jnp.exp(-math.log(10000.0) * jnp.arange(half_freq, dtype=F32) / half_freq)
    angles = values[:, None] * frequency[None, :]
    return jnp.concatenate([jnp.cos(angles), jnp.sin(angles)], axis=1)


def nn(a, b, precision=None):
    return lax.dot_general(
        a, b, (((1,), (0,)), ((), ())), preferred_element_type=F32, precision=precision
    )


def nt(a, b):
    return lax.dot_general(a, b, (((1,), (1,)), ((), ())), preferred_element_type=F32)


def tn(a, b):
    return lax.dot_general(a, b, (((0,), (0,)), ((), ())), preferred_element_type=F32)


def lane_of(shape):
    return lax.broadcasted_iota(jnp.int32, shape, 1)


def spread_matrix(shape, token_dim, hp, b, dtype):
    token = lax.broadcasted_iota(jnp.int32, shape, token_dim)
    col = lax.broadcasted_iota(jnp.int32, shape, 1 - token_dim)
    hit = col + 128 * hp == 2 * token + b
    return jnp.where(hit, 1.0, 0.0).astype(dtype)


def patch_rows(scaled):
    halves = []
    for b in range(2):
        total = None
        for hp in range(2):
            rows = scaled[2 * hp : 2 * hp + 2].reshape(2 * C, LANES)
            term = nn(rows, spread_matrix((LANES, TOK), 1, hp, b, BF16))
            total = term if total is None else total + term
        halves.append(total)
    return jnp.concatenate(halves, axis=0).astype(BF16)


def prep_kernel(scalar_ref, lat_ref, out_ref):
    scaled = (lat_ref[...] * scalar_ref[0]).astype(BF16)
    out_ref[...] = patch_rows(scaled)


def columns_around(x):
    lane = lax.broadcasted_iota(jnp.int32, (C, LANES), 1)
    before = jnp.where(lane == 0, 0.0, pltpu.roll(x, 1, 1))
    after = jnp.where(lane == LANES - 1, 0.0, pltpu.roll(x, LANES - 1, 1))
    return jnp.concatenate([before, x, after], axis=0)


def convolved(frames, mix_ref):
    around = [[None if x is None else columns_around(x) for x in rows] for rows in frames]
    blank = jnp.zeros((3 * C, LANES), F32)
    columns = []
    for r in range(len(frames[0]) - 2):
        pieces = [
            blank if around[td][r + dr] is None else around[td][r + dr]
            for td in range(3)
            for dr in range(3)
        ]
        columns.append(jnp.concatenate(pieces, axis=0))
    mixed = nn(mix_ref[...], jnp.concatenate(columns, axis=1), HIGHEST)
    return [mixed[:, r * LANES : (r + 1) * LANES] for r in range(len(columns))]


def middle_kernel(
    scalar_ref, flag_ref, noise_ref, next_ref, after_ref, lat_ref, new_ref, mix_ref,
    lat_out, edge_out, patch_out,
):
    frames = [
        [None, None] + [ref[r] for r in range(4)] + [None, None]
        for ref in (noise_ref, next_ref, after_ref)
    ]
    mixed = convolved(frames, mix_ref)
    last = flag_ref[0] == 1
    drop = lat_ref[4, 0:1, :]
    rows = []
    for r in range(4):
        moved = lat_ref[r] + drop * (next_ref[r] + mixed[r + 1])
        rows.append(jnp.where(last, new_ref[r], moved))
        lat_out[r] = rows[r]
    above = jnp.where(last, 0.0, drop * mixed[0])
    below = jnp.where(last, 0.0, drop * mixed[5])
    edge_out[0] = above
    edge_out[1] = below
    patches = patch_rows((jnp.stack(rows) * scalar_ref[0]).astype(BF16))
    above = (above * scalar_ref[0]).astype(BF16)
    below = (below * scalar_ref[0]).astype(BF16)
    edges = [
        nn(above, spread_matrix((LANES, TOK), 1, 0, b, BF16))
        + nn(below, spread_matrix((LANES, TOK), 1, 1, b, BF16))
        for b in range(2)
    ]
    patches = jnp.concatenate([patches, jnp.concatenate(edges, axis=0).astype(BF16)], axis=0)
    for t in range(TILE):
        patch_out[t] = patches


def final_kernel(
    scalar_ref, before_ref, noise_ref, next_ref, up_ref, down_ref, lat_ref, mix_ref, out_ref
):
    frames = [
        [up_ref[td]] + [ref[r] for r in range(4)] + [down_ref[td]]
        for td, ref in enumerate((before_ref, noise_ref, next_ref))
    ]
    mixed = convolved(frames, mix_ref)
    for r in range(4):
        latent = lat_ref[r]
        if r == 0:
            latent = latent + up_ref[3]
        if r == 3:
            latent = latent + down_ref[3]
        out_ref[r] = latent + scalar_ref[0] * (noise_ref[r] + mixed[r])


def spread_kernel(x_ref, pick_ref, emb_ref, mod_ref, order_ref, patch_ref, pay_ref, out_t_ref):
    out_t_ref[...] = nt(order_ref[...], x_ref[:, 256:384]).astype(BF16)
    cols = x_ref[:, 128:256]
    halves = []
    for h in range(2):
        found = jnp.concatenate(
            [nn(pick_ref[h], cols), nn(emb_ref[h], cols), jnp.zeros((48, LANES), F32)], axis=0
        )
        turned = pltpu.roll(found, 40, 1).T[0:40]
        mod = mod_ref[40 * h : 40 * h + 40]
        lane = lane_of((40, LANES))
        valid = lax.broadcasted_iota(jnp.int32, (40, LANES), 0) < ROWS
        block = jnp.where(lane < PF, turned, jnp.where(lane == 76, 1.0, 0.0))
        for step in range(STEPS):
            hidden = turned[:, PF + step : PF + step + 1]
            condition = hidden / (1.0 + jnp.exp(-hidden))
            for j, kind in enumerate((1, 0, 2)):
                value = condition * mod[:, kind : kind + 1] + mod[:, 3 + kind : 4 + kind]
                if kind == 1:
                    value = value + 1.0
                upper = value.astype(BF16).astype(F32)
                block = jnp.where(lane == PF + 3 * step + j, upper, block)
                block = jnp.where(lane == PF + 6 + 3 * step + j, value - upper, block)
        halves.append(jnp.where(valid, block, 0.0))
    pay = jnp.concatenate(halves, axis=0).astype(BF16)
    pay = jnp.concatenate([patch_ref[...], pay], axis=0)
    for t in range(TILE):
        pay_ref[t] = pay


def fold_kernel(step, feat_ref, x_ref, out_ref, *gram_refs):
    lane = lane_of((WIDE, LANES))
    feat = jnp.concatenate([feat_ref[t, PF:].astype(F32) for t in range(TILE)], axis=0)
    mods = feat + pltpu.roll(feat, LANES - 6, 1)
    wide = jnp.where(lane < PF, feat, 0.0)
    mean = jnp.sum(wide, axis=0, keepdims=True) * (1.0 / D)
    centred = (wide - mean) * feat[:, 76:77]
    for gram_ref in gram_refs:
        upper = centred.astype(BF16)
        lower = (centred - upper.astype(F32)).astype(BF16)
        gram = tn(upper, upper) + tn(upper, lower) + tn(lower, upper)
        gram = gram[0:PF, 0:PF]
        upper = gram.astype(BF16)
        gram_ref[0:PF] = upper
        gram_ref[PF : 2 * PF] = (gram - upper.astype(F32)).astype(BF16)
    at = PF + 3 * step
    lines = jnp.where(
        lane < PF,
        centred * mods[:, at : at + 1],
        jnp.where(lane == PF, mods[:, at + 1 : at + 2], 0.0),
    )
    upper = lines.astype(BF16)
    lower = (lines - upper.astype(F32)).astype(BF16)
    weights = x_ref[:, 0:256]
    folded = tn(weights, upper) + tn(weights, lower)
    unit = [folded[HEAD * j : HEAD * j + HEAD] for j in range(3)]
    spot = lane_of((HEAD, LANES))
    top = jnp.where(spot < PF, unit[0], pltpu.roll(unit[1], PF, 1))
    low = jnp.where(spot < PF, unit[2], 0.0)
    low = jnp.where(spot == PF, unit[0], low)
    low = jnp.where(spot == PF + 1, pltpu.roll(unit[1], 1, 1), low)
    low = jnp.where(spot == PF + 2, pltpu.roll(unit[2], 2, 1), low)
    packed = jnp.concatenate([top, low], axis=0).astype(BF16)
    for t in range(TILE):
        out_ref[t] = packed


def heads_kernel(folded_ref, widen_ref, n_ref, mvt_ref, units):
    spot = lane_of((HEAD, LANES))
    for t in range(TILE):
        both = folded_ref[t].astype(F32)
        top, low = both[0:HEAD], both[HEAD : 2 * HEAD]
        parts = (
            (top, low),
            (pltpu.roll(top, PF, 1), pltpu.roll(low, LANES - 1, 1)),
            (low, pltpu.roll(low, LANES - 2, 1)),
        )
        for j, (main, bias) in enumerate(parts):
            unit = jnp.where(spot < PF, main, jnp.where(spot == PF, bias, 0.0))
            units[3 * t + j] = unit
    fold_scale = math.log2(math.e) / math.sqrt(HEAD)
    for h in range(HEADS):
        q, k, v = (units[HEADS * kind + h].astype(BF16) for kind in range(3))
        n_ref[h] = (tn(q, k) * fold_scale).astype(BF16)
        mvt_ref[h] = nn(widen_ref[...], v).astype(BF16)


def with_edges(pt_ref, j):
    patches = pt_ref[j].astype(F32)[0:PF]
    lane = lane_of((2 * C, LANES))
    blank = jnp.zeros((2 * C, LANES), F32)
    first, last = blank, blank
    if j > 0:
        edge = pltpu.roll(pt_ref[j - 1].astype(F32)[PF : PF + 2 * C], PF, 1)
        first = jnp.where(lane < PF, edge, 0.0)
    if j < TILE - 1:
        edge = pltpu.roll(pt_ref[j + 1].astype(F32)[PF : PF + 2 * C], PF, 1)
        last = jnp.where(lane >= PF, edge, 0.0)
    added = jnp.concatenate([first[0:C], last[0:C], first[C:], last[C:]], axis=0)
    return (patches + added).astype(BF16)


def attend_kernel(
    edges, spot_ref, pt_ref, gram_ref, n_ref, mvt_ref, att_ref, own_ref, keys_t, keys, held
):
    me = spot_ref[0]
    row = lax.broadcasted_iota(jnp.int32, (PF, TOK), 0)
    ones = jnp.where(row == 0, 1.0, 0.0).astype(F32)
    blocks = []
    for j in range(TILE):
        rounded = with_edges(pt_ref, j) if edges else pt_ref[j, 0:PF]
        held[j] = rounded
        blocks.append(rounded)
    patches = jnp.concatenate(blocks, axis=1)
    product = nn(gram_ref[...], patches)
    patches = patches.astype(F32)
    product = patches * (product[0:PF] + product[PF : 2 * PF])
    spread = jnp.maximum(jnp.sum(product, axis=0, keepdims=True), 0.0)
    unit = patches * lax.rsqrt(spread * (1.0 / D) + NORM_EPS)
    for j in range(TILE):
        wide = jnp.concatenate([unit[:, j * TOK : (j + 1) * TOK], ones], axis=0)
        keys_t[:, j * TOK : (j + 1) * TOK] = wide.astype(BF16)
        keys[j * TOK : (j + 1) * TOK, :] = wide.T.astype(BF16)
    own_ref[...] = held[me]

    def two_heads(pair):
        own = keys[pl.ds(pl.multiple_of(me * TOK, TOK), TOK), :]
        queries = jnp.concatenate(
            [nn(own, n_ref[2 * pair]), nn(own, n_ref[2 * pair + 1])], axis=0
        ).astype(BF16)
        scores = nn(queries, keys_t[...])
        highest = jnp.max(scores, axis=1, keepdims=True)
        weights = jnp.exp2(scores - highest).astype(BF16)
        summed = nn(weights, keys[...])
        mean = (summed / summed[:, PF : PF + 1]).astype(BF16)
        for k in range(2):
            head = 2 * pair + k
            value = nt(mvt_ref[head], mean[k * TOK : (k + 1) * TOK])
            att_ref[pl.ds(pl.multiple_of(head * 80, 80), 80), :] = value.astype(BF16)

    @pl.loop(0, HEADS // 8)
    def _(i):
        for k in range(4):
            two_heads(4 * i + k)


def output_kernel(
    step, att_ref, own_ref, feat_ref, wot_ref, out_ref
):
    delta = nn(wot_ref[...], att_ref[...])
    feat = jnp.concatenate([feat_ref[t, PF:] for t in range(TILE)], axis=0)
    own = jnp.concatenate([own_ref[...], jnp.zeros((PF, TOK), BF16)], axis=0)
    at = PF + 3 * step + 2
    gate = feat[:, at : at + 1].astype(F32) + feat[:, at + 6 : at + 7].astype(F32)
    valid = feat[:, 76:77].astype(F32)
    stream = (nn(feat, own) + gate * delta) * valid
    mean = jnp.sum(stream, axis=0, keepdims=True) * (1.0 / D)
    center = (stream - mean) * valid
    spread = jnp.sum(center * center, axis=0, keepdims=True) * (1.0 / D)
    final = (center * lax.rsqrt(spread + NORM_EPS)).astype(BF16)
    out_rows = [wot_ref[80 * b + 32 : 80 * b + 48, :] for b in range(TILE)]
    noise = nn(jnp.concatenate(out_rows, axis=0), final)
    feature = lax.broadcasted_iota(jnp.int32, (PF, 256), 0)
    source = lane_of((PF, 256))
    block = source >> 4
    q = (source & 15) - 4
    wanted = ((q & 1) << 5) + ((q >> 1) << 4) + block
    order = jnp.where((q >= 0) & (q < 4) & (feature == wanted), 1.0, 0.0).astype(F32)
    noise = nn(order, noise, HIGHEST)
    for hp in range(2):
        rows = None
        for b in range(2):
            term = nn(
                noise[b * 32 : (b + 1) * 32], spread_matrix((TOK, LANES), 0, hp, b, F32), HIGHEST
            )
            rows = term if rows is None else rows + term
        out_ref[2 * hp] = rows[0:C]
        out_ref[2 * hp + 1] = rows[C : 2 * C]


VMEM = pl.BlockSpec(memory_space=pltpu.VMEM)
SMEM = pl.BlockSpec(memory_space=pltpu.SMEM)
BLOCK = pl.BlockSpec()


def spread(x, emb, mod, patches):
    return pl.pallas_call(
        spread_kernel,
        out_shape=(
            jax.ShapeDtypeStruct((TILE, PF + 80, LANES), BF16),
            jax.ShapeDtypeStruct((80, WIDE), BF16),
        ),
        in_specs=[VMEM] * 6,
        out_specs=(VMEM, VMEM),
        compiler_params=pltpu.CompilerParams(vmem_limit_bytes=32 * 1024 * 1024),
        name="spread",
    )(x, jnp.asarray(PICK, BF16), emb, mod, jnp.asarray(ORDER, BF16), patches)


def fold(step, feat, x):
    shapes = [jax.ShapeDtypeStruct((TILE, 2 * HEAD, LANES), BF16)]
    if step == 0:
        shapes.append(jax.ShapeDtypeStruct((2 * PF, PF), BF16))
    return pl.pallas_call(
        functools.partial(fold_kernel, step),
        out_shape=tuple(shapes),
        in_specs=[VMEM] * 2,
        out_specs=(VMEM,) * len(shapes),
        compiler_params=pltpu.CompilerParams(vmem_limit_bytes=32 * 1024 * 1024),
        cost_estimate=pl.CostEstimate(
            flops=4 * WIDE * 256 * LANES, bytes_accessed=8 * WIDE * LANES, transcendentals=0
        ),
        name="fold",
    )(feat, x)


def heads(folded):
    return pl.pallas_call(
        heads_kernel,
        out_shape=(
            jax.ShapeDtypeStruct((HEADS, LANES, LANES), BF16),
            jax.ShapeDtypeStruct((HEADS, 80, LANES), BF16),
        ),
        in_specs=[VMEM] * 2,
        out_specs=(VMEM,) * 2,
        scratch_shapes=[pltpu.VMEM((3 * HEADS, HEAD, LANES), F32)],
        compiler_params=pltpu.CompilerParams(vmem_limit_bytes=32 * 1024 * 1024),
        name="heads",
    )(folded, jnp.asarray(ORDER[:, 0:HEAD], BF16))


def attend(edges, spot, pt, gram, n, mvt):
    return pl.pallas_call(
        functools.partial(attend_kernel, edges),
        out_shape=(
            jax.ShapeDtypeStruct((WIDE, TOK), BF16),
            jax.ShapeDtypeStruct((PF, TOK), BF16),
        ),
        in_specs=[SMEM] + [BLOCK] * 4,
        out_specs=(VMEM, VMEM),
        scratch_shapes=[
            pltpu.VMEM((LANES, SPAN), BF16),
            pltpu.VMEM((SPAN, LANES), BF16),
            pltpu.VMEM((TILE, PF, TOK), BF16),
        ],
        compiler_params=pltpu.CompilerParams(vmem_limit_bytes=40 * 1024 * 1024),
        cost_estimate=pl.CostEstimate(
            flops=4 * 2 * SPAN * SPAN * LANES,
            bytes_accessed=8 * SPAN * LANES,
            transcendentals=SPAN * SPAN,
        ),
        name="attend",
    )(spot, pt, gram, n, mvt)


def output(step, att, own, feat, wot):
    return pl.pallas_call(
        functools.partial(output_kernel, step),
        out_shape=jax.ShapeDtypeStruct((4, C, LANES), F32),
        in_specs=[VMEM] * 4,
        out_specs=VMEM,
        compiler_params=pltpu.CompilerParams(vmem_limit_bytes=32 * 1024 * 1024),
        name="output",
    )(att, own, feat, wot)


def prep(scale_in, latent):
    return pl.pallas_call(
        prep_kernel,
        out_shape=jax.ShapeDtypeStruct((PF, TOK), BF16),
        in_specs=[SMEM, VMEM],
        out_specs=VMEM,
        name="prep",
    )(scale_in, latent)


def middle(scale_in, last, noise, following, after, lat, new, mix):
    return pl.pallas_call(
        middle_kernel,
        out_shape=(
            jax.ShapeDtypeStruct((4, C, LANES), F32),
            jax.ShapeDtypeStruct((2, C, LANES), F32),
            jax.ShapeDtypeStruct((TILE, PF + 2 * C, TOK), BF16),
        ),
        in_specs=[SMEM, SMEM] + [BLOCK] * 6,
        out_specs=(VMEM,) * 3,
        compiler_params=pltpu.CompilerParams(vmem_limit_bytes=32 * 1024 * 1024),
        name="middle",
    )(scale_in, last, noise, following, after, lat, new, mix)


def finish(drop, before, noise, following, up, down, lat, mix):
    return pl.pallas_call(
        final_kernel,
        out_shape=jax.ShapeDtypeStruct((4, C, LANES), F32),
        in_specs=[SMEM] + [BLOCK] * 7,
        out_specs=VMEM,
        compiler_params=pltpu.CompilerParams(vmem_limit_bytes=32 * 1024 * 1024),
        name="finish",
    )(drop, before, noise, following, up, down, lat, mix)


def pick_matrix():
    pick = np.zeros((2, 2, 2, C, TM, 20, 2), np.float32)
    for h in range(2):
        for b in range(2):
            for a in range(2):
                for c in range(C):
                    pick[h, b, a, c, 2 * c + a, 16 + b, h] = 1.0
    return pick.reshape(2, PF, WIDE)


def order_matrix():
    order = np.zeros((80, LANES), np.float32)
    for j in range(ROWS):
        order[j, j] = 1.0
        order[40 + j, ROWS + j] = 1.0
    for j in range(4):
        order[ROWS + j, HEAD + j] = 1.0
    return order


PICK = pick_matrix()
ORDER = order_matrix()


def packed_weights(w_in, w_qkv, w_o, w_out, w_time, w_pos):
    small = jnp.concatenate([w_time, w_pos, w_in], axis=0).reshape(ROWS, ROWS)
    gap = jnp.zeros((ROWS, 4), BF16)
    tail = jnp.zeros((ROWS, 52), BF16)
    packed = jnp.concatenate([w_qkv, small, gap, w_o, w_out, tail], axis=1)
    return jnp.pad(packed, ((0, 4), (0, 0)))


def embeddings(level, position):
    level_emb = sinusoid(level.astype(F32)).reshape(STEPS, TM, 8)
    position_emb = sinusoid(position.astype(F32)).reshape(STEPS, TM, 8)
    rest = jnp.zeros((STEPS, TM, 4), F32)
    emb = jnp.concatenate([level_emb, position_emb, rest], axis=2).astype(BF16)
    half = jnp.eye(2, dtype=BF16)[:, None, None, None, :]
    emb = (emb[None, :, :, :, None] * half).reshape(2, STEPS, WIDE)
    return jnp.pad(emb, ((0, 0), (0, 14), (0, 0)))


def own_mods(mod_gain, mod_bias, tile):
    mods = jnp.concatenate([mod_gain, mod_bias, jnp.zeros((2, D), F32)], axis=0)
    mods = lax.dynamic_slice_in_dim(mods.reshape(8, TILE, HEAD), tile, 1, axis=1)
    return jnp.pad(mods.reshape(8, 2, ROWS), ((0, 0), (0, 0), (0, 4))).reshape(8, 80).T


def per_device(
    latents, new_frames, levels, offset, w_in, w_qkv, w_o, w_out, w_time, w_pos,
    mod_gain, mod_bias, refiner,
):
    frame = lax.axis_index(TM_AXES)
    tile = lax.axis_index(TILE_AXES)
    spot = tile.astype(jnp.int32)[None]
    mix = refiner.reshape(C, 27 * C)
    latent = latents[0]
    level = levels[:, 0]
    sigma_now = sigma_of(level)
    drop = sigma_of(level - 1) - sigma_now
    scale_in = lax.rsqrt(1.0 + sigma_now * sigma_now)

    packed = packed_weights(w_in, w_qkv, w_o, w_out, w_time, w_pos)
    rows = exchanged(jnp.broadcast_to(packed[None], (TM,) + packed.shape), TM_AXES)
    rows = rows.reshape(WIDE, 384)

    own = prep(scale_in[0:1], latent)
    marked = jnp.concatenate([latent, jnp.full((1, C, LANES), drop[0], F32)], axis=0)
    marked = shifted(marked, TM_AXES, -1)
    steps = jnp.arange(STEPS, dtype=jnp.int32)
    emb = embeddings(level, offset + frame + steps)
    mods = own_mods(mod_gain, mod_bias, tile)
    rows, marked, mix = lax.optimization_barrier((rows, marked, mix))

    pay, out_t = spread(rows, emb, mods, own)
    feat = exchanged(pay, TILE_AXES)

    first, gram = fold(0, feat, rows)
    first, feat, rows = lax.optimization_barrier((first, feat, rows))
    first = exchanged(first, TILE_AXES)

    (second,) = fold(1, feat, rows)
    first, second = lax.optimization_barrier((first, second))
    n, mvt = heads(first)
    second = exchanged(second, TILE_AXES)

    full_o = lax.all_gather(out_t, TILE_AXES, tiled=True)

    att, own = attend(False, spot, feat, gram, n, mvt)
    noise = output(0, att, own, feat, full_o)

    following, after = shifted(noise, TM_AXES, -1), shifted(noise, TM_AXES, -2)
    following, second = lax.optimization_barrier((following, second))
    last = (frame == TM - 1).astype(jnp.int32)[None]
    latent, edges, patches = middle(
        scale_in[1:2], last, noise, following, after, marked, new_frames[0], mix
    )
    patches = exchanged(patches, TILE_AXES)
    n, mvt = heads(second)

    att, own = attend(True, spot, patches, gram, n, mvt)
    noise = output(1, att, own, feat, full_o)
    frames = [shifted(noise, TM_AXES, 1), noise, shifted(noise, TM_AXES, -1)]
    up = jnp.stack([x[3] for x in frames] + [edges[1]])
    down = jnp.stack([x[0] for x in frames] + [edges[0]])
    up, down = shifted(up, TILE_AXES, 1), shifted(down, TILE_AXES, -1)
    return finish(drop[1:2], *frames, up, down, latent, mix)[None]


def solution(mesh):
    mesh = jax.sharding.Mesh(mesh.devices.reshape(SPLIT), AXES)
    rows, cols = TM_AXES, TILE_AXES
    in_specs = (
        P(rows, cols, None, None),
        P(None, cols, None, None),
        P(None, rows),
        P(),
        P(rows, cols),
        P(rows, cols),
        P(rows, cols),
        P(rows, cols),
        P(rows, cols),
        P(rows, cols),
        P(),
        P(),
        P(),
    )
    out_specs = P(rows, cols, None, None)
    return jax.shard_map(
        per_device, mesh=mesh, in_specs=in_specs, out_specs=out_specs, check_vma=False
    )
```

```python
import functools
import math

import jax
import jax.numpy as jnp
import numpy as np
from jax import lax
from jax.experimental import pallas as pl
from jax.experimental.pallas import tpu as pltpu
from jax.sharding import PartitionSpec as P

D = 1152
HEADS = 16
HEAD = 72
C = 16
PF = 64
FREQ = 256
STEPS = 2
LEVELS = 64
TM = 32
TILE = 16
ROWS = 36
TOK = 128
LANES = 128
SPAN = TILE * TOK
WIDE = 32 * 40

SIGMA_LOW = 0.02
SIGMA_RATIO = 1000.0
NORM_EPS = 1e-06

AXES = ("zl", "y", "zh", "x", "core")
SPLIT = (4, 8, 2, 4, 2)
TM_AXES = AXES[:2]
TILE_AXES = AXES[2:]

F32 = jnp.float32
BF16 = jnp.bfloat16
HIGHEST = lax.Precision.HIGHEST


def swapped(block, axis):
    return lax.ppermute(block, axis, [(0, 1), (1, 0)])


def shifted(block, axis, distance):
    devices = range(lax.axis_size(axis))
    route = [(i - distance, i) for i in devices if i - distance in devices]
    return lax.ppermute(block, axis, route)


def exchanged(copies, axis):
    return lax.all_to_all(copies, axis, split_axis=0, concat_axis=0, tiled=True)


def sigma_of(level_ids):
    scaled_level = level_ids.astype(F32) / LEVELS
    return jnp.where(
        level_ids > 0, SIGMA_LOW * jnp.exp(math.log(SIGMA_RATIO) * scaled_level), F32(0.0)
    )


def sinusoid(values):
    half_freq = FREQ // 2
    frequency = jnp.exp(-math.log(10000.0) * jnp.arange(half_freq, dtype=F32) / half_freq)
    angles = values[:, None] * frequency[None, :]
    return jnp.concatenate([jnp.cos(angles), jnp.sin(angles)], axis=1)


def nn(a, b, precision=None):
    return lax.dot_general(
        a, b, (((1,), (0,)), ((), ())), preferred_element_type=F32, precision=precision
    )


def nt(a, b):
    return lax.dot_general(a, b, (((1,), (1,)), ((), ())), preferred_element_type=F32)


def tn(a, b):
    return lax.dot_general(a, b, (((0,), (0,)), ((), ())), preferred_element_type=F32)


def lane_of(shape):
    return lax.broadcasted_iota(jnp.int32, shape, 1)


def spread_matrix(shape, token_dim, hp, b, dtype):
    token = lax.broadcasted_iota(jnp.int32, shape, token_dim)
    col = lax.broadcasted_iota(jnp.int32, shape, 1 - token_dim)
    hit = col + 128 * hp == 2 * token + b
    return jnp.where(hit, 1.0, 0.0).astype(dtype)


def patch_rows(scaled):
    halves = []
    for b in range(2):
        total = None
        for hp in range(2):
            rows = scaled[2 * hp : 2 * hp + 2].reshape(2 * C, LANES)
            term = nn(rows, spread_matrix((LANES, TOK), 1, hp, b, BF16))
            total = term if total is None else total + term
        halves.append(total)
    return jnp.concatenate(halves, axis=0).astype(BF16)


def prep_kernel(scalar_ref, lat_ref, out_ref):
    scaled = (lat_ref[...] * scalar_ref[0]).astype(BF16)
    out_ref[...] = patch_rows(scaled)


def columns_around(x):
    lane = lax.broadcasted_iota(jnp.int32, (C, LANES), 1)
    before = jnp.where(lane == 0, 0.0, pltpu.roll(x, 1, 1))
    after = jnp.where(lane == LANES - 1, 0.0, pltpu.roll(x, LANES - 1, 1))
    return jnp.concatenate([before, x, after], axis=0)


def convolved(frames, mix_ref):
    around = [[None if x is None else columns_around(x) for x in rows] for rows in frames]
    blank = jnp.zeros((3 * C, LANES), F32)
    columns = []
    for r in range(len(frames[0]) - 2):
        pieces = [
            blank if around[td][r + dr] is None else around[td][r + dr]
            for td in range(3)
            for dr in range(3)
        ]
        columns.append(jnp.concatenate(pieces, axis=0))
    mixed = nn(mix_ref[...], jnp.concatenate(columns, axis=1), HIGHEST)
    return [mixed[:, r * LANES : (r + 1) * LANES] for r in range(len(columns))]


def middle_kernel(
    scalar_ref, flag_ref, noise_ref, next_ref, after_ref, lat_ref, new_ref, mix_ref,
    lat_out, edge_out, patch_out,
):
    frames = [
        [None, None] + [ref[r] for r in range(4)] + [None, None]
        for ref in (noise_ref, next_ref, after_ref)
    ]
    mixed = convolved(frames, mix_ref)
    last = flag_ref[0] == 1
    drop = lat_ref[4, 0:1, :]
    rows = []
    for r in range(4):
        moved = lat_ref[r] + drop * (next_ref[r] + mixed[r + 1])
        rows.append(jnp.where(last, new_ref[r], moved))
        lat_out[r] = rows[r]
    above = jnp.where(last, 0.0, drop * mixed[0])
    below = jnp.where(last, 0.0, drop * mixed[5])
    edge_out[0] = above
    edge_out[1] = below
    patches = patch_rows((jnp.stack(rows) * scalar_ref[0]).astype(BF16))
    above = (above * scalar_ref[0]).astype(BF16)
    below = (below * scalar_ref[0]).astype(BF16)
    edges = [
        nn(above, spread_matrix((LANES, TOK), 1, 0, b, BF16))
        + nn(below, spread_matrix((LANES, TOK), 1, 1, b, BF16))
        for b in range(2)
    ]
    patches = jnp.concatenate([patches, jnp.concatenate(edges, axis=0).astype(BF16)], axis=0)
    for t in range(TILE):
        patch_out[t] = patches


def final_kernel(
    scalar_ref, before_ref, noise_ref, next_ref, up_ref, down_ref, lat_ref, mix_ref, out_ref
):
    frames = [
        [up_ref[td]] + [ref[r] for r in range(4)] + [down_ref[td]]
        for td, ref in enumerate((before_ref, noise_ref, next_ref))
    ]
    mixed = convolved(frames, mix_ref)
    for r in range(4):
        latent = lat_ref[r]
        if r == 0:
            latent = latent + up_ref[3]
        if r == 3:
            latent = latent + down_ref[3]
        out_ref[r] = latent + scalar_ref[0] * (noise_ref[r] + mixed[r])


def pack_kernel(in_ref, qkv_ref, o_ref, last_ref, time_ref, pos_ref, out_ref, held):
    held[...] = jnp.zeros_like(held)
    held[0:ROWS, 0:216] = qkv_ref[...].astype(F32)
    held[0:ROWS, 256:328] = o_ref[...].astype(F32)
    held[0:ROWS, 328:332] = last_ref[...].astype(F32)
    at = 0
    for ref in (time_ref, pos_ref, in_ref):
        block = ref[...].astype(F32)
        for q in range(ref.shape[0]):
            for h in range(2):
                held[at : at + 1, 216:252] = block[q : q + 1, ROWS * h : ROWS * h + ROWS]
                at += 1
    packed = held[...].astype(BF16)
    for i in range(TM):
        out_ref[i] = packed


def spread_kernel(x_ref, pick_ref, emb_ref, mod_ref, order_ref, patch_ref, pay_ref, out_t_ref):
    out_t_ref[...] = nt(order_ref[...], x_ref[:, 256:384]).astype(BF16)
    cols = x_ref[:, 128:256]
    halves = []
    for h in range(2):
        found = jnp.concatenate(
            [nn(pick_ref[h], cols), nn(emb_ref[h], cols), jnp.zeros((48, LANES), F32)], axis=0
        )
        turned = pltpu.roll(found, 40, 1).T[0:40]
        mod = mod_ref[40 * h : 40 * h + 40]
        lane = lane_of((40, LANES))
        valid = lax.broadcasted_iota(jnp.int32, (40, LANES), 0) < ROWS
        block = jnp.where(lane < PF, turned, jnp.where(lane == 76, 1.0, 0.0))
        for step in range(STEPS):
            hidden = turned[:, PF + step : PF + step + 1]
            condition = hidden / (1.0 + jnp.exp(-hidden))
            for j, kind in enumerate((1, 0, 2)):
                value = condition * mod[:, kind : kind + 1] + mod[:, 3 + kind : 4 + kind]
                if kind == 1:
                    value = value + 1.0
                upper = value.astype(BF16).astype(F32)
                block = jnp.where(lane == PF + 3 * step + j, upper, block)
                block = jnp.where(lane == PF + 6 + 3 * step + j, value - upper, block)
        halves.append(jnp.where(valid, block, 0.0))
    pay = jnp.concatenate(halves, axis=0).astype(BF16)
    pay = jnp.concatenate([patch_ref[...], pay], axis=0)
    for t in range(TILE):
        pay_ref[t] = pay


def fold_kernel(step, feat_ref, x_ref, out_ref, *gram_refs):
    lane = lane_of((WIDE, LANES))
    feat = jnp.concatenate([feat_ref[t, PF:].astype(F32) for t in range(TILE)], axis=0)
    mods = feat + pltpu.roll(feat, LANES - 6, 1)
    wide = jnp.where(lane < PF, feat, 0.0)
    mean = jnp.sum(wide, axis=0, keepdims=True) * (1.0 / D)
    centred = (wide - mean) * feat[:, 76:77]
    for gram_ref in gram_refs:
        upper = centred.astype(BF16)
        lower = (centred - upper.astype(F32)).astype(BF16)
        gram = tn(upper, upper) + tn(upper, lower) + tn(lower, upper)
        gram = gram[0:PF, 0:PF]
        upper = gram.astype(BF16)
        gram_ref[0:PF] = upper
        gram_ref[PF : 2 * PF] = (gram - upper.astype(F32)).astype(BF16)
    at = PF + 3 * step
    lines = jnp.where(
        lane < PF,
        centred * mods[:, at : at + 1],
        jnp.where(lane == PF, mods[:, at + 1 : at + 2], 0.0),
    )
    upper = lines.astype(BF16)
    lower = (lines - upper.astype(F32)).astype(BF16)
    weights = x_ref[:, 0:256]
    folded = tn(weights, upper) + tn(weights, lower)
    unit = [folded[HEAD * j : HEAD * j + HEAD] for j in range(3)]
    spot = lane_of((HEAD, LANES))
    top = jnp.where(spot < PF, unit[0], pltpu.roll(unit[1], PF, 1))
    low = jnp.where(spot < PF, unit[2], 0.0)
    low = jnp.where(spot == PF, unit[0], low)
    low = jnp.where(spot == PF + 1, pltpu.roll(unit[1], 1, 1), low)
    low = jnp.where(spot == PF + 2, pltpu.roll(unit[2], 2, 1), low)
    packed = jnp.concatenate([top, low], axis=0).astype(BF16)
    for t in range(TILE):
        out_ref[t] = packed


def heads_kernel(folded_ref, widen_ref, n_ref, mvt_ref, units):
    spot = lane_of((HEAD, LANES))
    for t in range(TILE):
        both = folded_ref[t].astype(F32)
        top, low = both[0:HEAD], both[HEAD : 2 * HEAD]
        parts = (
            (top, low),
            (pltpu.roll(top, PF, 1), pltpu.roll(low, LANES - 1, 1)),
            (low, pltpu.roll(low, LANES - 2, 1)),
        )
        for j, (main, bias) in enumerate(parts):
            unit = jnp.where(spot < PF, main, jnp.where(spot == PF, bias, 0.0))
            units[3 * t + j] = unit
    fold_scale = math.log2(math.e) / math.sqrt(HEAD)
    for h in range(HEADS):
        q, k, v = (units[HEADS * kind + h].astype(BF16) for kind in range(3))
        n_ref[h] = (tn(q, k) * fold_scale).astype(BF16)
        mvt_ref[h] = nn(widen_ref[...], v).astype(BF16)


def with_edges(pt_ref, j):
    patches = pt_ref[j].astype(F32)[0:PF]
    lane = lane_of((2 * C, LANES))
    blank = jnp.zeros((2 * C, LANES), F32)
    first, last = blank, blank
    if j > 0:
        edge = pltpu.roll(pt_ref[j - 1].astype(F32)[PF : PF + 2 * C], PF, 1)
        first = jnp.where(lane < PF, edge, 0.0)
    if j < TILE - 1:
        edge = pltpu.roll(pt_ref[j + 1].astype(F32)[PF : PF + 2 * C], PF, 1)
        last = jnp.where(lane >= PF, edge, 0.0)
    added = jnp.concatenate([first[0:C], last[0:C], first[C:], last[C:]], axis=0)
    return (patches + added).astype(BF16)


def block_kernel(
    step, spot_ref, pt_ref, gram_ref, n_ref, mvt_ref, feat_ref, far_ref, out_ref,
    keys_t, keys, held, att_ref, wot_ref, stream_ref, fetched,
):
    fetch = pltpu.make_async_copy(far_ref, wot_ref, fetched)
    fetch.start()
    edges = step > 0
    me = spot_ref[0]
    row = lax.broadcasted_iota(jnp.int32, (PF, TOK), 0)
    ones = jnp.where(row == 0, 1.0, 0.0).astype(F32)
    blocks = []
    for j in range(TILE):
        rounded = with_edges(pt_ref, j) if edges else pt_ref[j, 0:PF]
        held[j] = rounded
        blocks.append(rounded)
    patches = jnp.concatenate(blocks, axis=1)
    product = nn(gram_ref[...], patches)
    patches = patches.astype(F32)
    product = patches * (product[0:PF] + product[PF : 2 * PF])
    spread = jnp.maximum(jnp.sum(product, axis=0, keepdims=True), 0.0)
    unit = patches * lax.rsqrt(spread * (1.0 / D) + NORM_EPS)
    for j in range(TILE):
        wide = jnp.concatenate([unit[:, j * TOK : (j + 1) * TOK], ones], axis=0)
        keys_t[:, j * TOK : (j + 1) * TOK] = wide.astype(BF16)
        keys[j * TOK : (j + 1) * TOK, :] = wide.T.astype(BF16)

    def two_heads(pair):
        own = keys[pl.ds(pl.multiple_of(me * TOK, TOK), TOK), :]
        queries = jnp.concatenate(
            [nn(own, n_ref[2 * pair]), nn(own, n_ref[2 * pair + 1])], axis=0
        ).astype(BF16)
        scores = nn(queries, keys_t[...])
        highest = jnp.max(scores, axis=1, keepdims=True)
        weights = jnp.exp2(scores - highest).astype(BF16)
        summed = nn(weights, keys[...])
        mean = (summed / summed[:, PF : PF + 1]).astype(BF16)
        for k in range(2):
            head = 2 * pair + k
            value = nt(mvt_ref[head], mean[k * TOK : (k + 1) * TOK])
            att_ref[pl.ds(pl.multiple_of(head * 80, 80), 80), :] = value.astype(BF16)

    @pl.loop(0, HEADS // 8)
    def _(i):
        for k in range(4):
            two_heads(4 * i + k)

    fetch.wait()
    delta = nn(wot_ref[...], att_ref[...])
    for b in range(TILE):
        tile = ((me ^ (8 * (b % 2))) & 8) + b // 2
        rows = pl.ds(pl.multiple_of(tile * 80, 80), 80)
        stream_ref[rows, :] = delta[80 * b : 80 * b + 80]
    feat = jnp.concatenate([feat_ref[t, PF:] for t in range(TILE)], axis=0)
    own = jnp.concatenate([held[me], jnp.zeros((PF, TOK), BF16)], axis=0)
    at = PF + 3 * step + 2
    gate = feat[:, at : at + 1].astype(F32) + feat[:, at + 6 : at + 7].astype(F32)
    valid = feat[:, 76:77].astype(F32)
    stream = (nn(feat, own) + gate * stream_ref[...]) * valid
    mean = jnp.sum(stream, axis=0, keepdims=True) * (1.0 / D)
    center = (stream - mean) * valid
    spread = jnp.sum(center * center, axis=0, keepdims=True) * (1.0 / D)
    final = (center * lax.rsqrt(spread + NORM_EPS)).astype(BF16)
    out_rows = [wot_ref[80 * b + 32 : 80 * b + 48, :] for b in range(TILE)]
    noise = nn(jnp.concatenate(out_rows, axis=0), final)
    feature = lax.broadcasted_iota(jnp.int32, (PF, 256), 0)
    source = lane_of((PF, 256))
    block = source >> 4
    tile = ((me ^ ((block & 1) << 3)) & 8) + (block >> 1)
    q = (source & 15) - 4
    wanted = ((q & 1) << 5) + ((q >> 1) << 4) + tile
    order = jnp.where((q >= 0) & (q < 4) & (feature == wanted), 1.0, 0.0).astype(F32)
    noise = nn(order, noise, HIGHEST)
    for hp in range(2):
        rows = None
        for b in range(2):
            term = nn(
                noise[b * 32 : (b + 1) * 32], spread_matrix((TOK, LANES), 0, hp, b, F32), HIGHEST
            )
            rows = term if rows is None else rows + term
        out_ref[2 * hp] = rows[0:C]
        out_ref[2 * hp + 1] = rows[C : 2 * C]


VMEM = pl.BlockSpec(memory_space=pltpu.VMEM)
SMEM = pl.BlockSpec(memory_space=pltpu.SMEM)
BLOCK = pl.BlockSpec()


def spread(x, emb, mod, patches):
    return pl.pallas_call(
        spread_kernel,
        out_shape=(
            jax.ShapeDtypeStruct((TILE, PF + 80, LANES), BF16),
            jax.ShapeDtypeStruct((80, WIDE), BF16),
        ),
        in_specs=[VMEM] * 6,
        out_specs=(VMEM, VMEM),
        compiler_params=pltpu.CompilerParams(vmem_limit_bytes=32 * 1024 * 1024),
        name="spread",
    )(x, jnp.asarray(PICK, BF16), emb, mod, jnp.asarray(ORDER, BF16), patches)


def fold(step, feat, x):
    shapes = [jax.ShapeDtypeStruct((TILE, 2 * HEAD, LANES), BF16)]
    if step == 0:
        shapes.append(jax.ShapeDtypeStruct((2 * PF, PF), BF16))
    return pl.pallas_call(
        functools.partial(fold_kernel, step),
        out_shape=tuple(shapes),
        in_specs=[VMEM] * 2,
        out_specs=(VMEM,) * len(shapes),
        compiler_params=pltpu.CompilerParams(vmem_limit_bytes=32 * 1024 * 1024),
        cost_estimate=pl.CostEstimate(
            flops=4 * WIDE * 256 * LANES, bytes_accessed=8 * WIDE * LANES, transcendentals=0
        ),
        name="fold",
    )(feat, x)


def heads(folded):
    return pl.pallas_call(
        heads_kernel,
        out_shape=(
            jax.ShapeDtypeStruct((HEADS, LANES, LANES), BF16),
            jax.ShapeDtypeStruct((HEADS, 80, LANES), BF16),
        ),
        in_specs=[VMEM] * 2,
        out_specs=(VMEM,) * 2,
        scratch_shapes=[pltpu.VMEM((3 * HEADS, HEAD, LANES), F32)],
        compiler_params=pltpu.CompilerParams(vmem_limit_bytes=32 * 1024 * 1024),
        name="heads",
    )(folded, jnp.asarray(ORDER[:, 0:HEAD], BF16))


def frame_block(step, spot, pt, gram, n, mvt, feat, wot):
    return pl.pallas_call(
        functools.partial(block_kernel, step),
        out_shape=jax.ShapeDtypeStruct((4, C, LANES), F32),
        in_specs=[SMEM] + [BLOCK] * 5 + [pl.BlockSpec(memory_space=pl.ANY)],
        out_specs=VMEM,
        scratch_shapes=[
            pltpu.VMEM((LANES, SPAN), BF16),
            pltpu.VMEM((SPAN, LANES), BF16),
            pltpu.VMEM((TILE, PF, TOK), BF16),
            pltpu.VMEM((WIDE, TOK), BF16),
            pltpu.VMEM((WIDE, WIDE), BF16),
            pltpu.VMEM((WIDE, TOK), F32),
            pltpu.SemaphoreType.DMA,
        ],
        compiler_params=pltpu.CompilerParams(vmem_limit_bytes=48 * 1024 * 1024),
        cost_estimate=pl.CostEstimate(
            flops=4 * 2 * SPAN * SPAN * LANES,
            bytes_accessed=8 * SPAN * LANES,
            transcendentals=SPAN * SPAN,
        ),
        name="frame_block",
    )(spot, pt, gram, n, mvt, feat, wot)


def prep(scale_in, latent):
    return pl.pallas_call(
        prep_kernel,
        out_shape=jax.ShapeDtypeStruct((PF, TOK), BF16),
        in_specs=[SMEM, VMEM],
        out_specs=VMEM,
        name="prep",
    )(scale_in, latent)


def middle(scale_in, last, noise, following, after, lat, new, mix):
    return pl.pallas_call(
        middle_kernel,
        out_shape=(
            jax.ShapeDtypeStruct((4, C, LANES), F32),
            jax.ShapeDtypeStruct((2, C, LANES), F32),
            jax.ShapeDtypeStruct((TILE, PF + 2 * C, TOK), BF16),
        ),
        in_specs=[SMEM, SMEM] + [BLOCK] * 6,
        out_specs=(VMEM,) * 3,
        compiler_params=pltpu.CompilerParams(vmem_limit_bytes=32 * 1024 * 1024),
        name="middle",
    )(scale_in, last, noise, following, after, lat, new, mix)


def finish(drop, before, noise, following, up, down, lat, mix):
    return pl.pallas_call(
        final_kernel,
        out_shape=jax.ShapeDtypeStruct((4, C, LANES), F32),
        in_specs=[SMEM] + [BLOCK] * 7,
        out_specs=VMEM,
        compiler_params=pltpu.CompilerParams(vmem_limit_bytes=32 * 1024 * 1024),
        name="finish",
    )(drop, before, noise, following, up, down, lat, mix)


def pick_matrix():
    pick = np.zeros((2, 2, 2, C, TM, 20, 2), np.float32)
    for h in range(2):
        for b in range(2):
            for a in range(2):
                for c in range(C):
                    pick[h, b, a, c, 2 * c + a, 16 + b, h] = 1.0
    return pick.reshape(2, PF, WIDE)


def order_matrix():
    order = np.zeros((80, LANES), np.float32)
    for j in range(ROWS):
        order[j, j] = 1.0
        order[40 + j, ROWS + j] = 1.0
    for j in range(4):
        order[ROWS + j, HEAD + j] = 1.0
    return order


PICK = pick_matrix()
ORDER = order_matrix()


def packed_weights(w_in, w_qkv, w_o, w_out, w_time, w_pos):
    return pl.pallas_call(
        pack_kernel,
        out_shape=jax.ShapeDtypeStruct((TM, 40, 384), BF16),
        in_specs=[BLOCK] * 6,
        out_specs=VMEM,
        scratch_shapes=[pltpu.VMEM((40, 384), F32)],
        name="pack",
    )(w_in, w_qkv, w_o, w_out, w_time, w_pos)


def embeddings(level, position):
    level_emb = sinusoid(level.astype(F32)).reshape(STEPS, TM, 8)
    position_emb = sinusoid(position.astype(F32)).reshape(STEPS, TM, 8)
    rest = jnp.zeros((STEPS, TM, 4), F32)
    emb = jnp.concatenate([level_emb, position_emb, rest], axis=2).astype(BF16)
    half = jnp.eye(2, dtype=BF16)[:, None, None, None, :]
    emb = (emb[None, :, :, :, None] * half).reshape(2, STEPS, WIDE)
    return jnp.pad(emb, ((0, 0), (0, 14), (0, 0)))


def own_mods(mod_gain, mod_bias, tile):
    mods = jnp.concatenate([mod_gain, mod_bias, jnp.zeros((2, D), F32)], axis=0)
    mods = lax.dynamic_slice_in_dim(mods.reshape(8, TILE, HEAD), tile, 1, axis=1)
    return jnp.pad(mods.reshape(8, 2, ROWS), ((0, 0), (0, 0), (0, 4))).reshape(8, 80).T


def per_device(
    latents, new_frames, levels, offset, w_in, w_qkv, w_o, w_out, w_time, w_pos,
    mod_gain, mod_bias, refiner,
):
    frame = lax.axis_index(TM_AXES)
    tile = lax.axis_index(TILE_AXES)
    spot = tile.astype(jnp.int32)[None]
    mix = refiner.reshape(C, 27 * C)
    latent = latents[0]
    level = levels[:, 0]
    sigma_now = sigma_of(level)
    drop = sigma_of(level - 1) - sigma_now
    scale_in = lax.rsqrt(1.0 + sigma_now * sigma_now)

    packed = packed_weights(w_in, w_qkv, w_o, w_out, w_time, w_pos)
    rows = exchanged(packed, TM_AXES)
    rows = rows.reshape(WIDE, 384)

    own = prep(scale_in[0:1], latent)
    marked = jnp.concatenate([latent, jnp.full((1, C, LANES), drop[0], F32)], axis=0)
    marked = shifted(marked, TM_AXES, -1)
    steps = jnp.arange(STEPS, dtype=jnp.int32)
    emb = embeddings(level, offset + frame + steps)
    mods = own_mods(mod_gain, mod_bias, tile)
    rows, marked, mix = lax.optimization_barrier((rows, marked, mix))

    pay, out_t = spread(rows, emb, mods, own)
    feat = exchanged(pay, TILE_AXES)

    first, gram = fold(0, feat, rows)
    first, feat, rows = lax.optimization_barrier((first, feat, rows))
    first = exchanged(first, TILE_AXES)

    (second,) = fold(1, feat, rows)
    first, second = lax.optimization_barrier((first, second))
    n, mvt = heads(first)
    second = exchanged(second, TILE_AXES)

    both = jnp.stack([out_t, swapped(out_t, "zh")])
    full_o = lax.all_gather(both, ("x", "core")).reshape(WIDE, WIDE)

    noise = frame_block(0, spot, feat, gram, n, mvt, feat, full_o)

    following, after = shifted(noise, TM_AXES, -1), shifted(noise, TM_AXES, -2)
    following, second = lax.optimization_barrier((following, second))
    last = (frame == TM - 1).astype(jnp.int32)[None]
    latent, edges, patches = middle(
        scale_in[1:2], last, noise, following, after, marked, new_frames[0], mix
    )
    patches = exchanged(patches, TILE_AXES)
    n, mvt = heads(second)

    noise = frame_block(1, spot, patches, gram, n, mvt, feat, full_o)
    frames = [shifted(noise, TM_AXES, 1), noise, shifted(noise, TM_AXES, -1)]
    up = jnp.stack([x[3] for x in frames] + [edges[1]])
    down = jnp.stack([x[0] for x in frames] + [edges[0]])
    up, down = shifted(up, TILE_AXES, 1), shifted(down, TILE_AXES, -1)
    return finish(drop[1:2], *frames, up, down, latent, mix)[None]


def solution(mesh):
    mesh = jax.sharding.Mesh(mesh.devices.reshape(SPLIT), AXES)
    rows, cols = TM_AXES, TILE_AXES
    in_specs = (
        P(rows, cols, None, None),
        P(None, cols, None, None),
        P(None, rows),
        P(),
        P(rows, cols),
        P(rows, cols),
        P(rows, cols),
        P(rows, cols),
        P(rows, cols),
        P(rows, cols),
        P(),
        P(),
        P(),
    )
    out_specs = P(rows, cols, None, None)
    return jax.shard_map(
        per_device, mesh=mesh, in_specs=in_specs, out_specs=out_specs, check_vma=False
    )
```

```python
import functools
import math

import jax
import jax.numpy as jnp
import numpy as np
from jax import lax
from jax.experimental import pallas as pl
from jax.experimental.pallas import tpu as pltpu
from jax.sharding import PartitionSpec as P

D = 1152
HEADS = 16
HEAD = 72
C = 16
PF = 64
FREQ = 256
STEPS = 2
LEVELS = 64
TM = 32
TILE = 16
ROWS = 36
TOK = 128
LANES = 128
SPAN = TILE * TOK
WIDE = 32 * 40

SIGMA_LOW = 0.02
SIGMA_RATIO = 1000.0
NORM_EPS = 1e-06

AXES = ("zl", "y", "zh", "x", "core")
SPLIT = (4, 8, 2, 4, 2)
TM_AXES = AXES[:2]
TILE_AXES = AXES[2:]

F32 = jnp.float32
BF16 = jnp.bfloat16
HIGHEST = lax.Precision.HIGHEST


def swapped(block, axis):
    return lax.ppermute(block, axis, [(0, 1), (1, 0)])


def shifted(block, axis, distance):
    devices = range(lax.axis_size(axis))
    route = [(i - distance, i) for i in devices if i - distance in devices]
    return lax.ppermute(block, axis, route)


def exchanged(copies, axis):
    return lax.all_to_all(copies, axis, split_axis=0, concat_axis=0, tiled=True)


def sigma_of(level_ids):
    scaled_level = level_ids.astype(F32) / LEVELS
    return jnp.where(
        level_ids > 0, SIGMA_LOW * jnp.exp(math.log(SIGMA_RATIO) * scaled_level), F32(0.0)
    )


def sinusoid(values):
    half_freq = FREQ // 2
    frequency = jnp.exp(-math.log(10000.0) * jnp.arange(half_freq, dtype=F32) / half_freq)
    angles = values[:, None] * frequency[None, :]
    return jnp.concatenate([jnp.cos(angles), jnp.sin(angles)], axis=1)


def nn(a, b, precision=None):
    return lax.dot_general(
        a, b, (((1,), (0,)), ((), ())), preferred_element_type=F32, precision=precision
    )


def nt(a, b):
    return lax.dot_general(a, b, (((1,), (1,)), ((), ())), preferred_element_type=F32)


def tn(a, b):
    return lax.dot_general(a, b, (((0,), (0,)), ((), ())), preferred_element_type=F32)


def lane_of(shape):
    return lax.broadcasted_iota(jnp.int32, shape, 1)


def spread_matrix(shape, token_dim, hp, b, dtype):
    token = lax.broadcasted_iota(jnp.int32, shape, token_dim)
    col = lax.broadcasted_iota(jnp.int32, shape, 1 - token_dim)
    hit = col + 128 * hp == 2 * token + b
    return jnp.where(hit, 1.0, 0.0).astype(dtype)


def patch_rows(scaled):
    halves = []
    for b in range(2):
        total = None
        for hp in range(2):
            rows = scaled[2 * hp : 2 * hp + 2].reshape(2 * C, LANES)
            term = nn(rows, spread_matrix((LANES, TOK), 1, hp, b, BF16))
            total = term if total is None else total + term
        halves.append(total)
    return jnp.concatenate(halves, axis=0).astype(BF16)


def prep_kernel(scalar_ref, lat_ref, out_ref):
    scaled = (lat_ref[...] * scalar_ref[0]).astype(BF16)
    out_ref[...] = patch_rows(scaled)


def columns_around(x):
    lane = lax.broadcasted_iota(jnp.int32, (C, LANES), 1)
    before = jnp.where(lane == 0, 0.0, pltpu.roll(x, 1, 1))
    after = jnp.where(lane == LANES - 1, 0.0, pltpu.roll(x, LANES - 1, 1))
    return jnp.concatenate([before, x, after], axis=0)


def convolved(frames, mix_ref):
    around = [[None if x is None else columns_around(x) for x in rows] for rows in frames]
    blank = jnp.zeros((3 * C, LANES), F32)
    columns = []
    for r in range(len(frames[0]) - 2):
        pieces = [
            blank if around[td][r + dr] is None else around[td][r + dr]
            for td in range(3)
            for dr in range(3)
        ]
        columns.append(jnp.concatenate(pieces, axis=0))
    mixed = nn(mix_ref[...], jnp.concatenate(columns, axis=1), HIGHEST)
    return [mixed[:, r * LANES : (r + 1) * LANES] for r in range(len(columns))]


def middle_kernel(
    scalar_ref, flag_ref, noise_ref, next_ref, after_ref, lat_ref, new_ref, mix_ref,
    lat_out, edge_out, patch_out,
):
    frames = [
        [None, None] + [ref[r] for r in range(4)] + [None, None]
        for ref in (noise_ref, next_ref, after_ref)
    ]
    mixed = convolved(frames, mix_ref)
    last = flag_ref[0] == 1
    drop = lat_ref[4, 0:1, :]
    rows = []
    for r in range(4):
        moved = lat_ref[r] + drop * (next_ref[r] + mixed[r + 1])
        rows.append(jnp.where(last, new_ref[r], moved))
        lat_out[r] = rows[r]
    above = jnp.where(last, 0.0, drop * mixed[0])
    below = jnp.where(last, 0.0, drop * mixed[5])
    edge_out[0] = above
    edge_out[1] = below
    patches = patch_rows((jnp.stack(rows) * scalar_ref[0]).astype(BF16))
    above = (above * scalar_ref[0]).astype(BF16)
    below = (below * scalar_ref[0]).astype(BF16)
    edges = [
        nn(above, spread_matrix((LANES, TOK), 1, 0, b, BF16))
        + nn(below, spread_matrix((LANES, TOK), 1, 1, b, BF16))
        for b in range(2)
    ]
    patches = jnp.concatenate([patches, jnp.concatenate(edges, axis=0).astype(BF16)], axis=0)
    for t in range(TILE):
        patch_out[t] = patches


def final_kernel(
    scalar_ref, before_ref, noise_ref, next_ref, up_ref, down_ref, lat_ref, mix_ref, out_ref
):
    frames = [
        [up_ref[td]] + [ref[r] for r in range(4)] + [down_ref[td]]
        for td, ref in enumerate((before_ref, noise_ref, next_ref))
    ]
    mixed = convolved(frames, mix_ref)
    for r in range(4):
        latent = lat_ref[r]
        if r == 0:
            latent = latent + up_ref[3]
        if r == 3:
            latent = latent + down_ref[3]
        out_ref[r] = latent + scalar_ref[0] * (noise_ref[r] + mixed[r])


def pack_kernel(in_ref, qkv_ref, o_ref, last_ref, time_ref, pos_ref, out_ref, held):
    held[...] = jnp.zeros_like(held)
    held[0:ROWS, 0:216] = qkv_ref[...].astype(F32)
    held[0:ROWS, 256:328] = o_ref[...].astype(F32)
    held[0:ROWS, 328:332] = last_ref[...].astype(F32)
    at = 0
    for ref in (time_ref, pos_ref, in_ref):
        block = ref[...].astype(F32)
        for q in range(ref.shape[0]):
            for h in range(2):
                held[at : at + 1, 216:252] = block[q : q + 1, ROWS * h : ROWS * h + ROWS]
                at += 1
    packed = held[...].astype(BF16)
    for i in range(TM):
        out_ref[i] = packed


def spread_kernel(x_ref, pick_ref, emb_ref, mod_ref, order_ref, patch_ref, pay_ref, out_t_ref):
    out_t_ref[...] = nt(order_ref[...], x_ref[:, 256:384]).astype(BF16)
    cols = x_ref[:, 128:256]
    halves = []
    for h in range(2):
        found = jnp.concatenate(
            [nn(pick_ref[h], cols), nn(emb_ref[h], cols), jnp.zeros((48, LANES), F32)], axis=0
        )
        turned = pltpu.roll(found, 40, 1).T[0:40]
        mod = mod_ref[40 * h : 40 * h + 40]
        lane = lane_of((40, LANES))
        valid = lax.broadcasted_iota(jnp.int32, (40, LANES), 0) < ROWS
        block = jnp.where(lane < PF, turned, jnp.where(lane == 76, 1.0, 0.0))
        for step in range(STEPS):
            hidden = turned[:, PF + step : PF + step + 1]
            condition = hidden / (1.0 + jnp.exp(-hidden))
            for j, kind in enumerate((1, 0, 2)):
                value = condition * mod[:, kind : kind + 1] + mod[:, 3 + kind : 4 + kind]
                if kind == 1:
                    value = value + 1.0
                upper = value.astype(BF16).astype(F32)
                block = jnp.where(lane == PF + 3 * step + j, upper, block)
                block = jnp.where(lane == PF + 6 + 3 * step + j, value - upper, block)
        halves.append(jnp.where(valid, block, 0.0))
    pay = jnp.concatenate(halves, axis=0).astype(BF16)
    pay = jnp.concatenate([patch_ref[...], pay], axis=0)
    for t in range(TILE):
        pay_ref[t] = pay


def fold_kernel(step, feat_ref, x_ref, out_ref, *gram_refs):
    lane = lane_of((WIDE, LANES))
    feat = jnp.concatenate([feat_ref[t, PF:].astype(F32) for t in range(TILE)], axis=0)
    mods = feat + pltpu.roll(feat, LANES - 6, 1)
    wide = jnp.where(lane < PF, feat, 0.0)
    mean = jnp.sum(wide, axis=0, keepdims=True) * (1.0 / D)
    centred = (wide - mean) * feat[:, 76:77]
    for gram_ref in gram_refs:
        upper = centred.astype(BF16)
        lower = (centred - upper.astype(F32)).astype(BF16)
        gram = tn(upper, upper) + tn(upper, lower) + tn(lower, upper)
        gram = gram[0:PF, 0:PF]
        upper = gram.astype(BF16)
        gram_ref[0:PF] = upper
        gram_ref[PF : 2 * PF] = (gram - upper.astype(F32)).astype(BF16)
    at = PF + 3 * step
    lines = jnp.where(
        lane < PF,
        centred * mods[:, at : at + 1],
        jnp.where(lane == PF, mods[:, at + 1 : at + 2], 0.0),
    )
    upper = lines.astype(BF16)
    lower = (lines - upper.astype(F32)).astype(BF16)
    weights = x_ref[:, 0:256]
    folded = tn(weights, upper) + tn(weights, lower)
    unit = [folded[HEAD * j : HEAD * j + HEAD] for j in range(3)]
    spot = lane_of((HEAD, LANES))
    top = jnp.where(spot < PF, unit[0], pltpu.roll(unit[1], PF, 1))
    low = jnp.where(spot < PF, unit[2], 0.0)
    low = jnp.where(spot == PF, unit[0], low)
    low = jnp.where(spot == PF + 1, pltpu.roll(unit[1], 1, 1), low)
    low = jnp.where(spot == PF + 2, pltpu.roll(unit[2], 2, 1), low)
    packed = jnp.concatenate([top, low], axis=0).astype(BF16)
    for t in range(TILE):
        out_ref[t] = packed


def heads_kernel(folded_ref, widen_ref, n_ref, mvt_ref, units):
    spot = lane_of((HEAD, LANES))
    for t in range(TILE):
        both = folded_ref[t].astype(F32)
        top, low = both[0:HEAD], both[HEAD : 2 * HEAD]
        parts = (
            (top, low),
            (pltpu.roll(top, PF, 1), pltpu.roll(low, LANES - 1, 1)),
            (low, pltpu.roll(low, LANES - 2, 1)),
        )
        for j, (main, bias) in enumerate(parts):
            unit = jnp.where(spot < PF, main, jnp.where(spot == PF, bias, 0.0))
            units[3 * t + j] = unit
    fold_scale = math.log2(math.e) / math.sqrt(HEAD)
    for h in range(HEADS):
        q, k, v = (units[HEADS * kind + h].astype(BF16) for kind in range(3))
        n_ref[h] = (tn(q, k) * fold_scale).astype(BF16)
        mvt_ref[h] = nn(widen_ref[...], v).astype(BF16)


def with_edges(pt_ref, j):
    patches = pt_ref[j].astype(F32)[0:PF]
    lane = lane_of((2 * C, LANES))
    blank = jnp.zeros((2 * C, LANES), F32)
    first, last = blank, blank
    if j > 0:
        edge = pltpu.roll(pt_ref[j - 1].astype(F32)[PF : PF + 2 * C], PF, 1)
        first = jnp.where(lane < PF, edge, 0.0)
    if j < TILE - 1:
        edge = pltpu.roll(pt_ref[j + 1].astype(F32)[PF : PF + 2 * C], PF, 1)
        last = jnp.where(lane >= PF, edge, 0.0)
    added = jnp.concatenate([first[0:C], last[0:C], first[C:], last[C:]], axis=0)
    return (patches + added).astype(BF16)


def attend_kernel(
    edges, spot_ref, pt_ref, gram_ref, n_ref, mvt_ref, att_ref, own_ref, keys_t, keys, held
):
    me = spot_ref[0]
    row = lax.broadcasted_iota(jnp.int32, (PF, TOK), 0)
    ones = jnp.where(row == 0, 1.0, 0.0).astype(F32)
    blocks = []
    for j in range(TILE):
        rounded = with_edges(pt_ref, j) if edges else pt_ref[j, 0:PF]
        held[j] = rounded
        blocks.append(rounded)
    patches = jnp.concatenate(blocks, axis=1)
    product = nn(gram_ref[...], patches)
    patches = patches.astype(F32)
    product = patches * (product[0:PF] + product[PF : 2 * PF])
    spread = jnp.maximum(jnp.sum(product, axis=0, keepdims=True), 0.0)
    unit = patches * lax.rsqrt(spread * (1.0 / D) + NORM_EPS)
    for j in range(TILE):
        wide = jnp.concatenate([unit[:, j * TOK : (j + 1) * TOK], ones], axis=0)
        keys_t[:, j * TOK : (j + 1) * TOK] = wide.astype(BF16)
        keys[j * TOK : (j + 1) * TOK, :] = wide.T.astype(BF16)
    own_ref[...] = held[me]

    def two_heads(pair):
        own = keys[pl.ds(pl.multiple_of(me * TOK, TOK), TOK), :]
        queries = jnp.concatenate(
            [nn(own, n_ref[2 * pair]), nn(own, n_ref[2 * pair + 1])], axis=0
        ).astype(BF16)
        scores = nn(queries, keys_t[...])
        highest = jnp.max(scores, axis=1, keepdims=True)
        weights = jnp.exp2(scores - highest).astype(BF16)
        summed = nn(weights, keys[...])
        mean = (summed / summed[:, PF : PF + 1]).astype(BF16)
        for k in range(2):
            head = 2 * pair + k
            value = nt(mvt_ref[head], mean[k * TOK : (k + 1) * TOK])
            att_ref[pl.ds(pl.multiple_of(head * 80, 80), 80), :] = value.astype(BF16)

    @pl.loop(0, HEADS // 8)
    def _(i):
        for k in range(4):
            two_heads(4 * i + k)


def output_kernel(
    step, spot_ref, att_ref, own_ref, feat_ref, wot_ref, out_ref, stream_ref
):
    me = spot_ref[0]
    delta = nn(wot_ref[...], att_ref[...])
    for b in range(TILE):
        tile = ((me ^ (8 * (b % 2))) & 8) + b // 2
        rows = pl.ds(pl.multiple_of(tile * 80, 80), 80)
        stream_ref[rows, :] = delta[80 * b : 80 * b + 80]
    feat = jnp.concatenate([feat_ref[t, PF:] for t in range(TILE)], axis=0)
    own = jnp.concatenate([own_ref[...], jnp.zeros((PF, TOK), BF16)], axis=0)
    at = PF + 3 * step + 2
    gate = feat[:, at : at + 1].astype(F32) + feat[:, at + 6 : at + 7].astype(F32)
    valid = feat[:, 76:77].astype(F32)
    stream = (nn(feat, own) + gate * stream_ref[...]) * valid
    mean = jnp.sum(stream, axis=0, keepdims=True) * (1.0 / D)
    center = (stream - mean) * valid
    spread = jnp.sum(center * center, axis=0, keepdims=True) * (1.0 / D)
    final = (center * lax.rsqrt(spread + NORM_EPS)).astype(BF16)
    out_rows = [wot_ref[80 * b + 32 : 80 * b + 48, :] for b in range(TILE)]
    noise = nn(jnp.concatenate(out_rows, axis=0), final)
    feature = lax.broadcasted_iota(jnp.int32, (PF, 256), 0)
    source = lane_of((PF, 256))
    block = source >> 4
    tile = ((me ^ ((block & 1) << 3)) & 8) + (block >> 1)
    q = (source & 15) - 4
    wanted = ((q & 1) << 5) + ((q >> 1) << 4) + tile
    order = jnp.where((q >= 0) & (q < 4) & (feature == wanted), 1.0, 0.0).astype(F32)
    noise = nn(order, noise, HIGHEST)
    for hp in range(2):
        rows = None
        for b in range(2):
            term = nn(
                noise[b * 32 : (b + 1) * 32], spread_matrix((TOK, LANES), 0, hp, b, F32), HIGHEST
            )
            rows = term if rows is None else rows + term
        out_ref[2 * hp] = rows[0:C]
        out_ref[2 * hp + 1] = rows[C : 2 * C]


VMEM = pl.BlockSpec(memory_space=pltpu.VMEM)
SMEM = pl.BlockSpec(memory_space=pltpu.SMEM)
BLOCK = pl.BlockSpec()


def spread(x, emb, mod, patches):
    return pl.pallas_call(
        spread_kernel,
        out_shape=(
            jax.ShapeDtypeStruct((TILE, PF + 80, LANES), BF16),
            jax.ShapeDtypeStruct((80, WIDE), BF16),
        ),
        in_specs=[VMEM] * 6,
        out_specs=(VMEM, VMEM),
        compiler_params=pltpu.CompilerParams(vmem_limit_bytes=32 * 1024 * 1024),
        name="spread",
    )(x, jnp.asarray(PICK, BF16), emb, mod, jnp.asarray(ORDER, BF16), patches)


def fold(step, feat, x):
    shapes = [jax.ShapeDtypeStruct((TILE, 2 * HEAD, LANES), BF16)]
    if step == 0:
        shapes.append(jax.ShapeDtypeStruct((2 * PF, PF), BF16))
    return pl.pallas_call(
        functools.partial(fold_kernel, step),
        out_shape=tuple(shapes),
        in_specs=[VMEM] * 2,
        out_specs=(VMEM,) * len(shapes),
        compiler_params=pltpu.CompilerParams(vmem_limit_bytes=32 * 1024 * 1024),
        cost_estimate=pl.CostEstimate(
            flops=4 * WIDE * 256 * LANES, bytes_accessed=8 * WIDE * LANES, transcendentals=0
        ),
        name="fold",
    )(feat, x)


def heads(folded):
    return pl.pallas_call(
        heads_kernel,
        out_shape=(
            jax.ShapeDtypeStruct((HEADS, LANES, LANES), BF16),
            jax.ShapeDtypeStruct((HEADS, 80, LANES), BF16),
        ),
        in_specs=[VMEM] * 2,
        out_specs=(VMEM,) * 2,
        scratch_shapes=[pltpu.VMEM((3 * HEADS, HEAD, LANES), F32)],
        compiler_params=pltpu.CompilerParams(vmem_limit_bytes=32 * 1024 * 1024),
        name="heads",
    )(folded, jnp.asarray(ORDER[:, 0:HEAD], BF16))


def attend(edges, spot, pt, gram, n, mvt):
    return pl.pallas_call(
        functools.partial(attend_kernel, edges),
        out_shape=(
            jax.ShapeDtypeStruct((WIDE, TOK), BF16),
            jax.ShapeDtypeStruct((PF, TOK), BF16),
        ),
        in_specs=[SMEM] + [BLOCK] * 4,
        out_specs=(VMEM, VMEM),
        scratch_shapes=[
            pltpu.VMEM((LANES, SPAN), BF16),
            pltpu.VMEM((SPAN, LANES), BF16),
            pltpu.VMEM((TILE, PF, TOK), BF16),
        ],
        compiler_params=pltpu.CompilerParams(vmem_limit_bytes=40 * 1024 * 1024),
        cost_estimate=pl.CostEstimate(
            flops=4 * 2 * SPAN * SPAN * LANES,
            bytes_accessed=8 * SPAN * LANES,
            transcendentals=SPAN * SPAN,
        ),
        name="attend",
    )(spot, pt, gram, n, mvt)


def output(step, spot, att, own, feat, wot):
    return pl.pallas_call(
        functools.partial(output_kernel, step),
        out_shape=jax.ShapeDtypeStruct((4, C, LANES), F32),
        in_specs=[SMEM] + [VMEM] * 4,
        out_specs=VMEM,
        scratch_shapes=[pltpu.VMEM((WIDE, TOK), F32)],
        compiler_params=pltpu.CompilerParams(vmem_limit_bytes=32 * 1024 * 1024),
        name="output",
    )(spot, att, own, feat, wot)


def prep(scale_in, latent):
    return pl.pallas_call(
        prep_kernel,
        out_shape=jax.ShapeDtypeStruct((PF, TOK), BF16),
        in_specs=[SMEM, VMEM],
        out_specs=VMEM,
        name="prep",
    )(scale_in, latent)


def middle(scale_in, last, noise, following, after, lat, new, mix):
    return pl.pallas_call(
        middle_kernel,
        out_shape=(
            jax.ShapeDtypeStruct((4, C, LANES), F32),
            jax.ShapeDtypeStruct((2, C, LANES), F32),
            jax.ShapeDtypeStruct((TILE, PF + 2 * C, TOK), BF16),
        ),
        in_specs=[SMEM, SMEM] + [BLOCK] * 6,
        out_specs=(VMEM,) * 3,
        compiler_params=pltpu.CompilerParams(vmem_limit_bytes=32 * 1024 * 1024),
        name="middle",
    )(scale_in, last, noise, following, after, lat, new, mix)


def finish(drop, before, noise, following, up, down, lat, mix):
    return pl.pallas_call(
        final_kernel,
        out_shape=jax.ShapeDtypeStruct((4, C, LANES), F32),
        in_specs=[SMEM] + [BLOCK] * 7,
        out_specs=VMEM,
        compiler_params=pltpu.CompilerParams(vmem_limit_bytes=32 * 1024 * 1024),
        name="finish",
    )(drop, before, noise, following, up, down, lat, mix)


def pick_matrix():
    pick = np.zeros((2, 2, 2, C, TM, 20, 2), np.float32)
    for h in range(2):
        for b in range(2):
            for a in range(2):
                for c in range(C):
                    pick[h, b, a, c, 2 * c + a, 16 + b, h] = 1.0
    return pick.reshape(2, PF, WIDE)


def order_matrix():
    order = np.zeros((80, LANES), np.float32)
    for j in range(ROWS):
        order[j, j] = 1.0
        order[40 + j, ROWS + j] = 1.0
    for j in range(4):
        order[ROWS + j, HEAD + j] = 1.0
    return order


PICK = pick_matrix()
ORDER = order_matrix()


def packed_weights(w_in, w_qkv, w_o, w_out, w_time, w_pos):
    return pl.pallas_call(
        pack_kernel,
        out_shape=jax.ShapeDtypeStruct((TM, 40, 384), BF16),
        in_specs=[BLOCK] * 6,
        out_specs=VMEM,
        scratch_shapes=[pltpu.VMEM((40, 384), F32)],
        name="pack",
    )(w_in, w_qkv, w_o, w_out, w_time, w_pos)


def embeddings(level, position):
    level_emb = sinusoid(level.astype(F32)).reshape(STEPS, TM, 8)
    position_emb = sinusoid(position.astype(F32)).reshape(STEPS, TM, 8)
    rest = jnp.zeros((STEPS, TM, 4), F32)
    emb = jnp.concatenate([level_emb, position_emb, rest], axis=2).astype(BF16)
    half = jnp.eye(2, dtype=BF16)[:, None, None, None, :]
    emb = (emb[None, :, :, :, None] * half).reshape(2, STEPS, WIDE)
    return jnp.pad(emb, ((0, 0), (0, 14), (0, 0)))


def own_mods(mod_gain, mod_bias, tile):
    mods = jnp.concatenate([mod_gain, mod_bias, jnp.zeros((2, D), F32)], axis=0)
    mods = lax.dynamic_slice_in_dim(mods.reshape(8, TILE, HEAD), tile, 1, axis=1)
    return jnp.pad(mods.reshape(8, 2, ROWS), ((0, 0), (0, 0), (0, 4))).reshape(8, 80).T


def per_device(
    latents, new_frames, levels, offset, w_in, w_qkv, w_o, w_out, w_time, w_pos,
    mod_gain, mod_bias, refiner,
):
    frame = lax.axis_index(TM_AXES)
    tile = lax.axis_index(TILE_AXES)
    spot = tile.astype(jnp.int32)[None]
    mix = refiner.reshape(C, 27 * C)
    latent = latents[0]
    level = levels[:, 0]
    sigma_now = sigma_of(level)
    drop = sigma_of(level - 1) - sigma_now
    scale_in = lax.rsqrt(1.0 + sigma_now * sigma_now)

    packed = packed_weights(w_in, w_qkv, w_o, w_out, w_time, w_pos)
    rows = exchanged(packed, TM_AXES)
    rows = rows.reshape(WIDE, 384)

    own = prep(scale_in[0:1], latent)
    marked = jnp.concatenate([latent, jnp.full((1, C, LANES), drop[0], F32)], axis=0)
    marked = shifted(marked, TM_AXES, -1)
    steps = jnp.arange(STEPS, dtype=jnp.int32)
    emb = embeddings(level, offset + frame + steps)
    mods = own_mods(mod_gain, mod_bias, tile)
    rows, marked, mix = lax.optimization_barrier((rows, marked, mix))

    pay, out_t = spread(rows, emb, mods, own)
    across = swapped(out_t, "zh")
    feat = exchanged(pay, TILE_AXES)
    feat, out_t = lax.optimization_barrier((feat, out_t))

    first, gram = fold(0, feat, rows)
    first, feat, rows = lax.optimization_barrier((first, feat, rows))
    first = exchanged(first, TILE_AXES)

    (second,) = fold(1, feat, rows)
    first, second = lax.optimization_barrier((first, second))
    n, mvt = heads(first)
    second = exchanged(second, TILE_AXES)

    both = jnp.stack([out_t, across])
    full_o = lax.all_gather(both, ("x", "core")).reshape(WIDE, WIDE)

    att, own = attend(False, spot, feat, gram, n, mvt)
    noise = output(0, spot, att, own, feat, full_o)

    following, after = shifted(noise, TM_AXES, -1), shifted(noise, TM_AXES, -2)
    following, second = lax.optimization_barrier((following, second))
    last = (frame == TM - 1).astype(jnp.int32)[None]
    latent, edges, patches = middle(
        scale_in[1:2], last, noise, following, after, marked, new_frames[0], mix
    )
    patches = exchanged(patches, TILE_AXES)
    n, mvt = heads(second)

    att, own = attend(True, spot, patches, gram, n, mvt)
    noise = output(1, spot, att, own, feat, full_o)
    frames = [shifted(noise, TM_AXES, 1), noise, shifted(noise, TM_AXES, -1)]
    up = jnp.stack([x[3] for x in frames] + [edges[1]])
    down = jnp.stack([x[0] for x in frames] + [edges[0]])
    up, down = shifted(up, TILE_AXES, 1), shifted(down, TILE_AXES, -1)
    return finish(drop[1:2], *frames, up, down, latent, mix)[None]


def solution(mesh):
    mesh = jax.sharding.Mesh(mesh.devices.reshape(SPLIT), AXES)
    rows, cols = TM_AXES, TILE_AXES
    in_specs = (
        P(rows, cols, None, None),
        P(None, cols, None, None),
        P(None, rows),
        P(),
        P(rows, cols),
        P(rows, cols),
        P(rows, cols),
        P(rows, cols),
        P(rows, cols),
        P(rows, cols),
        P(),
        P(),
        P(),
    )
    out_specs = P(rows, cols, None, None)
    return jax.shard_map(
        per_device, mesh=mesh, in_specs=in_specs, out_specs=out_specs, check_vma=False
    )
```
